32 devices in a mesh: rollout: 4 (over z), ctx: 8 (over y, x, core).
Axes of the slice: x: 2, y: 2, z: 4, core: 2. Of those that a mesh axis runs over, the one named last changes fastest.
Arguments:
- queries: bfloat16 [4, 1024, 4096], P('rollout', 'ctx'), may hold values from -6 to 6
- keys_values: bfloat16 [4, 2, 1024, 1024], P('rollout', None, 'ctx'), may hold values from -6 to 6
- image_rows: bfloat16 [4, 256, 6144], P('rollout', 'ctx'), may hold values from -6 to 6
- cotangent: bfloat16 [4, 1024, 4096], P('rollout', 'ctx'), may hold values from -96 to 96
- seq_image: int32 [4], replicated, may hold values from 0 to 3, as said below
- vis_start: int32 [4], P('rollout'), may hold values from 1 to 63
- comp_lengths: int32 [4, 16], P('rollout'), may hold values from 1 to 58, 704 in all within a row
Outputs:
- grad_queries: bfloat16 [4, 1024, 4096], P('rollout', 'ctx')
- grad_keys_values: bfloat16 [4, 2, 1024, 1024], P('rollout', None, 'ctx')
- grad_image: bfloat16 [4, 256, 6144], P('rollout', 'ctx')
The draws below stay inside these ranges and needn't reach their ends.
Inputs may be any that keep to these rules, and one draw needn't show every extreme that they name: `seq_image`: each image belongs to exactly one group. The image's rows take positions vis_start to vis_start + 255 of the group's sequence. `comp_lengths`: each group's lengths sum to 704.
All inputs are finite; a program needn't handle non-finite values.
Results may differ from the reference program's by a relative error of at most 0.0068.
Values may be sent and summed in bfloat16 or wider, within the bound.
No kernel may reach another device: no remote copies, remote signals or barrier semaphores. Data moves between devices by JAX's collectives and lax.ppermute only.
A program may use at most 128 MiB of HBM per device.

```python
import math
import jax
import jax.numpy as jnp
import numpy as np
from jax import lax

HEADS = 32
KV_HEADS = 8
HEAD_DIM = 128
VIS = 256
PROMPT = 64
NCOMP = 16
SEQ = 1024
GROUPS = 4
MOST = 58


def draw_seq_image(key, part):
    key = jax.random.fold_in(key, 7)
    rotation = jax.random.randint(key, (), 0, GROUPS).astype(jnp.int32)
    group_ids = jnp.arange(GROUPS, dtype=jnp.int32)
    moved = (group_ids - rotation) % GROUPS
    half_count = GROUPS // 2
    base_map = jnp.where(moved < half_count, 2 * moved + 1, 2 * moved - GROUPS)
    return ((base_map + rotation) % GROUPS).astype(jnp.int32)


def draw_queries(key, part):
    key = jax.random.fold_in(key, 3)
    noise_shape = (GROUPS, SEQ, HEADS, HEAD_DIM)
    noise_base = jnp.clip(jax.random.normal(key, noise_shape, jnp.float32), -6.0, 6.0)
    return noise_base.reshape(GROUPS, SEQ, HEADS * HEAD_DIM).astype(jnp.bfloat16)


def draw_keys_values(key, part):
    key = jax.random.fold_in(key, 5)
    kv_shape = (GROUPS, 2, SEQ, KV_HEADS, HEAD_DIM)
    noise_base = jnp.clip(jax.random.normal(key, kv_shape, jnp.float32), -6.0, 6.0)
    return noise_base.reshape(GROUPS, 2, SEQ, KV_HEADS * HEAD_DIM).astype(jnp.bfloat16)


def place_ends(values, rng, smallest, high):
    index_at = [jax.random.randint(jax.random.fold_in(rng, axis), (), 0, length) for axis, length in enumerate(values.shape)]
    widest = values.shape.index(max(values.shape))
    beside = index_at[:widest] + [(index_at[widest] + 1) % values.shape[widest]] + index_at[widest + 1:]
    return values.at[tuple(index_at)].set(smallest).at[tuple(beside)].set(high)


def shard_levels(key, extent, cuts, low, largest):
    def one(axis_at, blocks):
        heights = jax.random.uniform(jax.random.fold_in(jax.random.fold_in(key, 6), axis_at), (blocks,), jnp.float32, low / len(cuts), largest / len(cuts))
        return jnp.repeat(jnp.exp(heights), extent[axis_at] // blocks).reshape((-1,) + (1,) * (len(extent) - axis_at - 1))

    factor_of = one(*cuts[0])
    for cut in cuts[1:]:
        factor_of = factor_of * one(*cut)
    return factor_of


def length_profile(amount, total, reach, lean):
    loads = [(1 << 20) // math.isqrt(grade ** lean) + 1 for grade in range(2, amount + 1)]
    spare, given = total - reach - (amount - 1), [1] * (amount - 1)
    while spare > 0:
        free = [i for i in range(amount - 1) if given[i] < reach]
        mass, budget = sum([loads[i] for i in free]), spare
        for i in free:
            more = min(reach - given[i], max(1, budget * loads[i] // mass), spare)
            given[i] = given[i] + more
            spare = spare - more
    return np.array([reach] + given)


def uneven_parts(key, amount, total, reach, lean):
    if amount == 2:
        one = jax.random.randint(key, (), max(1, total - reach), min(reach, total - 1) + 1)
        return jnp.stack([one, total - one])
    sizes = jnp.asarray(length_profile(amount, total, reach, lean), jnp.int32)
    couples = (amount - 1) // 2
    source_of, sink = sizes[1:1 + 2 * couples:2], sizes[2:2 + 2 * couples:2]
    slack = jnp.minimum(source_of - 1, reach - sink)
    moved = jax.random.randint(jax.random.fold_in(key, 1), (couples,), 0, 1 << 20) % (slack + 1)
    sizes = sizes.at[1:1 + 2 * couples:2].set(source_of - moved).at[2:2 + 2 * couples:2].set(sink + moved)
    return sizes[jax.random.permutation(jax.random.fold_in(key, 2), amount)]


def scatter_about(own_key, shape, spread, most, shards=(), held_as=jnp.bfloat16):
    factor_of = shard_levels(own_key, shape, shards, -0.22, 0.18) if shards else 1.0
    entries = jax.random.normal(own_key, shape, jnp.float32) * spread * factor_of
    return jnp.minimum(jnp.maximum(entries, -most), most).astype(held_as)


def setup_inputs(seed: int = 0) -> dict:
    key_list = jax.random.split(jax.random.key(seed), 8)
    queries = draw_queries(jax.random.fold_in(key_list[7], 71), 0)
    keys_values = draw_keys_values(jax.random.fold_in(key_list[7], 71), 0)
    image_rows = scatter_about(key_list[2], (GROUPS, VIS, (HEADS + 2 * KV_HEADS) * HEAD_DIM), 1.0, 6.0, ((0, 4), (1, 8)))
    cotangent = scatter_about(key_list[3], (GROUPS, SEQ, HEADS * HEAD_DIM), 16.0, 96.0, ((0, 4), (1, 8)))
    seq_image = draw_seq_image(jax.random.fold_in(key_list[7], 71), 0)
    vis_start = place_ends(jax.random.randint(key_list[5], (GROUPS,), 1, PROMPT), jax.random.fold_in(key_list[5], 1), 1, PROMPT - 1).astype(jnp.int32)
    comp_lengths = jax.vmap(lambda own: uneven_parts(own, NCOMP, SEQ - VIS - PROMPT, MOST, 2))(jax.random.split(key_list[6], GROUPS)).reshape((GROUPS, NCOMP)).astype(jnp.int32)
    return {"queries": queries, "keys_values": keys_values, "image_rows": image_rows, "cotangent": cotangent, "seq_image": seq_image, "vis_start": vis_start, "comp_lengths": comp_lengths}


neg_large = -1e+30

def segment_table(lengths):
    prefix_len = VIS + PROMPT
    seg_ends = jnp.cumsum(lengths).astype(jnp.int32)
    positions = jnp.arange(SEQ, dtype=jnp.int32)
    later_ends = lax.optimization_barrier(jnp.sum((seg_ends[None, :] <= (positions - prefix_len)[:, None]).astype(jnp.int32), axis=1))
    return jnp.where(positions < prefix_len, 0, 1 + later_ends).astype(jnp.int32)

def rounded(value):
    return lax.optimization_barrier(value.astype(jnp.bfloat16)).astype(jnp.float32)

def head_grads(q_head, k_head, v_head, d_head, visible):
    score_scale = 1.0 / math.sqrt(HEAD_DIM)
    q_float = q_head.astype(jnp.float32)
    k_float = k_head.astype(jnp.float32)
    v_float = v_head.astype(jnp.float32)
    d_float = d_head.astype(jnp.float32)
    scores = jnp.dot(q_float, k_float.T, preferred_element_type=jnp.float32) * score_scale
    scores = jnp.where(visible, scores, neg_large)
    row_top = lax.optimization_barrier(jnp.max(scores, axis=1, keepdims=True))
    exp_terms = jnp.where(visible, jnp.exp(scores - row_top), 0.0)
    weights = exp_terms / lax.optimization_barrier(jnp.sum(exp_terms, axis=1, keepdims=True))
    d_weights = jnp.dot(d_float, v_float.T, preferred_element_type=jnp.float32)
    row_delta = lax.optimization_barrier(jnp.sum(weights * d_weights, axis=1, keepdims=True))
    d_scores = rounded(weights * (d_weights - row_delta))
    head_dq = (jnp.dot(d_scores, k_float, preferred_element_type=jnp.float32) * score_scale).astype(jnp.bfloat16)
    head_dk = jnp.dot(d_scores.T, q_float, preferred_element_type=jnp.float32) * score_scale
    head_dv = jnp.dot(rounded(weights).T, d_float, preferred_element_type=jnp.float32)
    return (head_dq, head_dk, head_dv)

def one_group(group_items):
    q_rows, kv_rows, d_rows, image_view, vis_begin, lengths = group_items
    query_width = HEADS * HEAD_DIM
    kv_width = KV_HEADS * HEAD_DIM
    head_ratio = HEADS // KV_HEADS
    vis_begin = vis_begin.astype(jnp.int32)
    q_full = lax.dynamic_update_slice_in_dim(q_rows, image_view[:, :query_width], vis_begin, 0)
    k_full = lax.dynamic_update_slice_in_dim(kv_rows[0], image_view[:, query_width:query_width + kv_width], vis_begin, 0)
    v_full = lax.dynamic_update_slice_in_dim(kv_rows[1], image_view[:, query_width + kv_width:], vis_begin, 0)
    segment_ids = segment_table(lengths)
    positions = jnp.arange(SEQ, dtype=jnp.int32)
    visible = (positions[None, :] <= positions[:, None]) & ((segment_ids[None, :] == 0) | (segment_ids[None, :] == segment_ids[:, None]))

    def per_head(head_index):
        kv_index = head_index // head_ratio
        q_head = lax.dynamic_slice_in_dim(q_full, head_index * HEAD_DIM, HEAD_DIM, 1)
        d_head = lax.dynamic_slice_in_dim(d_rows, head_index * HEAD_DIM, HEAD_DIM, 1)
        k_head = lax.dynamic_slice_in_dim(k_full, kv_index * HEAD_DIM, HEAD_DIM, 1)
        v_head = lax.dynamic_slice_in_dim(v_full, kv_index * HEAD_DIM, HEAD_DIM, 1)
        return head_grads(q_head, k_head, v_head, d_head, visible)
    head_dq, head_dk, head_dv = lax.map(per_head, jnp.arange(HEADS, dtype=jnp.int32))
    sum_keys = lax.optimization_barrier(jnp.sum(head_dk.reshape(KV_HEADS, head_ratio, SEQ, HEAD_DIM), axis=1)).astype(jnp.bfloat16)
    sum_values = lax.optimization_barrier(jnp.sum(head_dv.reshape(KV_HEADS, head_ratio, SEQ, HEAD_DIM), axis=1)).astype(jnp.bfloat16)
    grad_q = jnp.transpose(head_dq, (1, 0, 2)).reshape(SEQ, query_width)
    grad_k = jnp.transpose(sum_keys, (1, 0, 2)).reshape(SEQ, kv_width)
    grad_v = jnp.transpose(sum_values, (1, 0, 2)).reshape(SEQ, kv_width)
    image_grad = jnp.concatenate([lax.dynamic_slice_in_dim(grad_q, vis_begin, VIS, 0), lax.dynamic_slice_in_dim(grad_k, vis_begin, VIS, 0), lax.dynamic_slice_in_dim(grad_v, vis_begin, VIS, 0)], axis=1)
    inside = (positions >= vis_begin) & (positions < vis_begin + VIS)
    zero_value = jnp.zeros((), jnp.bfloat16)
    grad_q = jnp.where(inside[:, None], zero_value, grad_q)
    grad_kv = jnp.where(inside[None, :, None], zero_value, jnp.stack([grad_k, grad_v]))
    return (grad_q, grad_kv, image_grad)

def reference(queries, keys_values, image_rows, cotangent, seq_image, vis_start, comp_lengths):
    image_views = image_rows[seq_image]
    grad_queries, grad_keys_values, image_grads = lax.map(one_group, (queries, keys_values, cotangent, image_views, vis_start, comp_lengths))
    grad_image = jnp.zeros_like(image_rows).at[seq_image].set(image_grads)
    return (grad_queries, grad_keys_values, grad_image)
```

```python
import functools
import itertools
import math

import jax
import jax.numpy as jnp
from jax import lax
from jax.experimental import pallas as pl
from jax.experimental.pallas import tpu as pltpu
from jax.sharding import PartitionSpec as P

HEADS = 32
KV_HEADS = 8
HEAD_DIM = 128
VIS = 256
PROMPT = 64
NCOMP = 16

RATIO = HEADS // KV_HEADS
PREFIX = VIS + PROMPT
Q_WIDTH = HEADS * HEAD_DIM
KV_WIDTH = KV_HEADS * HEAD_DIM
GROUP_WIDTH = RATIO * HEAD_DIM
IMAGE_BLOCK = 32
HIDDEN = -1e30
SCORE_SCALE = 1.0 / math.sqrt(HEAD_DIM)


def dot_nt(left, right):
    return lax.dot_general(
        left, right, (((1,), (1,)), ((), ())), preferred_element_type=jnp.float32
    )


def dot_nn(left, right):
    return lax.dot_general(
        left, right, (((1,), (0,)), ((), ())), preferred_element_type=jnp.float32
    )


def dot_tn(left, right):
    return lax.dot_general(
        left, right, (((0,), (0,)), ((), ())), preferred_element_type=jnp.float32
    )


def first_kernel(halo, seq_ref, vis_ref, image_ref, kv_ref, number_ref, *out_refs):
    ikv_ref, iq_ref, text_ref, tail_ref = out_refs
    groups = seq_ref.shape[0]
    group = lax.axis_index("rollout")
    here = lax.axis_index("ctx")
    images = [seq_ref[at] for at in range(groups)]
    number = jnp.int32(0)
    if groups == 4:
        for at, weight in enumerate((6, 2, 1)):
            for later in range(at + 1, groups):
                number = number + jnp.where(images[later] < images[at], weight, 0)
    place = jnp.int32(0)
    user = jnp.int32(0)
    for at in range(groups):
        place = place + jnp.where(group == at, images[at], 0)
        user = user + jnp.where(images[at] == group, at, 0)
    number_ref[0] = number
    number_ref[1] = place
    number_ref[2] = user
    iq_ref[...] = image_ref[0, :, :Q_WIDTH]
    ikv_ref[0] = image_ref[0, :, Q_WIDTH : Q_WIDTH + KV_WIDTH]
    ikv_ref[1] = image_ref[0, :, Q_WIDTH + KV_WIDTH :]
    tok_rows = kv_ref.shape[2]
    late_shard = VIS // tok_rows
    at = lax.broadcasted_iota(jnp.int32, (PROMPT, KV_WIDTH), 0)
    ahead = jnp.where(here == 0, 1, 0)
    behind = jnp.where(here == late_shard, 1, 0)
    kept = jnp.where(at < vis_ref[0], ahead, behind) == 1
    for part in range(2):
        rows = kv_ref[0, part, :PROMPT].astype(jnp.float32)
        text_ref[part] = jnp.where(kept, rows, 0.0).astype(jnp.bfloat16)
        tail_ref[part] = kv_ref[0, part, tok_rows - halo :]


def first_arrays(seq_image, vis_start, image_rows, keys_values, halo):
    rows = image_rows.shape[1]
    smem = pl.BlockSpec(memory_space=pltpu.SMEM)
    vmem = pl.BlockSpec(memory_space=pltpu.VMEM)
    tail = min(halo, keys_values.shape[2])
    return pl.pallas_call(
        functools.partial(first_kernel, tail),
        in_specs=[smem, smem, vmem, vmem],
        out_specs=[smem, vmem, vmem, vmem, vmem],
        out_shape=[
            jax.ShapeDtypeStruct((3,), jnp.int32),
            jax.ShapeDtypeStruct((2, rows, KV_WIDTH), jnp.bfloat16),
            jax.ShapeDtypeStruct((rows, Q_WIDTH), jnp.bfloat16),
            jax.ShapeDtypeStruct((2, PROMPT, KV_WIDTH), jnp.bfloat16),
            jax.ShapeDtypeStruct((2, tail, KV_WIDTH), jnp.bfloat16),
        ],
    )(seq_image, vis_start, image_rows, keys_values)


def segments(positions, length_ref):
    end = jnp.int32(PREFIX)
    segment = jnp.where(positions < PREFIX, 0, 1)
    for at in range(NCOMP):
        end = end + length_ref[0, at]
        segment = segment + jnp.where(positions >= end, 1, 0)
    return segment


def hide(visible):
    return jnp.where(visible, 0.0, HIDDEN)


def second_kernel(
    rounds, tok_rows, image_rows, halo, vis_ref, length_ref, d_ref, t_ref, r_ref, *out_refs
):
    *window_refs, near_ref, whole_ref, image_ref, text_ref = out_refs
    here = lax.axis_index("ctx")
    ctx_size = lax.axis_size("ctx")
    row = lax.broadcasted_iota(jnp.int32, (IMAGE_BLOCK, tok_rows), 0)
    column = lax.broadcasted_iota(jnp.int32, (IMAGE_BLOCK, tok_rows), 1)
    place = jnp.where(row < image_rows, row, 1 << 20)
    picks = []
    for pairs in [[]] + rounds:
        target = here
        for source, other in pairs:
            target = jnp.where(here == source, other, target)
        begin = vis_ref[0] + image_rows * target - tok_rows * here
        picks.append(jnp.where(column == place + begin, 1.0, 0.0).astype(jnp.bfloat16))
    picked = dot_nn(jnp.concatenate(picks, axis=0), d_ref[...]).astype(jnp.bfloat16)
    for at, window_ref in enumerate(window_refs):
        window_ref[...] = picked[at * IMAGE_BLOCK : (at + 1) * IMAGE_BLOCK]

    @pl.when(pl.program_id(0) == 0)
    def _():
        vis = vis_ref[0]
        text = t_ref[...].astype(jnp.float32) + r_ref[...].astype(jnp.float32)
        text_ref[...] = text.astype(jnp.bfloat16)
        own_at = lax.broadcasted_iota(jnp.int32, (8, tok_rows), 1) + here * tok_rows
        own_segment = segments(own_at, length_ref)[:1]
        placeholder = (own_at >= vis) & (own_at < vis + VIS)
        own_row = jnp.where(placeholder, -1, own_at)
        whole_ref[...] = hide(own_row >= vis + VIS).astype(jnp.float32)
        own_row = own_row[:1]
        image_at = lax.broadcasted_iota(jnp.int32, (1, RATIO * IMAGE_BLOCK), 1) % IMAGE_BLOCK
        image_row = jnp.where(image_at < image_rows, vis + here * image_rows + image_at, -1)
        text_at = lax.broadcasted_iota(jnp.int32, (PROMPT, tok_rows), 0)
        text_at = text_at + jnp.where(text_at < vis, 0, VIS)
        near_ref[:PROMPT] = hide(text_at <= own_row)
        near_at = lax.broadcasted_iota(jnp.int32, (halo + tok_rows, tok_rows), 0)
        near_at = near_at + (here * tok_rows - halo)
        sees = (near_at <= own_row) & (near_at >= PREFIX)
        sees = sees & (segments(near_at, length_ref) == own_segment)
        near_ref[PROMPT:] = hide(sees)
        at = 0
        for core in range(2):
            for step in range(0, ctx_size, 2):
                begin = (here ^ (step + core)) * image_rows + vis
                shape = (image_rows, RATIO * IMAGE_BLOCK)
                block_at = lax.broadcasted_iota(jnp.int32, shape, 0) + begin
                image_ref[at : at + image_rows] = hide(block_at <= image_row)
                at += image_rows
        image_ref[VIS:] = hide(text_at <= image_row)


def second_arrays(vis_start, lengths, cotangent, text, received, image_rows, halo):
    tok_rows, width = cotangent.shape
    rounds = window_rounds(lax.axis_size("ctx"), tok_rows, image_rows)
    count = len(rounds) + 1
    block = 1024
    spec = pl.BlockSpec
    smem = spec(memory_space=pltpu.SMEM)
    lanes = RATIO * IMAGE_BLOCK
    near = PROMPT + halo + tok_rows
    whole = lambda *shape: spec(shape, lambda at: (0,) * len(shape))
    out = pl.pallas_call(
        functools.partial(second_kernel, rounds, tok_rows, image_rows, halo),
        grid=(width // block,),
        in_specs=[
            smem,
            smem,
            spec((tok_rows, block), lambda at: (0, at)),
            whole(2, PROMPT, KV_WIDTH),
            whole(2, PROMPT, KV_WIDTH),
        ],
        out_specs=[spec((IMAGE_BLOCK, block), lambda at: (0, at)) for _ in range(count)]
        + [
            whole(near, tok_rows),
            whole(8, tok_rows),
            whole(PREFIX, lanes),
            whole(2, PROMPT, KV_WIDTH),
        ],
        out_shape=[jax.ShapeDtypeStruct((IMAGE_BLOCK, width), jnp.bfloat16) for _ in range(count)]
        + [
            jax.ShapeDtypeStruct((near, tok_rows), jnp.float32),
            jax.ShapeDtypeStruct((8, tok_rows), jnp.float32),
            jax.ShapeDtypeStruct((PREFIX, lanes), jnp.float32),
            jax.ShapeDtypeStruct((2, PROMPT, KV_WIDTH), jnp.bfloat16),
        ],
    )(vis_start, lengths, cotangent, text, received)
    return out[:count], rounds, out[count:]


def rows_backward(parts, q_rows, d_rows):
    scale = SCORE_SCALE * math.log2(math.e)
    scores = []
    for keys, values, bias in parts:
        raw = dot_nt(keys, q_rows) * scale
        scores.append(raw if bias.shape[0] == 1 else raw + bias)
    tops = [jnp.max(part, axis=0, keepdims=True) for part in scores]
    tops = [
        top + bias if bias.shape[0] == 1 else top for top, (_, _, bias) in zip(tops, parts)
    ]
    top = functools.reduce(jnp.maximum, tops)
    total = 0.0
    mix = 0.0
    kept = []
    for part, (keys, values, bias) in zip(scores, parts):
        shift = bias - top if bias.shape[0] == 1 else -top
        terms = jnp.exp2(part + shift)
        d_weights = dot_nt(values, d_rows)
        total = total + jnp.sum(terms, axis=0, keepdims=True)
        mix = mix + jnp.sum(terms * d_weights, axis=0, keepdims=True)
        kept.append((terms, d_weights))
    inverse = jnp.where(top > 0.5 * HIDDEN, 1.0 / total, 0.0)
    delta = mix * inverse
    outcome = []
    for terms, d_weights in kept:
        weights = terms * inverse
        d_scores = weights * (d_weights - delta)
        outcome.append((weights.astype(jnp.bfloat16), d_scores.astype(jnp.bfloat16)))
    return outcome


def total_of(refs, at=slice(None)):
    if len(refs) == 1:
        return refs[0][at]
    return sum(ref[at].astype(jnp.float32) for ref in refs).astype(jnp.bfloat16)


def attend_kernel(
    block_count,
    window_count,
    heads,
    halo,
    own,
    number_ref,
    near_ref,
    whole_ref,
    image_bias_ref,
    q_ref,
    d_ref,
    iq_ref,
    text_ref,
    other_text_ref,
    halo_ref,
    own_ref,
    *refs,
):
    block_refs = refs[:block_count]
    window_refs = refs[block_count : block_count + window_count]
    dq_ref, diq_ref, dmine_ref, dpair_ref, dhalo_ref, down_ref = refs[
        block_count + window_count :
    ]
    near_bias = jnp.concatenate([near_ref[...]] * 2, axis=1)
    whole_bias = jnp.concatenate([whole_ref[:1]] * 2, axis=1)
    image_cotangent = total_of(window_refs)
    for head in range(heads):
        lanes = slice(head * HEAD_DIM, (head + 1) * HEAD_DIM)
        spans = [
            slice((head * RATIO + at) * HEAD_DIM, (head * RATIO + at + 1) * HEAD_DIM)
            for at in range(RATIO)
        ]
        visual, text, near = [], [], []
        for part in range(2):
            visual.append(jnp.concatenate([ref[part, :, lanes] for ref in block_refs], axis=0))
            text.append(total_of([text_ref, other_text_ref], (part, slice(None), lanes)))
            near.append(
                jnp.concatenate(
                    [text[part], halo_ref[part, :, lanes], own_ref[0, part, :, lanes]], axis=0
                )
            )
        keys = jnp.concatenate([visual[0], near[0]], axis=0)
        dk_sums = [0.0, 0.0]
        dv_sums = [0.0, 0.0]
        for first in range(0, RATIO, 2):
            pair = spans[first : first + 2]
            q_rows = jnp.concatenate([q_ref[:, span] for span in pair], axis=0)
            d_rows = jnp.concatenate([d_ref[:, span] for span in pair], axis=0)
            outcome = rows_backward(
                [(visual[0], visual[1], whole_bias), (near[0], near[1], near_bias)],
                q_rows,
                d_rows,
            )
            d_scores = jnp.concatenate([part[1] for part in outcome], axis=0)
            dq = dot_tn(keys, d_scores) * SCORE_SCALE
            for at, span in enumerate(pair):
                dq_ref[:, span] = dq[:, at * own : (at + 1) * own].T.astype(jnp.bfloat16)
            for at, (weights, d_part) in enumerate(outcome):
                dk_sums[at] = dk_sums[at] + dot_nn(d_part, q_rows)
                dv_sums[at] = dv_sums[at] + dot_nn(weights, d_rows)
        image_queries = iq_ref[number_ref[1]]
        q_rows = jnp.concatenate([image_queries[:, span] for span in spans], axis=0)
        d_rows = jnp.concatenate([image_cotangent[:, span] for span in spans], axis=0)
        outcome = rows_backward(
            [
                (visual[0], visual[1], image_bias_ref[:VIS]),
                (text[0], text[1], image_bias_ref[VIS:]),
            ],
            q_rows,
            d_rows,
        )
        d_scores = jnp.concatenate([part[1] for part in outcome], axis=0)
        dq = (dot_tn(keys[:PREFIX], d_scores) * SCORE_SCALE).T.astype(jnp.bfloat16)
        for at, span in enumerate(spans):
            diq_ref[:, span] = dq[at * IMAGE_BLOCK : (at + 1) * IMAGE_BLOCK]
        (visual_w, visual_d), (text_w, text_d) = outcome
        for part, sums, pieces, rows, scale in (
            (0, dk_sums, (visual_d, text_d), q_rows, SCORE_SCALE),
            (1, dv_sums, (visual_w, text_w), d_rows, 1.0),
        ):
            of_visual = (sums[0] + dot_nn(pieces[0], rows)) * scale
            of_text = (sums[1][:PROMPT] + dot_nn(pieces[1], rows)) * scale
            rest = sums[1][PROMPT:] * scale
            of_visual = of_visual.astype(jnp.bfloat16)
            dmine_ref[part, :, lanes] = of_visual[: VIS // 2]
            dpair_ref[part, : VIS // 2, lanes] = of_visual[VIS // 2 :]
            dpair_ref[part, VIS // 2 :, lanes] = of_text.astype(jnp.bfloat16)
            dhalo_ref[part, :, lanes] = rest[:halo].astype(jnp.bfloat16)
            down_ref[part, :, lanes] = rest[halo:]


def attend(
    number, masks, queries, cotangent, every_q, text, other_text, halo_kv, own_kv, blocks, windows
):
    heads = 2
    near_bias, whole_bias, image_bias = masks
    own = queries.shape[0]
    halo = halo_kv.shape[1]
    groups = every_q.shape[0]
    columns = PREFIX + halo + own
    products = RATIO * (own * columns + IMAGE_BLOCK * PREFIX) * KV_HEADS
    spec = pl.BlockSpec
    kv_spec = lambda rows: spec((2, rows, heads * HEAD_DIM), lambda at: (0, 0, at))
    q_spec = lambda rows: spec((rows, heads * GROUP_WIDTH), lambda at: (0, at))
    whole = lambda rows: spec((rows, 128), lambda at: (0, 0))
    return pl.pallas_call(
        functools.partial(attend_kernel, len(blocks), len(windows), heads, halo, own),
        grid=(KV_HEADS // heads,),
        in_specs=[
            spec(memory_space=pltpu.SMEM),
            whole(columns - VIS),
            whole(8),
            whole(PREFIX),
            q_spec(own),
            q_spec(own),
            spec((groups, IMAGE_BLOCK, heads * GROUP_WIDTH), lambda at: (0, 0, at)),
            kv_spec(PROMPT),
            kv_spec(PROMPT),
            kv_spec(halo),
            spec((1, 2, own, heads * HEAD_DIM), lambda at: (0, 0, 0, at)),
        ]
        + [kv_spec(block.shape[1]) for block in blocks]
        + [q_spec(IMAGE_BLOCK) for _ in windows],
        out_specs=[
            q_spec(own),
            q_spec(IMAGE_BLOCK),
            kv_spec(VIS // 2),
            kv_spec(VIS // 2 + PROMPT),
            kv_spec(halo),
            kv_spec(own),
        ],
        out_shape=[
            jax.ShapeDtypeStruct((own, Q_WIDTH), jnp.bfloat16),
            jax.ShapeDtypeStruct((IMAGE_BLOCK, Q_WIDTH), jnp.bfloat16),
            jax.ShapeDtypeStruct((2, VIS // 2, KV_WIDTH), jnp.bfloat16),
            jax.ShapeDtypeStruct((2, VIS // 2 + PROMPT, KV_WIDTH), jnp.bfloat16),
            jax.ShapeDtypeStruct((2, halo, KV_WIDTH), jnp.bfloat16),
            jax.ShapeDtypeStruct((2, own, KV_WIDTH), jnp.float32),
        ],
        cost_estimate=pl.CostEstimate(
            flops=10 * products * HEAD_DIM,
            bytes_accessed=12 * 1024 * 1024,
            transcendentals=products,
        ),
    )(
        number,
        near_bias,
        whole_bias,
        image_bias,
        queries,
        cotangent,
        every_q,
        text,
        other_text,
        halo_kv,
        own_kv,
        *blocks,
        *windows,
    )


def route(rows, number, back):
    groups = lax.axis_size("rollout")
    if groups != 4:
        every = lax.all_gather(rows, "rollout", axis=0)
        return lax.dynamic_index_in_dim(every, number[2 if back else 1], 0, keepdims=False)

    def branch(images):
        pairs = [(g, i) if back else (i, g) for g, i in enumerate(images)]
        return lambda moved: lax.ppermute(moved, "rollout", pairs)

    orders = itertools.permutations(range(groups))
    return lax.switch(number[0], [branch(images) for images in orders], rows)


def window_rounds(ctx_size, tok_rows, image_rows):
    rounds = []
    for target in range(ctx_size):
        lowest = (image_rows * target + 1) // tok_rows
        highest = (image_rows * target + image_rows - 1 + PROMPT - 1) // tok_rows
        for source in range(lowest, highest + 1):
            if source == target:
                continue
            for pairs in rounds:
                if all(s != source and t != target for s, t in pairs):
                    pairs.append((source, target))
                    break
            else:
                rounds.append([(source, target)])
    return rounds


def image_windows(windows, rounds):
    parts = [windows[0]] + [
        lax.ppermute(rows, "ctx", pairs) for rows, pairs in zip(windows[1:], rounds)
    ]
    if len(parts) > 8:
        parts = [sum(part.astype(jnp.float32) for part in parts).astype(jnp.bfloat16)]
    return parts


def text_strides(ctx_size, late_shard):
    strides = [1 << at for at in range(1, ctx_size.bit_length() - 1)]
    return [stride for stride in reversed(strides) if stride != late_shard]


def chip_steps(ctx_size):
    return list(range(2, ctx_size, 2))


def gather_prefix(image_kv):
    ctx_size = lax.axis_size("ctx")
    swap = [(at, at ^ 1) for at in range(ctx_size)]
    mine = [image_kv] + [
        lax.ppermute(image_kv, "ctx", [(at, at ^ step) for at in range(ctx_size)])
        for step in chip_steps(ctx_size)
    ]
    if len(mine) > 4:
        mine = [jnp.concatenate(mine, axis=1)]
    return mine + [lax.ppermute(block, "ctx", swap) for block in mine]


def reduce_prefix(d_mine, d_pair, image_rows, later):
    ctx_size = lax.axis_size("ctx")
    other = lax.ppermute(d_pair, "ctx", [(at, at ^ 1) for at in range(ctx_size)])
    chip = d_mine.astype(jnp.float32) + other[:, : VIS // 2].astype(jnp.float32)
    text = d_pair[:, VIS // 2 :].astype(jnp.float32) + other[:, VIS // 2 :].astype(jnp.float32)
    steps = chip_steps(ctx_size)
    rows = [
        chip[:, place * image_rows : (place + 1) * image_rows].astype(jnp.bfloat16)
        for place in range(1, len(steps) + 1)
    ]
    rows, later = lax.optimization_barrier((rows, later))
    total = chip[:, :image_rows]
    for step, part in zip(steps, rows):
        moved = lax.ppermute(part, "ctx", [(at, at ^ step) for at in range(ctx_size)])
        total = total + moved.astype(jnp.float32)
    return total, text.astype(jnp.bfloat16), later


def swap_text(text, late_shard):
    return lax.ppermute(text, "ctx", [(0, late_shard), (late_shard, 0)])


def spread_text(text, late_shard):
    ctx_size = lax.axis_size("ctx")
    holders = [0, late_shard]
    for stride in text_strides(ctx_size, late_shard):
        pairs = [(at, at + stride) for at in holders]
        text = text + lax.ppermute(text, "ctx", pairs)
        holders += [at + stride for at in holders]
    return text, lax.ppermute(text, "ctx", [(at, at + 1) for at in holders])


def collect_text(text, late_shard):
    ctx_size = lax.axis_size("ctx")

    def add(text, pairs):
        moved = lax.ppermute(text, "ctx", pairs)
        return (text.astype(jnp.float32) + moved.astype(jnp.float32)).astype(jnp.bfloat16)

    strides = text_strides(ctx_size, late_shard)
    for place in range(len(strides) - 1, -1, -1):
        holders = [0, late_shard]
        for stride in strides[:place]:
            holders += [at + stride for at in holders]
        text = add(text, [(at + strides[place], at) for at in holders])
    return text.astype(jnp.float32) + swap_text(text, late_shard).astype(jnp.float32)


def halo_cuts(tok_rows, halo):
    cuts = []
    left = halo
    while left > 0:
        cuts.append(min(left, tok_rows))
        left -= cuts[-1]
    return cuts


def halo_rows(tail, halo, tok_rows):
    ctx_size = lax.axis_size("ctx")
    parts = []
    for step, count in enumerate(halo_cuts(tok_rows, halo), 1):
        pairs = [(at, at + step) for at in range(ctx_size - step)]
        rows = tail if count == tail.shape[1] else tail[:, tail.shape[1] - count :]
        parts.insert(0, lax.ppermute(rows, "ctx", pairs))
    return jnp.concatenate(parts, axis=1) if len(parts) > 1 else parts[0]


def halo_return(d_halo, tok_rows):
    halo = d_halo.shape[1]
    ctx_size = lax.axis_size("ctx")
    total = None
    end = halo
    for step, count in enumerate(halo_cuts(tok_rows, halo), 1):
        pairs = [(at + step, at) for at in range(ctx_size - step)]
        part = lax.ppermute(d_halo[:, end - count : end], "ctx", pairs).astype(jnp.float32)
        part = jnp.pad(part, ((0, 0), (tok_rows - count, 0), (0, 0)))
        total = part if total is None else total + part
        end -= count
    return total


def gather_queries(image_q):
    every = lax.all_gather(image_q, "rollout", axis=0)
    missing = IMAGE_BLOCK - every.shape[1]
    return jnp.pad(every, ((0, 0), (0, missing), (0, 0))) if missing else every


def per_device(queries, keys_values, image_rows, cotangent, seq_image, vis_start, comp_lengths):
    tok_rows = queries.shape[1]
    image_count = image_rows.shape[1]
    ctx_size = lax.axis_size("ctx")
    here = lax.axis_index("ctx")
    seq_len = tok_rows * ctx_size
    late_shard = VIS // tok_rows
    longest = 4 * (seq_len - PREFIX) // (3 * NCOMP)
    halo = -(-(longest - 1) // 64) * 64
    q_own, d_own = queries[0], cotangent[0]

    number, image_kv, image_q, text, tail = first_arrays(
        seq_image, vis_start, image_rows, keys_values, halo
    )
    every_q = gather_queries(image_q)
    swapped = swap_text(text, late_shard)
    image_kv = route(image_kv, number, False)
    blocks = gather_prefix(image_kv)
    image_kv, d_later = lax.optimization_barrier((image_kv, d_own))
    windows, rounds, (*masks, text) = second_arrays(
        vis_start, comp_lengths, d_later, text, swapped, image_count, halo
    )
    windows = image_windows(windows, rounds)
    text, other_text = spread_text(text, late_shard)
    halo_kv = halo_rows(tail, halo, tok_rows)

    grad_q, d_image_q, d_mine, d_pair, d_halo, d_own_kv = attend(
        number,
        masks,
        q_own,
        d_own,
        every_q,
        text,
        other_text,
        halo_kv,
        keys_values,
        blocks,
        windows,
    )

    sums, d_text, d_image_q = reduce_prefix(d_mine, d_pair, image_count, d_image_q)
    image_dq = route(d_image_q[:image_count], number, True)
    d_text, d_halo, image_dq = lax.optimization_barrier((d_text, d_halo, image_dq))
    text_at = jnp.arange(PROMPT, dtype=jnp.int32)
    text_here = jnp.where(text_at < vis_start[0], here == 0, here == late_shard)[None, :, None]
    text_part = jnp.where(text_here, collect_text(d_text, late_shard), 0.0)
    text_part = jnp.pad(text_part, ((0, 0), (0, tok_rows - PROMPT), (0, 0)))
    grad_kv = (d_own_kv + halo_return(d_halo, tok_rows) + text_part).astype(jnp.bfloat16)
    grad_image = jnp.pad(image_dq, ((0, 0), (0, 2 * KV_WIDTH)))
    sums, grad_image = lax.optimization_barrier((sums, grad_image))
    sums = jnp.concatenate([sums[0], sums[1]], axis=1).astype(jnp.bfloat16)
    image_dkv = route(sums, number, True)
    grad_image = lax.dynamic_update_slice(grad_image, image_dkv, (0, Q_WIDTH))
    return (grad_q[None], grad_kv[None], grad_image[None])


def solution(mesh):
    placed = (
        P("rollout", "ctx", None),
        P("rollout", None, "ctx", None),
        P("rollout", "ctx", None),
        P("rollout", "ctx", None),
        P(),
        P("rollout"),
        P("rollout", None),
    )
    return jax.shard_map(
        per_device,
        mesh=mesh,
        in_specs=placed,
        out_specs=(
            P("rollout", "ctx", None),
            P("rollout", None, "ctx", None),
            P("rollout", "ctx", None),
        ),
        check_vma=False,
    )
```

```python
import functools
import itertools
import math

import jax
import jax.numpy as jnp
from jax import lax
from jax.experimental import pallas as pl
from jax.experimental.pallas import tpu as pltpu
from jax.sharding import PartitionSpec as P

HEADS = 32
KV_HEADS = 8
HEAD_DIM = 128
VIS = 256
PROMPT = 64
NCOMP = 16

RATIO = HEADS // KV_HEADS
PREFIX = VIS + PROMPT
Q_WIDTH = HEADS * HEAD_DIM
KV_WIDTH = KV_HEADS * HEAD_DIM
GROUP_WIDTH = RATIO * HEAD_DIM
IMAGE_BLOCK = 32
HIDDEN = -1e30
SCORE_SCALE = 1.0 / math.sqrt(HEAD_DIM)


def dot_nt(left, right):
    return lax.dot_general(
        left, right, (((1,), (1,)), ((), ())), preferred_element_type=jnp.float32
    )


def dot_nn(left, right):
    return lax.dot_general(
        left, right, (((1,), (0,)), ((), ())), preferred_element_type=jnp.float32
    )


def dot_tn(left, right):
    return lax.dot_general(
        left, right, (((0,), (0,)), ((), ())), preferred_element_type=jnp.float32
    )


def first_kernel(halo, seq_ref, vis_ref, image_ref, kv_ref, number_ref, *out_refs):
    ikv_ref, iq_ref, text_ref, tail_ref = out_refs
    groups = seq_ref.shape[0]
    group = lax.axis_index("rollout")
    here = lax.axis_index("ctx")
    images = [seq_ref[at] for at in range(groups)]
    number = jnp.int32(0)
    if groups == 4:
        for at, weight in enumerate((6, 2, 1)):
            for later in range(at + 1, groups):
                number = number + jnp.where(images[later] < images[at], weight, 0)
    place = jnp.int32(0)
    user = jnp.int32(0)
    for at in range(groups):
        place = place + jnp.where(group == at, images[at], 0)
        user = user + jnp.where(images[at] == group, at, 0)
    number_ref[0] = number
    number_ref[1] = place
    number_ref[2] = user
    iq_ref[...] = image_ref[0, :, :Q_WIDTH]
    ikv_ref[0] = image_ref[0, :, Q_WIDTH : Q_WIDTH + KV_WIDTH]
    ikv_ref[1] = image_ref[0, :, Q_WIDTH + KV_WIDTH :]
    tok_rows = kv_ref.shape[2]
    late_shard = VIS // tok_rows
    at = lax.broadcasted_iota(jnp.int32, (PROMPT, KV_WIDTH), 0)
    ahead = jnp.where(here == 0, 1, 0)
    behind = jnp.where(here == late_shard, 1, 0)
    kept = jnp.where(at < vis_ref[0], ahead, behind) == 1
    for part in range(2):
        rows = kv_ref[0, part, :PROMPT].astype(jnp.float32)
        text_ref[part] = jnp.where(kept, rows, 0.0).astype(jnp.bfloat16)
        tail_ref[part] = kv_ref[0, part, tok_rows - halo :]


def first_arrays(seq_image, vis_start, image_rows, keys_values, halo):
    rows = image_rows.shape[1]
    smem = pl.BlockSpec(memory_space=pltpu.SMEM)
    vmem = pl.BlockSpec(memory_space=pltpu.VMEM)
    tail = min(halo, keys_values.shape[2])
    return pl.pallas_call(
        functools.partial(first_kernel, tail),
        in_specs=[smem, smem, vmem, vmem],
        out_specs=[smem, vmem, vmem, vmem, vmem],
        out_shape=[
            jax.ShapeDtypeStruct((3,), jnp.int32),
            jax.ShapeDtypeStruct((2, rows, KV_WIDTH), jnp.bfloat16),
            jax.ShapeDtypeStruct((rows, Q_WIDTH), jnp.bfloat16),
            jax.ShapeDtypeStruct((2, PROMPT, KV_WIDTH), jnp.bfloat16),
            jax.ShapeDtypeStruct((2, tail, KV_WIDTH), jnp.bfloat16),
        ],
    )(seq_image, vis_start, image_rows, keys_values)


def segments(positions, length_ref):
    end = jnp.int32(PREFIX)
    segment = jnp.where(positions < PREFIX, 0, 1)
    for at in range(NCOMP):
        end = end + length_ref[0, at]
        segment = segment + jnp.where(positions >= end, 1, 0)
    return segment


def hide(visible):
    return jnp.where(visible, 0.0, HIDDEN)


def second_kernel(
    rounds, tok_rows, image_rows, halo, vis_ref, length_ref, d_ref, *out_refs
):
    *window_refs, near_ref, whole_ref, image_ref = out_refs
    here = lax.axis_index("ctx")
    ctx_size = lax.axis_size("ctx")
    row = lax.broadcasted_iota(jnp.int32, (IMAGE_BLOCK, tok_rows), 0)
    column = lax.broadcasted_iota(jnp.int32, (IMAGE_BLOCK, tok_rows), 1)
    place = jnp.where(row < image_rows, row, 1 << 20)
    picks = []
    for pairs in [[]] + rounds:
        target = here
        for source, other in pairs:
            target = jnp.where(here == source, other, target)
        begin = vis_ref[0] + image_rows * target - tok_rows * here
        picks.append(jnp.where(column == place + begin, 1.0, 0.0).astype(jnp.bfloat16))
    picked = dot_nn(jnp.concatenate(picks, axis=0), d_ref[...]).astype(jnp.bfloat16)
    for at, window_ref in enumerate(window_refs):
        window_ref[...] = picked[at * IMAGE_BLOCK : (at + 1) * IMAGE_BLOCK]

    @pl.when(pl.program_id(0) == 0)
    def _():
        vis = vis_ref[0]
        own_at = lax.broadcasted_iota(jnp.int32, (8, tok_rows), 1) + here * tok_rows
        own_segment = segments(own_at, length_ref)[:1]
        placeholder = (own_at >= vis) & (own_at < vis + VIS)
        own_row = jnp.where(placeholder, -1, own_at)
        whole_ref[...] = hide(own_row >= vis + VIS).astype(jnp.float32)
        own_row = own_row[:1]
        image_at = lax.broadcasted_iota(jnp.int32, (1, RATIO * IMAGE_BLOCK), 1) % IMAGE_BLOCK
        image_row = jnp.where(image_at < image_rows, vis + here * image_rows + image_at, -1)
        text_at = lax.broadcasted_iota(jnp.int32, (PROMPT, tok_rows), 0)
        text_at = text_at + jnp.where(text_at < vis, 0, VIS)
        near_ref[:PROMPT] = hide(text_at <= own_row)
        near_at = lax.broadcasted_iota(jnp.int32, (halo + tok_rows, tok_rows), 0)
        near_at = near_at + (here * tok_rows - halo)
        sees = (near_at <= own_row) & (near_at >= PREFIX)
        sees = sees & (segments(near_at, length_ref) == own_segment)
        near_ref[PROMPT:] = hide(sees)
        at = 0
        for core in range(2):
            for step in range(0, ctx_size, 2):
                begin = (here ^ (step + core)) * image_rows + vis
                shape = (image_rows, RATIO * IMAGE_BLOCK)
                block_at = lax.broadcasted_iota(jnp.int32, shape, 0) + begin
                image_ref[at : at + image_rows] = hide(block_at <= image_row)
                at += image_rows
        image_ref[VIS:] = hide(text_at <= image_row)


def second_arrays(vis_start, lengths, cotangent, image_rows, halo):
    tok_rows, width = cotangent.shape
    rounds = window_rounds(lax.axis_size("ctx"), tok_rows, image_rows)
    count = len(rounds) + 1
    block = 2048
    spec = pl.BlockSpec
    smem = spec(memory_space=pltpu.SMEM)
    lanes = RATIO * IMAGE_BLOCK
    near = PROMPT + halo + tok_rows
    whole = lambda *shape: spec(shape, lambda at: (0,) * len(shape))
    out = pl.pallas_call(
        functools.partial(second_kernel, rounds, tok_rows, image_rows, halo),
        grid=(width // block,),
        in_specs=[smem, smem, spec((tok_rows, block), lambda at: (0, at))],
        out_specs=[spec((IMAGE_BLOCK, block), lambda at: (0, at)) for _ in range(count)]
        + [whole(near, tok_rows), whole(8, tok_rows), whole(PREFIX, lanes)],
        out_shape=[jax.ShapeDtypeStruct((IMAGE_BLOCK, width), jnp.bfloat16) for _ in range(count)]
        + [
            jax.ShapeDtypeStruct((near, tok_rows), jnp.float32),
            jax.ShapeDtypeStruct((8, tok_rows), jnp.float32),
            jax.ShapeDtypeStruct((PREFIX, lanes), jnp.float32),
        ],
        cost_estimate=pl.CostEstimate(
            flops=2 * count * IMAGE_BLOCK * tok_rows * width,
            bytes_accessed=8 * 1024 * 1024,
            transcendentals=0,
        ),
    )(vis_start, lengths, cotangent)
    return out[:count], rounds, list(out[count:])


def rows_backward(parts, q_rows, d_rows):
    scale = SCORE_SCALE * math.log2(math.e)
    scores = []
    for keys, values, bias in parts:
        raw = dot_nt(keys, q_rows) * scale
        scores.append(raw if bias.shape[0] == 1 else raw + bias)
    tops = [jnp.max(part, axis=0, keepdims=True) for part in scores]
    tops = [
        top + bias if bias.shape[0] == 1 else top for top, (_, _, bias) in zip(tops, parts)
    ]
    top = functools.reduce(jnp.maximum, tops)
    total = 0.0
    mix = 0.0
    kept = []
    for part, (keys, values, bias) in zip(scores, parts):
        shift = bias - top if bias.shape[0] == 1 else -top
        terms = jnp.exp2(part + shift)
        d_weights = dot_nt(values, d_rows)
        total = total + jnp.sum(terms, axis=0, keepdims=True)
        mix = mix + jnp.sum(terms * d_weights, axis=0, keepdims=True)
        kept.append((terms, d_weights))
    inverse = jnp.where(top > 0.5 * HIDDEN, 1.0 / total, 0.0)
    delta = mix * inverse
    outcome = []
    for terms, d_weights in kept:
        weights = terms * inverse
        d_scores = weights * (d_weights - delta)
        outcome.append((weights.astype(jnp.bfloat16), d_scores.astype(jnp.bfloat16)))
    return outcome


def total_of(values):
    if len(values) == 1:
        return values[0]
    return sum(value.astype(jnp.float32) for value in values).astype(jnp.bfloat16)


def attend_kernel(
    block_rows,
    block_count,
    text_count,
    window_count,
    heads,
    halo,
    own,
    number_ref,
    near_ref,
    whole_ref,
    image_bias_ref,
    q_ref,
    d_ref,
    iq_ref,
    halo_ref,
    own_ref,
    *refs,
):
    block_refs, refs = refs[:block_count], refs[block_count:]
    text_refs, refs = refs[:text_count], refs[text_count:]
    window_refs, refs = refs[:window_count], refs[window_count:]
    dq_ref, diq_ref, dmine_ref, dpair_ref, dhalo_ref, down_ref = refs
    text_refs = text_refs or [ref for ref in block_refs if ref.shape[1] > block_rows]
    near_bias = jnp.concatenate([near_ref[...]] * 2, axis=1)
    whole_bias = jnp.concatenate([whole_ref[:1]] * 2, axis=1)
    image_cotangent = total_of([ref[...] for ref in window_refs])
    for head in range(heads):
        lanes = slice(head * HEAD_DIM, (head + 1) * HEAD_DIM)
        spans = [
            slice((head * RATIO + at) * HEAD_DIM, (head * RATIO + at + 1) * HEAD_DIM)
            for at in range(RATIO)
        ]
        visual, text, near = [], [], []
        for part in range(2):
            visual.append(
                jnp.concatenate([ref[part, :block_rows, lanes] for ref in block_refs], axis=0)
            )
            text.append(total_of([ref[part, -PROMPT:, lanes] for ref in text_refs]))
            near.append(
                jnp.concatenate(
                    [text[part], halo_ref[part, :, lanes], own_ref[0, part, :, lanes]], axis=0
                )
            )
        keys = jnp.concatenate([visual[0], near[0]], axis=0)
        dk_sums = [0.0, 0.0]
        dv_sums = [0.0, 0.0]
        for first in range(0, RATIO, 2):
            pair = spans[first : first + 2]
            q_rows = jnp.concatenate([q_ref[:, span] for span in pair], axis=0)
            d_rows = jnp.concatenate([d_ref[:, span] for span in pair], axis=0)
            outcome = rows_backward(
                [(visual[0], visual[1], whole_bias), (near[0], near[1], near_bias)],
                q_rows,
                d_rows,
            )
            d_scores = jnp.concatenate([part[1] for part in outcome], axis=0)
            dq = dot_tn(keys, d_scores) * SCORE_SCALE
            for at, span in enumerate(pair):
                dq_ref[:, span] = dq[:, at * own : (at + 1) * own].T.astype(jnp.bfloat16)
            for at, (weights, d_part) in enumerate(outcome):
                dk_sums[at] = dk_sums[at] + dot_nn(d_part, q_rows)
                dv_sums[at] = dv_sums[at] + dot_nn(weights, d_rows)
        image_queries = iq_ref[number_ref[1]]
        q_rows = jnp.concatenate([image_queries[:, span] for span in spans], axis=0)
        d_rows = jnp.concatenate([image_cotangent[:, span] for span in spans], axis=0)
        outcome = rows_backward(
            [
                (visual[0], visual[1], image_bias_ref[:VIS]),
                (text[0], text[1], image_bias_ref[VIS:]),
            ],
            q_rows,
            d_rows,
        )
        d_scores = jnp.concatenate([part[1] for part in outcome], axis=0)
        dq = (dot_tn(keys[:PREFIX], d_scores) * SCORE_SCALE).T.astype(jnp.bfloat16)
        for at, span in enumerate(spans):
            diq_ref[:, span] = dq[at * IMAGE_BLOCK : (at + 1) * IMAGE_BLOCK]
        (visual_w, visual_d), (text_w, text_d) = outcome
        for part, sums, pieces, rows, scale in (
            (0, dk_sums, (visual_d, text_d), q_rows, SCORE_SCALE),
            (1, dv_sums, (visual_w, text_w), d_rows, 1.0),
        ):
            of_visual = (sums[0] + dot_nn(pieces[0], rows)) * scale
            of_text = (sums[1][:PROMPT] + dot_nn(pieces[1], rows)) * scale
            rest = sums[1][PROMPT:] * scale
            of_visual = of_visual.astype(jnp.bfloat16)
            dmine_ref[part, :, lanes] = of_visual[: VIS // 2]
            dpair_ref[part, : VIS // 2, lanes] = of_visual[VIS // 2 :]
            dpair_ref[part, VIS // 2 :, lanes] = of_text.astype(jnp.bfloat16)
            dhalo_ref[part, :, lanes] = rest[:halo].astype(jnp.bfloat16)
            down_ref[part, :, lanes] = rest[halo:]


def attend(
    number, masks, queries, cotangent, every_q, halo_kv, own_kv, blocks, texts, windows
):
    heads = 2
    near_bias, whole_bias, image_bias = masks
    own = queries.shape[0]
    halo = halo_kv.shape[1]
    groups = every_q.shape[0]
    columns = PREFIX + halo + own
    products = RATIO * (own * columns + IMAGE_BLOCK * PREFIX) * KV_HEADS
    spec = pl.BlockSpec
    kv_spec = lambda rows: spec((2, rows, heads * HEAD_DIM), lambda at: (0, 0, at))
    q_spec = lambda rows: spec((rows, heads * GROUP_WIDTH), lambda at: (0, at))
    whole = lambda rows: spec((rows, 128), lambda at: (0, 0))
    return pl.pallas_call(
        functools.partial(
            attend_kernel,
            VIS // len(blocks),
            len(blocks),
            len(texts),
            len(windows),
            heads,
            halo,
            own,
        ),
        grid=(KV_HEADS // heads,),
        in_specs=[
            spec(memory_space=pltpu.SMEM),
            whole(columns - VIS),
            whole(8),
            whole(PREFIX),
            q_spec(own),
            q_spec(own),
            spec((groups, IMAGE_BLOCK, heads * GROUP_WIDTH), lambda at: (0, 0, at)),
            kv_spec(halo),
            spec((1, 2, own, heads * HEAD_DIM), lambda at: (0, 0, 0, at)),
        ]
        + [kv_spec(block.shape[1]) for block in [*blocks, *texts]]
        + [q_spec(IMAGE_BLOCK) for _ in windows],
        out_specs=[
            q_spec(own),
            q_spec(IMAGE_BLOCK),
            kv_spec(VIS // 2),
            kv_spec(VIS // 2 + PROMPT),
            kv_spec(halo),
            kv_spec(own),
        ],
        out_shape=[
            jax.ShapeDtypeStruct((own, Q_WIDTH), jnp.bfloat16),
            jax.ShapeDtypeStruct((IMAGE_BLOCK, Q_WIDTH), jnp.bfloat16),
            jax.ShapeDtypeStruct((2, VIS // 2, KV_WIDTH), jnp.bfloat16),
            jax.ShapeDtypeStruct((2, VIS // 2 + PROMPT, KV_WIDTH), jnp.bfloat16),
            jax.ShapeDtypeStruct((2, halo, KV_WIDTH), jnp.bfloat16),
            jax.ShapeDtypeStruct((2, own, KV_WIDTH), jnp.float32),
        ],
        cost_estimate=pl.CostEstimate(
            flops=10 * products * HEAD_DIM,
            bytes_accessed=12 * 1024 * 1024,
            transcendentals=products,
        ),
    )(
        number,
        near_bias,
        whole_bias,
        image_bias,
        queries,
        cotangent,
        every_q,
        halo_kv,
        own_kv,
        *blocks,
        *texts,
        *windows,
    )


def route(rows, number, back, beside=()):
    groups = lax.axis_size("rollout")
    arrays = [array for array, _ in beside]

    def move_beside(arrays):
        return [lax.ppermute(array, "ctx", pairs) for array, (_, pairs) in zip(arrays, beside)]

    if groups != 4:
        every = lax.all_gather(rows, "rollout", axis=0)
        picked = lax.dynamic_index_in_dim(every, number[2 if back else 1], 0, keepdims=False)
        return [picked] + move_beside(arrays)

    def branch(images):
        pairs = [(g, i) if back else (i, g) for g, i in enumerate(images)]
        if all(source == target for source, target in pairs):
            return lambda rows, arrays: [rows] + move_beside(arrays)
        return lambda rows, arrays: [lax.ppermute(rows, "rollout", pairs)] + move_beside(arrays)

    orders = itertools.permutations(range(groups))
    return lax.switch(number[0], [branch(images) for images in orders], rows, arrays)


def window_rounds(ctx_size, tok_rows, image_rows):
    rounds = []
    for target in range(ctx_size):
        lowest = (image_rows * target + 1) // tok_rows
        highest = (image_rows * target + image_rows - 1 + PROMPT - 1) // tok_rows
        for source in range(lowest, highest + 1):
            if source == target:
                continue
            for pairs in rounds:
                if all(s != source and t != target for s, t in pairs):
                    pairs.append((source, target))
                    break
            else:
                rounds.append([(source, target)])
    return rounds


def window_beside(ctx_size, rounds):
    return [2, 3, 4] if ctx_size == 8 and len(rounds) == 6 else []


def image_windows(windows, rounds, beside, moved):
    moved = dict(zip(beside, moved))
    parts = [windows[0]]
    for at, (rows, pairs) in enumerate(zip(windows[1:], rounds)):
        parts.append(moved[at] if at in moved else lax.ppermute(rows, "ctx", pairs))
    if len(parts) > 8:
        parts = [sum(part.astype(jnp.float32) for part in parts).astype(jnp.bfloat16)]
    return parts


def xor_pairs(step):
    return [(at, at ^ step) for at in range(lax.axis_size("ctx"))]


def xor_permute(rows, step):
    return lax.ppermute(rows, "ctx", xor_pairs(step))


def on_device(function, *arrays):
    if lax.axis_size("ctx") != 8:
        return function(*arrays)
    block = KV_WIDTH // 2
    shapes = jax.eval_shape(function, *arrays)

    def kernel(*refs):
        for out_ref, value in zip(
            refs[len(arrays) :], function(*[ref[...] for ref in refs[: len(arrays)]])
        ):
            out_ref[...] = value

    spec = lambda array: pl.BlockSpec(array.shape[:2] + (block,), lambda at: (0, 0, at))
    return pl.pallas_call(
        kernel,
        grid=(2,),
        in_specs=[spec(array) for array in arrays],
        out_specs=[spec(shape) for shape in shapes],
        out_shape=[jax.ShapeDtypeStruct(shape.shape, shape.dtype) for shape in shapes],
        cost_estimate=pl.CostEstimate(flops=1, bytes_accessed=1, transcendentals=0),
    )(*arrays)


def text_strides(ctx_size, late_shard):
    strides = [1 << at for at in range(1, ctx_size.bit_length() - 1)]
    return [stride for stride in reversed(strides) if stride != late_shard]


def chip_steps(ctx_size):
    return list(range(2, ctx_size, 2))


def join_text(image_kv, text, received):
    return [jnp.concatenate([image_kv, add_text(text, received)], axis=1)]


def add_text(text, received):
    return (text.astype(jnp.float32) + received.astype(jnp.float32)).astype(jnp.bfloat16)


def gather_prefix(image_kv, text, received, late_shard):
    ctx_size = lax.axis_size("ctx")
    steps = chip_steps(ctx_size)
    if ctx_size == 8:
        (text,) = on_device(join_text, image_kv, text, received)
        mine = [text, xor_permute(image_kv, 2), xor_permute(text, 4), xor_permute(image_kv, 6)]
        pair = [xor_permute(mine[0], 1)]
        for at, earlier in ((1, None), (3, 0), (2, 1)):
            block = mine[at]
            if earlier is not None:
                block, pair[earlier] = lax.optimization_barrier((block, pair[earlier]))
            pair.append(xor_permute(block, 1))
        return mine + [pair[0], pair[1], pair[3], pair[2]], []
    mine = jnp.concatenate(
        [image_kv] + [xor_permute(image_kv, step) for step in steps], axis=1
    )
    return [mine, xor_permute(mine, 1)], list(spread_text(add_text(text, received), late_shard))


def split_sums(image_rows, steps, d_mine, d_pair, other):
    half = VIS // 2
    add = lambda one, two: one.astype(jnp.float32) + two.astype(jnp.float32)
    text = add(d_pair[:, half:], other[:, half:])
    out = []
    for at in range(len(steps) + 1):
        rows = slice(at * image_rows, (at + 1) * image_rows)
        sums = add(d_mine[:, rows], other[:, rows])
        if len(steps) == 3 and steps[at - 1] == 4 and at:
            sums = jnp.concatenate([sums, text], axis=1)
        out.append(sums.astype(jnp.bfloat16) if at else sums)
    return out + [text]


def add_sums(image_rows, own, text, *parts):
    for part in parts:
        own = own + part[:, :image_rows].astype(jnp.float32)
        if part.shape[1] > image_rows:
            text = text + part[:, image_rows:].astype(jnp.float32)
    return [own.astype(jnp.bfloat16), text.astype(jnp.bfloat16)]


def spread_text(text, late_shard):
    for stride in text_strides(lax.axis_size("ctx"), late_shard):
        text = text + xor_permute(text, stride)
    return text, xor_permute(text, 1)


def collect_text(text, late_shard):
    for stride in reversed(text_strides(lax.axis_size("ctx"), late_shard)):
        moved = xor_permute(text.astype(jnp.bfloat16), stride)
        text = text.astype(jnp.float32) + moved.astype(jnp.float32)
    return text.astype(jnp.bfloat16)


def halo_cuts(tok_rows, halo):
    cuts = []
    left = halo
    while left > 0:
        cuts.append(min(left, tok_rows))
        left -= cuts[-1]
    return cuts


def halo_rows(tail, halo, tok_rows):
    ctx_size = lax.axis_size("ctx")
    parts = []
    for step, count in enumerate(halo_cuts(tok_rows, halo), 1):
        pairs = [(at, at + step) for at in range(ctx_size - step)]
        rows = tail if count == tail.shape[1] else tail[:, tail.shape[1] - count :]
        parts.insert(0, lax.ppermute(rows, "ctx", pairs))
    return jnp.concatenate(parts, axis=1) if len(parts) > 1 else parts[0]


def halo_parts(d_halo, tok_rows):
    ctx_size = lax.axis_size("ctx")
    cuts = halo_cuts(tok_rows, d_halo.shape[1])
    parts = []
    end = d_halo.shape[1]
    for step, count in enumerate(cuts, 1):
        rows = d_halo if len(cuts) == 1 else d_halo[:, end - count : end]
        parts.append((rows, [(at + step, at) for at in range(ctx_size - step)]))
        end -= count
    return parts


def last_kernel(
    number_ref, vis_ref, dq_ref, dkv_ref, down_ref, text_ref, other_ref, *refs
):
    *part_refs, image_ref, kv_ref = refs
    here = lax.axis_index("ctx")
    tok_rows = down_ref.shape[1]
    image_ref[0, :, :Q_WIDTH] = dq_ref[0]
    image_ref[0, :, Q_WIDTH : Q_WIDTH + KV_WIDTH] = dkv_ref[0]
    image_ref[0, :, Q_WIDTH + KV_WIDTH :] = dkv_ref[1]
    at = lax.broadcasted_iota(jnp.int32, (PROMPT, KV_WIDTH), 0)
    ahead = jnp.where(here == 0, 1, 0)
    behind = jnp.where(here == VIS // tok_rows, 1, 0)
    kept = jnp.where(at < vis_ref[0], ahead, behind) == 1
    for part in range(2):
        text = text_ref[part].astype(jnp.float32) + other_ref[part].astype(jnp.float32)
        text = jnp.where(kept, text, 0.0)
        sums = down_ref[part] + jnp.concatenate(
            [text, jnp.zeros((tok_rows - PROMPT, KV_WIDTH), jnp.float32)], axis=0
        )
        for part_ref in part_refs:
            back = part_ref[part].astype(jnp.float32)
            if back.shape[0] < tok_rows:
                missing = jnp.zeros((tok_rows - back.shape[0], KV_WIDTH), jnp.float32)
                back = jnp.concatenate([missing, back], axis=0)
            sums = sums + back
        kv_ref[0, part] = sums.astype(jnp.bfloat16)


def last_arrays(number, vis_start, every_dq, image_dkv, d_own_kv, text, other_text, parts):
    rows = image_dkv.shape[1]
    whole = lambda array: pl.BlockSpec(array.shape, lambda at, number: (0,) * len(array.shape))
    kept = [image_dkv, d_own_kv, text, other_text, *parts]
    shapes = [
        jax.ShapeDtypeStruct((1, rows, Q_WIDTH + 2 * KV_WIDTH), jnp.bfloat16),
        jax.ShapeDtypeStruct((1,) + d_own_kv.shape, jnp.bfloat16),
    ]
    return pl.pallas_call(
        last_kernel,
        grid_spec=pltpu.PrefetchScalarGridSpec(
            num_scalar_prefetch=1,
            grid=(1,),
            in_specs=[
                pl.BlockSpec(memory_space=pltpu.SMEM),
                pl.BlockSpec((1, rows, Q_WIDTH), lambda at, number: (number[2], 0, 0)),
            ]
            + [whole(array) for array in kept],
            out_specs=[whole(shape) for shape in shapes],
        ),
        out_shape=shapes,
    )(number, vis_start, every_dq, *kept)


def gather_queries(image_q):
    every = lax.all_gather(image_q, "rollout", axis=0)
    missing = IMAGE_BLOCK - every.shape[1]
    return jnp.pad(every, ((0, 0), (0, missing), (0, 0))) if missing else every


def per_device(queries, keys_values, image_rows, cotangent, seq_image, vis_start, comp_lengths):
    tok_rows = queries.shape[1]
    image_count = image_rows.shape[1]
    ctx_size = lax.axis_size("ctx")
    seq_len = tok_rows * ctx_size
    late_shard = VIS // tok_rows
    longest = 4 * (seq_len - PREFIX) // (3 * NCOMP)
    halo = -(-(longest - 1) // 64) * 64
    q_own, d_own = queries[0], cotangent[0]

    number, image_kv, image_q, text, tail = first_arrays(
        seq_image, vis_start, image_rows, keys_values, halo
    )
    every_q = gather_queries(image_q)
    windows, rounds, masks = second_arrays(vis_start, comp_lengths, d_own, image_count, halo)
    beside = window_beside(ctx_size, rounds)
    image_kv, received, *moved = route(
        image_kv,
        number,
        False,
        [(text, xor_pairs(late_shard))] + [(windows[at + 1], rounds[at]) for at in beside],
    )
    windows = image_windows(windows, rounds, beside, moved)
    blocks, texts = gather_prefix(image_kv, text, received, late_shard)
    halo_kv = halo_rows(tail, halo, tok_rows)

    grad_q, d_image_q, d_mine, d_pair, d_halo, d_own_kv = attend(
        number,
        masks,
        q_own,
        d_own,
        every_q,
        halo_kv,
        keys_values,
        blocks,
        texts,
        windows,
    )

    every_dq = lax.all_gather(d_image_q[:image_count], "rollout", axis=0)
    steps = chip_steps(ctx_size)
    other = xor_permute(d_pair, 1)
    own, *sent, d_text = on_device(
        functools.partial(split_sums, image_count, steps), d_mine, d_pair, other
    )
    moved = [xor_permute(rows, step) for rows, step in zip(sent, steps)]
    halo_back = [
        lax.ppermute(rows, "ctx", pairs) for rows, pairs in halo_parts(d_halo, tok_rows)
    ]
    sums, d_text = on_device(functools.partial(add_sums, image_count), own, d_text, *moved)
    if ctx_size != 8:
        d_text = collect_text(d_text, late_shard)
    image_dkv, other_text = route(sums, number, True, [(d_text, xor_pairs(late_shard))])
    grad_image, grad_kv = last_arrays(
        number, vis_start, every_dq, image_dkv, d_own_kv, d_text, other_text, halo_back
    )
    return (grad_q[None], grad_kv, grad_image)


def solution(mesh):
    placed = (
        P("rollout", "ctx", None),
        P("rollout", None, "ctx", None),
        P("rollout", "ctx", None),
        P("rollout", "ctx", None),
        P(),
        P("rollout"),
        P("rollout", None),
    )
    return jax.shard_map(
        per_device,
        mesh=mesh,
        in_specs=placed,
        out_specs=(
            P("rollout", "ctx", None),
            P("rollout", None, "ctx", None),
            P("rollout", "ctx", None),
        ),
        check_vma=False,
    )
```

```python
import functools
import itertools
import math

import jax
import jax.numpy as jnp
from jax import lax
from jax.experimental import pallas as pl
from jax.experimental.pallas import tpu as pltpu
from jax.sharding import PartitionSpec as P

HEADS = 32
KV_HEADS = 8
HEAD_DIM = 128
VIS = 256
PROMPT = 64
NCOMP = 16

RATIO = HEADS // KV_HEADS
PREFIX = VIS + PROMPT
Q_WIDTH = HEADS * HEAD_DIM
KV_WIDTH = KV_HEADS * HEAD_DIM
GROUP_WIDTH = RATIO * HEAD_DIM
IMAGE_BLOCK = 32
IMAGE_HALF = IMAGE_BLOCK // 2
HIDDEN = -1e30
SCORE_SCALE = 1.0 / math.sqrt(HEAD_DIM)


def dot_nt(left, right):
    return lax.dot_general(
        left, right, (((1,), (1,)), ((), ())), preferred_element_type=jnp.float32
    )


def dot_nn(left, right):
    return lax.dot_general(
        left, right, (((1,), (0,)), ((), ())), preferred_element_type=jnp.float32
    )


def dot_tn(left, right):
    return lax.dot_general(
        left, right, (((0,), (0,)), ((), ())), preferred_element_type=jnp.float32
    )


def send_first(halo, seq_ref, vis_ref, image_ref, kv_ref, number_ref, *out_refs):
    ikv_ref, iq_ref, text_ref, tail_ref = out_refs
    groups = seq_ref.shape[0]
    group = lax.axis_index("rollout")
    here = lax.axis_index("ctx")
    images = [seq_ref[at] for at in range(groups)]
    number = jnp.int32(0)
    if groups == 4:
        for at, weight in enumerate((6, 2, 1)):
            for later in range(at + 1, groups):
                number = number + jnp.where(images[later] < images[at], weight, 0)
    place = jnp.int32(0)
    user = jnp.int32(0)
    for at in range(groups):
        place = place + jnp.where(group == at, images[at], 0)
        user = user + jnp.where(images[at] == group, at, 0)
    number_ref[0] = number
    number_ref[1] = place
    number_ref[2] = user
    iq_ref[...] = image_ref[0, :, :Q_WIDTH]
    ikv_ref[0] = image_ref[0, :, Q_WIDTH : Q_WIDTH + KV_WIDTH]
    ikv_ref[1] = image_ref[0, :, Q_WIDTH + KV_WIDTH :]
    tok_rows = kv_ref.shape[2]
    late_shard = VIS // tok_rows
    at = lax.broadcasted_iota(jnp.int32, (PROMPT, KV_WIDTH), 0)
    ahead = jnp.where(here == 0, 1, 0)
    behind = jnp.where(here == late_shard, 1, 0)
    kept = jnp.where(at < vis_ref[0], ahead, behind) == 1
    for part in range(2):
        rows = kv_ref[0, part, :PROMPT].astype(jnp.float32)
        text_ref[part] = jnp.where(kept, rows, 0.0).astype(jnp.bfloat16)
        tail_ref[part] = kv_ref[0, part, tok_rows - halo :]


def segments(positions, length_ref):
    end = jnp.int32(PREFIX)
    segment = jnp.where(positions < PREFIX, 0, 1)
    for at in range(NCOMP):
        end = end + length_ref[0, at]
        segment = segment + jnp.where(positions >= end, 1, 0)
    return segment


def hide(visible):
    return jnp.where(visible, 0.0, HIDDEN)


def first_kernel(targets, halo, tail, seq_ref, vis_ref, length_ref, *refs):
    image_in_ref, kv_ref, d_ref, *out_refs = refs
    first_refs, window_refs, mask_refs = out_refs[:5], out_refs[5:-3], out_refs[-3:]
    near_ref, whole_ref, image_ref = mask_refs
    here = lax.axis_index("ctx")
    ctx_size = lax.axis_size("ctx")
    tok_rows = d_ref.shape[0]
    image_rows = image_in_ref.shape[1]
    row = lax.broadcasted_iota(jnp.int32, (IMAGE_BLOCK, tok_rows), 0)
    column = lax.broadcasted_iota(jnp.int32, (IMAGE_BLOCK, tok_rows), 1)
    place = jnp.where(row < image_rows, row, 1 << 20)
    picks = []
    for blocks in targets:
        for default, special in blocks:
            target = here if default is None else default
            for source, other in special:
                target = jnp.where(here == source, other, target)
            begin = vis_ref[0] + image_rows * target - tok_rows * here
            picks.append(jnp.where(column == place + begin, 1.0, 0.0).astype(jnp.bfloat16))
    picked = dot_nn(jnp.concatenate(picks, axis=0), d_ref[...]).astype(jnp.bfloat16)
    at = 0
    for window_ref in window_refs:
        window_ref[...] = picked[at : at + window_ref.shape[0]]
        at += window_ref.shape[0]

    @pl.when(pl.program_id(0) == 0)
    def _():
        send_first(tail, seq_ref, vis_ref, image_in_ref, kv_ref, *first_refs)
        vis = vis_ref[0]
        own_at = lax.broadcasted_iota(jnp.int32, (8, tok_rows), 1) + here * tok_rows
        own_segment = segments(own_at, length_ref)[:1]
        placeholder = (own_at >= vis) & (own_at < vis + VIS)
        own_row = jnp.where(placeholder, -1, own_at)
        whole_ref[...] = hide(own_row >= vis + VIS).astype(jnp.float32)
        own_row = own_row[:1]
        image_at = lax.broadcasted_iota(jnp.int32, (1, RATIO * IMAGE_BLOCK), 1) % IMAGE_BLOCK
        image_row = jnp.where(image_at < image_rows, vis + here * image_rows + image_at, -1)
        text_at = lax.broadcasted_iota(jnp.int32, (PROMPT, tok_rows), 0)
        text_at = text_at + jnp.where(text_at < vis, 0, VIS)
        near_ref[:PROMPT] = hide(text_at <= own_row)
        near_at = lax.broadcasted_iota(jnp.int32, (halo + tok_rows, tok_rows), 0)
        near_at = near_at + (here * tok_rows - halo)
        sees = (near_at <= own_row) & (near_at >= PREFIX)
        sees = sees & (segments(near_at, length_ref) == own_segment)
        near_ref[PROMPT:] = hide(sees)
        at = 0
        for core in range(2):
            for step in range(0, ctx_size, 2):
                begin = (here ^ (step + core)) * image_rows + vis
                shape = (image_rows, RATIO * IMAGE_BLOCK)
                block_at = lax.broadcasted_iota(jnp.int32, shape, 0) + begin
                image_ref[at : at + image_rows] = hide(block_at <= image_row)
                at += image_rows
        image_ref[VIS:] = hide(text_at <= image_row)


def first_arrays(seq_image, vis_start, lengths, image_rows, keys_values, cotangent, halo, targets):
    rows = image_rows.shape[1]
    tok_rows, width = cotangent.shape
    tail = min(halo, tok_rows)
    block = 2048
    spec = pl.BlockSpec
    smem = spec(memory_space=pltpu.SMEM)
    lanes = RATIO * IMAGE_BLOCK
    near = PROMPT + halo + tok_rows
    whole = lambda *shape: spec(shape, lambda at: (0,) * len(shape))
    kept = [
        ((2, rows, KV_WIDTH), jnp.bfloat16),
        ((rows, Q_WIDTH), jnp.bfloat16),
        ((2, PROMPT, KV_WIDTH), jnp.bfloat16),
        ((2, tail, KV_WIDTH), jnp.bfloat16),
    ]
    masks = [
        ((near, tok_rows), jnp.float32),
        ((8, tok_rows), jnp.float32),
        ((PREFIX, lanes), jnp.float32),
    ]
    counts = [len(blocks) * IMAGE_BLOCK for blocks in targets]
    number, *out = pl.pallas_call(
        functools.partial(first_kernel, targets, halo, tail),
        grid=(width // block,),
        in_specs=[
            smem,
            smem,
            smem,
            whole(*image_rows.shape),
            whole(*keys_values.shape),
            spec((tok_rows, block), lambda at: (0, at)),
        ],
        out_specs=[smem]
        + [whole(*shape) for shape, _ in kept]
        + [spec((count, block), lambda at: (0, at)) for count in counts]
        + [whole(*shape) for shape, _ in masks],
        out_shape=[jax.ShapeDtypeStruct((3,), jnp.int32)]
        + [jax.ShapeDtypeStruct(*pair) for pair in kept]
        + [jax.ShapeDtypeStruct((count, width), jnp.bfloat16) for count in counts]
        + [jax.ShapeDtypeStruct(*pair) for pair in masks],
        compiler_params=pltpu.CompilerParams(vmem_limit_bytes=40 * 1024 * 1024),
    )(seq_image, vis_start, lengths, image_rows, keys_values, cotangent)
    return number, out[:4], out[4 : 4 + len(targets)], out[4 + len(targets) :]


def rows_backward(parts, q_rows, d_rows):
    scale = SCORE_SCALE * math.log2(math.e)
    scores = []
    for keys, values, bias in parts:
        raw = dot_nt(keys, q_rows) * scale
        scores.append(raw if bias.shape[0] == 1 else raw + bias)
    tops = [jnp.max(part, axis=0, keepdims=True) for part in scores]
    tops = [
        top + bias if bias.shape[0] == 1 else top for top, (_, _, bias) in zip(tops, parts)
    ]
    top = functools.reduce(jnp.maximum, tops)
    total = 0.0
    mix = 0.0
    kept = []
    for part, (keys, values, bias) in zip(scores, parts):
        shift = bias - top if bias.shape[0] == 1 else -top
        terms = jnp.exp2(part + shift)
        d_weights = dot_nt(values, d_rows)
        total = total + jnp.sum(terms, axis=0, keepdims=True)
        mix = mix + jnp.sum(terms * d_weights, axis=0, keepdims=True)
        kept.append((terms, d_weights))
    inverse = jnp.where(top > 0.5 * HIDDEN, 1.0 / total, 0.0)
    delta = mix * inverse
    outcome = []
    for terms, d_weights in kept:
        weights = terms * inverse
        d_scores = weights * (d_weights - delta)
        outcome.append((weights.astype(jnp.bfloat16), d_scores.astype(jnp.bfloat16)))
    return outcome


def total_of(values):
    if len(values) == 1:
        return values[0]
    return sum(value.astype(jnp.float32) for value in values).astype(jnp.bfloat16)


def attend_kernel(
    block_rows,
    block_count,
    text_count,
    window_count,
    heads,
    halo,
    own,
    number_ref,
    near_ref,
    whole_ref,
    image_bias_ref,
    q_ref,
    d_ref,
    iq_ref,
    halo_ref,
    own_ref,
    *refs,
):
    block_refs, refs = refs[:block_count], refs[block_count:]
    text_refs, refs = refs[:text_count], refs[text_count:]
    window_refs, refs = refs[:window_count], refs[window_count:]
    dq_ref, *diq_refs, dmine_ref, dpair_ref, dhalo_ref, down_ref = refs
    text_refs = text_refs or [ref for ref in block_refs if ref.shape[1] > block_rows]
    near_bias = jnp.concatenate([near_ref[...]] * 2, axis=1)
    whole_bias = jnp.concatenate([whole_ref[:1]] * 2, axis=1)
    image_cotangent = total_of([ref[...] for ref in window_refs])
    for head in range(heads):
        lanes = slice(head * HEAD_DIM, (head + 1) * HEAD_DIM)
        spans = [
            slice((head * RATIO + at) * HEAD_DIM, (head * RATIO + at + 1) * HEAD_DIM)
            for at in range(RATIO)
        ]
        visual, text, near = [], [], []
        for part in range(2):
            visual.append(
                jnp.concatenate([ref[part, :block_rows, lanes] for ref in block_refs], axis=0)
            )
            text.append(total_of([ref[part, -PROMPT:, lanes] for ref in text_refs]))
            near.append(
                jnp.concatenate(
                    [text[part], halo_ref[part, :, lanes], own_ref[0, part, :, lanes]], axis=0
                )
            )
        keys = jnp.concatenate([visual[0], near[0]], axis=0)
        dk_sums = [0.0, 0.0]
        dv_sums = [0.0, 0.0]
        for first in range(0, RATIO, 2):
            pair = spans[first : first + 2]
            q_rows = jnp.concatenate([q_ref[:, span] for span in pair], axis=0)
            d_rows = jnp.concatenate([d_ref[:, span] for span in pair], axis=0)
            outcome = rows_backward(
                [(visual[0], visual[1], whole_bias), (near[0], near[1], near_bias)],
                q_rows,
                d_rows,
            )
            d_scores = jnp.concatenate([part[1] for part in outcome], axis=0)
            dq = dot_tn(keys, d_scores) * SCORE_SCALE
            for at, span in enumerate(pair):
                dq_ref[:, span] = dq[:, at * own : (at + 1) * own].T.astype(jnp.bfloat16)
            for at, (weights, d_part) in enumerate(outcome):
                dk_sums[at] = dk_sums[at] + dot_nn(d_part, q_rows)
                dv_sums[at] = dv_sums[at] + dot_nn(weights, d_rows)
        image_queries = iq_ref[number_ref[1]]
        q_rows = jnp.concatenate([image_queries[:, span] for span in spans], axis=0)
        d_rows = jnp.concatenate([image_cotangent[:, span] for span in spans], axis=0)
        outcome = rows_backward(
            [
                (visual[0], visual[1], image_bias_ref[:VIS]),
                (text[0], text[1], image_bias_ref[VIS:]),
            ],
            q_rows,
            d_rows,
        )
        d_scores = jnp.concatenate([part[1] for part in outcome], axis=0)
        dq = (dot_tn(keys[:PREFIX], d_scores) * SCORE_SCALE).T.astype(jnp.bfloat16)
        for at, span in enumerate(spans):
            for half, diq_ref in enumerate(diq_refs):
                begin = at * IMAGE_BLOCK + half * IMAGE_HALF
                diq_ref[:, span] = dq[begin : begin + IMAGE_HALF]
        (visual_w, visual_d), (text_w, text_d) = outcome
        for part, sums, pieces, rows, scale in (
            (0, dk_sums, (visual_d, text_d), q_rows, SCORE_SCALE),
            (1, dv_sums, (visual_w, text_w), d_rows, 1.0),
        ):
            of_visual = (sums[0] + dot_nn(pieces[0], rows)) * scale
            of_text = (sums[1][:PROMPT] + dot_nn(pieces[1], rows)) * scale
            rest = sums[1][PROMPT:] * scale
            of_visual = of_visual.astype(jnp.bfloat16)
            dmine_ref[part, :, lanes] = of_visual[: VIS // 2]
            dpair_ref[part, : VIS // 2, lanes] = of_visual[VIS // 2 :]
            dpair_ref[part, VIS // 2 :, lanes] = of_text.astype(jnp.bfloat16)
            dhalo_ref[part, :, lanes] = rest[:halo].astype(jnp.bfloat16)
            down_ref[part, :, lanes] = rest[halo:]


def attend(
    number, masks, queries, cotangent, every_q, halo_kv, own_kv, blocks, texts, windows
):
    heads = 2
    near_bias, whole_bias, image_bias = masks
    own = queries.shape[0]
    halo = halo_kv.shape[1]
    groups = every_q.shape[0]
    columns = PREFIX + halo + own
    products = RATIO * (own * columns + IMAGE_BLOCK * PREFIX) * KV_HEADS
    spec = pl.BlockSpec
    kv_spec = lambda rows: spec((2, rows, heads * HEAD_DIM), lambda at: (0, 0, at))
    q_spec = lambda rows: spec((rows, heads * GROUP_WIDTH), lambda at: (0, at))
    whole = lambda rows: spec((rows, 128), lambda at: (0, 0))
    return pl.pallas_call(
        functools.partial(
            attend_kernel,
            VIS // len(blocks),
            len(blocks),
            len(texts),
            len(windows),
            heads,
            halo,
            own,
        ),
        grid=(KV_HEADS // heads,),
        in_specs=[
            spec(memory_space=pltpu.SMEM),
            whole(columns - VIS),
            whole(8),
            whole(PREFIX),
            q_spec(own),
            q_spec(own),
            spec((groups, IMAGE_BLOCK, heads * GROUP_WIDTH), lambda at: (0, 0, at)),
            kv_spec(halo),
            spec((1, 2, own, heads * HEAD_DIM), lambda at: (0, 0, 0, at)),
        ]
        + [kv_spec(block.shape[1]) for block in [*blocks, *texts]]
        + [q_spec(IMAGE_BLOCK) for _ in windows],
        out_specs=[
            q_spec(own),
            q_spec(IMAGE_HALF),
            q_spec(IMAGE_HALF),
            kv_spec(VIS // 2),
            kv_spec(VIS // 2 + PROMPT),
            kv_spec(halo),
            kv_spec(own),
        ],
        out_shape=[
            jax.ShapeDtypeStruct((own, Q_WIDTH), jnp.bfloat16),
            jax.ShapeDtypeStruct((IMAGE_HALF, Q_WIDTH), jnp.bfloat16),
            jax.ShapeDtypeStruct((IMAGE_HALF, Q_WIDTH), jnp.bfloat16),
            jax.ShapeDtypeStruct((2, VIS // 2, KV_WIDTH), jnp.bfloat16),
            jax.ShapeDtypeStruct((2, VIS // 2 + PROMPT, KV_WIDTH), jnp.bfloat16),
            jax.ShapeDtypeStruct((2, halo, KV_WIDTH), jnp.bfloat16),
            jax.ShapeDtypeStruct((2, own, KV_WIDTH), jnp.float32),
        ],
        cost_estimate=pl.CostEstimate(
            flops=10 * products * HEAD_DIM,
            bytes_accessed=12 * 1024 * 1024,
            transcendentals=products,
        ),
    )(
        number,
        near_bias,
        whole_bias,
        image_bias,
        queries,
        cotangent,
        every_q,
        halo_kv,
        own_kv,
        *blocks,
        *texts,
        *windows,
    )


def route(rows, number, back, beside=()):
    groups = lax.axis_size("rollout")
    arrays = [array for array, _ in beside]

    def move_beside(arrays):
        return [lax.ppermute(array, "ctx", pairs) for array, (_, pairs) in zip(arrays, beside)]

    if groups != 4:
        every = lax.all_gather(rows, "rollout", axis=0)
        picked = lax.dynamic_index_in_dim(every, number[2 if back else 1], 0, keepdims=False)
        return [picked] + move_beside(arrays)

    def branch(images):
        pairs = [(g, i) if back else (i, g) for g, i in enumerate(images)]
        if all(source == target for source, target in pairs):
            return lambda rows, arrays: [rows] + move_beside(arrays)
        return lambda rows, arrays: [lax.ppermute(rows, "rollout", pairs)] + move_beside(arrays)

    orders = itertools.permutations(range(groups))
    return lax.switch(number[0], [branch(images) for images in orders], rows, arrays)


def window_rounds(ctx_size, tok_rows, image_rows):
    rounds = []
    for target in range(ctx_size):
        lowest = (image_rows * target + 1) // tok_rows
        highest = (image_rows * target + image_rows - 1 + PROMPT - 1) // tok_rows
        for source in range(lowest, highest + 1):
            if source == target:
                continue
            for pairs in rounds:
                if all(s != source and t != target for s, t in pairs):
                    pairs.append((source, target))
                    break
            else:
                rounds.append([(source, target)])
    return rounds


def window_targets(ctx_size, tok_rows, image_rows):
    rounds = window_rounds(ctx_size, tok_rows, image_rows)
    if ctx_size != 8:
        return [[(None, [])]] + [[(None, pairs)] for pairs in rounds], rounds
    rounds = [[(0, 2), (1, 4), (2, 6)], [(0, 3), (1, 5), (2, 7)], [(1, 6)], [(1, 7)]]
    swapped = [(2, [(0, 1)]), (3, [])]
    return [[(None, [])]] + [[(None, pairs)] for pairs in rounds] + [swapped], rounds


def join_first(image_kv, text, received, own, one, two, swapped):
    here = lax.axis_index("ctx")
    wide = lambda rows: rows.astype(jnp.float32)
    near, far = swapped[:IMAGE_BLOCK], swapped[IMAGE_BLOCK:]
    sums = [
        jnp.where(here == 1, wide(own) + wide(near), wide(own)),
        jnp.where(here == 0, wide(one) + wide(near), wide(one)),
        jnp.where(here == 0, wide(two) + wide(far), wide(two)),
    ]
    kv = jnp.concatenate([image_kv, add_text(text, received)], axis=1)
    return [kv] + [part.astype(jnp.bfloat16) for part in sums]


def xor_pairs(step):
    return [(at, at ^ step) for at in range(lax.axis_size("ctx"))]


def xor_permute(rows, step):
    return lax.ppermute(rows, "ctx", xor_pairs(step))


def on_device(function, *arrays):
    if lax.axis_size("ctx") != 8:
        return function(*arrays)
    shapes = jax.eval_shape(function, *arrays)

    def kernel(*refs):
        for out_ref, value in zip(
            refs[len(arrays) :], function(*[ref[...] for ref in refs[: len(arrays)]])
        ):
            out_ref[...] = value

    def spec(array):
        *rows, width = array.shape
        return pl.BlockSpec((*rows, width // 2), lambda at: (0,) * len(rows) + (at,))

    return pl.pallas_call(
        kernel,
        grid=(2,),
        in_specs=[spec(array) for array in arrays],
        out_specs=[spec(shape) for shape in shapes],
        out_shape=[jax.ShapeDtypeStruct(shape.shape, shape.dtype) for shape in shapes],
        cost_estimate=pl.CostEstimate(flops=1, bytes_accessed=1, transcendentals=0),
    )(*arrays)


def text_strides(ctx_size, late_shard):
    strides = [1 << at for at in range(1, ctx_size.bit_length() - 1)]
    return [stride for stride in reversed(strides) if stride != late_shard]


def chip_steps(ctx_size):
    return list(range(2, ctx_size, 2))


def add_text(text, received):
    return (text.astype(jnp.float32) + received.astype(jnp.float32)).astype(jnp.bfloat16)


def gather_prefix(image_kv, text):
    ctx_size = lax.axis_size("ctx")
    steps = chip_steps(ctx_size)
    if ctx_size == 8:
        mine = [text, xor_permute(image_kv, 2), xor_permute(text, 4), xor_permute(image_kv, 6)]
        pair = [xor_permute(mine[0], 1)]
        for at, earlier in ((1, None), (3, 0), (2, 1)):
            block = mine[at]
            if earlier is not None:
                block, pair[earlier] = lax.optimization_barrier((block, pair[earlier]))
            pair.append(xor_permute(block, 1))
        return mine + [pair[0], pair[1], pair[3], pair[2]], []
    mine = jnp.concatenate(
        [image_kv] + [xor_permute(image_kv, step) for step in steps], axis=1
    )
    return [mine, xor_permute(mine, 1)], None


def split_sums(image_rows, steps, d_mine, d_pair, other):
    half = VIS // 2
    add = lambda one, two: one.astype(jnp.float32) + two.astype(jnp.float32)
    text = add(d_pair[:, half:], other[:, half:])
    out = []
    for at in range(len(steps) + 1):
        rows = slice(at * image_rows, (at + 1) * image_rows)
        sums = add(d_mine[:, rows], other[:, rows])
        if len(steps) == 3 and steps[at - 1] == 4 and at:
            sums = jnp.concatenate([sums, text], axis=1)
        out.append(sums.astype(jnp.bfloat16) if at else sums)
    return out + [text]


def add_sums(image_rows, own, text, *parts):
    for part in parts:
        own = own + part[:, :image_rows].astype(jnp.float32)
        if part.shape[1] > image_rows:
            text = text + part[:, image_rows:].astype(jnp.float32)
    return [own.astype(jnp.bfloat16), text.astype(jnp.bfloat16)]


def spread_text(text, late_shard):
    for stride in text_strides(lax.axis_size("ctx"), late_shard):
        text = text + xor_permute(text, stride)
    return text, xor_permute(text, 1)


def collect_text(text, late_shard):
    for stride in reversed(text_strides(lax.axis_size("ctx"), late_shard)):
        moved = xor_permute(text.astype(jnp.bfloat16), stride)
        text = text.astype(jnp.float32) + moved.astype(jnp.float32)
    return text.astype(jnp.bfloat16)


def halo_cuts(tok_rows, halo):
    cuts = []
    left = halo
    while left > 0:
        cuts.append(min(left, tok_rows))
        left -= cuts[-1]
    return cuts


def halo_rows(tail, halo, tok_rows):
    ctx_size = lax.axis_size("ctx")
    parts = []
    for step, count in enumerate(halo_cuts(tok_rows, halo), 1):
        pairs = [(at, at + step) for at in range(ctx_size - step)]
        rows = tail if count == tail.shape[1] else tail[:, tail.shape[1] - count :]
        parts.insert(0, lax.ppermute(rows, "ctx", pairs))
    return jnp.concatenate(parts, axis=1) if len(parts) > 1 else parts[0]


def halo_parts(d_halo, tok_rows):
    ctx_size = lax.axis_size("ctx")
    cuts = halo_cuts(tok_rows, d_halo.shape[1])
    parts = []
    end = d_halo.shape[1]
    for step, count in enumerate(cuts, 1):
        rows = d_halo if len(cuts) == 1 else d_halo[:, end - count : end]
        parts.append((rows, [(at + step, at) for at in range(ctx_size - step)]))
        end -= count
    return parts


def last_kernel(part_count, vis_ref, dkv_ref, down_ref, text_ref, other_ref, *refs):
    part_refs = refs[:part_count]
    *dq_refs, image_ref, kv_ref = refs[part_count:]
    here = lax.axis_index("ctx")
    tok_rows = down_ref.shape[1]
    at = 0
    for dq_ref in dq_refs:
        image_ref[0, at : at + dq_ref.shape[0], :Q_WIDTH] = dq_ref[...]
        at += dq_ref.shape[0]
    image_ref[0, :, Q_WIDTH : Q_WIDTH + KV_WIDTH] = dkv_ref[0]
    image_ref[0, :, Q_WIDTH + KV_WIDTH :] = dkv_ref[1]
    at = lax.broadcasted_iota(jnp.int32, (PROMPT, KV_WIDTH), 0)
    ahead = jnp.where(here == 0, 1, 0)
    behind = jnp.where(here == VIS // tok_rows, 1, 0)
    kept = jnp.where(at < vis_ref[0], ahead, behind) == 1
    for part in range(2):
        text = text_ref[part].astype(jnp.float32) + other_ref[part].astype(jnp.float32)
        text = jnp.where(kept, text, 0.0)
        sums = down_ref[part] + jnp.concatenate(
            [text, jnp.zeros((tok_rows - PROMPT, KV_WIDTH), jnp.float32)], axis=0
        )
        for part_ref in part_refs:
            back = part_ref[part].astype(jnp.float32)
            if back.shape[0] < tok_rows:
                missing = jnp.zeros((tok_rows - back.shape[0], KV_WIDTH), jnp.float32)
                back = jnp.concatenate([missing, back], axis=0)
            sums = sums + back
        kv_ref[0, part] = sums.astype(jnp.bfloat16)


def last_arrays(vis_start, image_dq, image_dkv, d_own_kv, text, other_text, parts):
    rows = image_dkv.shape[1]
    smem = pl.BlockSpec(memory_space=pltpu.SMEM)
    vmem = pl.BlockSpec(memory_space=pltpu.VMEM)
    return pl.pallas_call(
        functools.partial(last_kernel, len(parts)),
        in_specs=[smem] + [vmem] * (4 + len(parts) + len(image_dq)),
        out_specs=[vmem, vmem],
        out_shape=[
            jax.ShapeDtypeStruct((1, rows, Q_WIDTH + 2 * KV_WIDTH), jnp.bfloat16),
            jax.ShapeDtypeStruct((1,) + d_own_kv.shape, jnp.bfloat16),
        ],
    )(vis_start, image_dkv, d_own_kv, text, other_text, *parts, *image_dq)


def gather_queries(image_q):
    every = lax.all_gather(image_q, "rollout", axis=0)
    missing = IMAGE_BLOCK - every.shape[1]
    return jnp.pad(every, ((0, 0), (0, missing), (0, 0))) if missing else every


def per_device(queries, keys_values, image_rows, cotangent, seq_image, vis_start, comp_lengths):
    tok_rows = queries.shape[1]
    image_count = image_rows.shape[1]
    ctx_size = lax.axis_size("ctx")
    seq_len = tok_rows * ctx_size
    late_shard = VIS // tok_rows
    longest = 4 * (seq_len - PREFIX) // (3 * NCOMP)
    halo = -(-(longest - 1) // 64) * 64
    q_own, d_own = queries[0], cotangent[0]

    targets, rounds = window_targets(ctx_size, tok_rows, image_count)
    number, (image_kv, image_q, text, tail), windows, masks = first_arrays(
        seq_image, vis_start, comp_lengths, image_rows, keys_values, d_own, halo, targets
    )
    every_q = gather_queries(image_q)
    beside = [(text, xor_pairs(late_shard))]
    if ctx_size == 8:
        own, one, two, three, four, swapped = windows
        beside += [(swapped, xor_pairs(1)), (three, rounds[2]), (four, rounds[3])]
    image_kv, received, *moved = route(image_kv, number, False, beside)
    if ctx_size == 8:
        text, own, one, two = on_device(
            join_first, image_kv, text, received, own, one, two, moved[0]
        )
        windows = [own] + [
            lax.ppermute(rows, "ctx", pairs) for rows, pairs in zip((one, two), rounds)
        ]
        windows += moved[1:]
        blocks, texts = gather_prefix(image_kv, text)
    else:
        windows = [windows[0]] + [
            lax.ppermute(rows, "ctx", pairs) for rows, pairs in zip(windows[1:], rounds)
        ]
        windows = [sum(part.astype(jnp.float32) for part in windows).astype(jnp.bfloat16)]
        blocks, _ = gather_prefix(image_kv, text)
        texts = list(spread_text(add_text(text, received), late_shard))
    halo_kv = halo_rows(tail, halo, tok_rows)

    grad_q, *d_image_q, d_mine, d_pair, d_halo, d_own_kv = attend(
        number,
        masks,
        q_own,
        d_own,
        every_q,
        halo_kv,
        keys_values,
        blocks,
        texts,
        windows,
    )

    d_image_q = [
        half[: image_count - at * IMAGE_HALF]
        for at, half in enumerate(d_image_q)
        if at * IMAGE_HALF < image_count
    ]
    image_dq, other = route(d_image_q[0], number, True, [(d_pair, xor_pairs(1))])
    image_dq = [image_dq]
    steps = chip_steps(ctx_size)
    own, *sent, d_text = on_device(
        functools.partial(split_sums, image_count, steps), d_mine, d_pair, other
    )
    beside = [(rows, xor_pairs(step)) for rows, step in zip(sent, steps)]
    if len(d_image_q) > 1:
        second, *moved = route(d_image_q[1], number, True, beside)
        image_dq.append(second)
    else:
        moved = [lax.ppermute(rows, "ctx", pairs) for rows, pairs in beside]
    sums, d_text = on_device(functools.partial(add_sums, image_count), own, d_text, *moved)
    if ctx_size != 8:
        d_text = collect_text(d_text, late_shard)
    image_dkv, other_text, *halo_back = route(
        sums, number, True, [(d_text, xor_pairs(late_shard))] + halo_parts(d_halo, tok_rows)
    )
    grad_image, grad_kv = last_arrays(
        vis_start, image_dq, image_dkv, d_own_kv, d_text, other_text, halo_back
    )
    return (grad_q[None], grad_kv, grad_image)


def solution(mesh):
    placed = (
        P("rollout", "ctx", None),
        P("rollout", None, "ctx", None),
        P("rollout", "ctx", None),
        P("rollout", "ctx", None),
        P(),
        P("rollout"),
        P("rollout", None),
    )
    return jax.shard_map(
        per_device,
        mesh=mesh,
        in_specs=placed,
        out_specs=(
            P("rollout", "ctx", None),
            P("rollout", None, "ctx", None),
            P("rollout", "ctx", None),
        ),
        check_vma=False,
    )
```

```python
import functools
import itertools
import math

import jax
import jax.numpy as jnp
from jax import lax
from jax.experimental import pallas as pl
from jax.experimental.pallas import tpu as pltpu
from jax.sharding import PartitionSpec as P

HEADS = 32
KV_HEADS = 8
HEAD_DIM = 128
VIS = 256
PROMPT = 64
NCOMP = 16

RATIO = HEADS // KV_HEADS
PREFIX = VIS + PROMPT
Q_WIDTH = HEADS * HEAD_DIM
KV_WIDTH = KV_HEADS * HEAD_DIM
GROUP_WIDTH = RATIO * HEAD_DIM
IMAGE_BLOCK = 32
IMAGE_HALF = IMAGE_BLOCK // 2
HIDDEN = -1e30
SCORE_SCALE = 1.0 / math.sqrt(HEAD_DIM)


def dot_nt(left, right):
    return lax.dot_general(
        left, right, (((1,), (1,)), ((), ())), preferred_element_type=jnp.float32
    )


def dot_nn(left, right):
    return lax.dot_general(
        left, right, (((1,), (0,)), ((), ())), preferred_element_type=jnp.float32
    )


def dot_tn(left, right):
    return lax.dot_general(
        left, right, (((0,), (0,)), ((), ())), preferred_element_type=jnp.float32
    )


def first_kernel(halo, seq_ref, vis_ref, image_ref, kv_ref, number_ref, *out_refs):
    ikv_ref, iq_ref, text_ref, tail_ref = out_refs
    groups = seq_ref.shape[0]
    group = lax.axis_index("rollout")
    here = lax.axis_index("ctx")
    images = [seq_ref[at] for at in range(groups)]
    number = jnp.int32(0)
    if groups == 4:
        for at, weight in enumerate((6, 2, 1)):
            for later in range(at + 1, groups):
                number = number + jnp.where(images[later] < images[at], weight, 0)
    place = jnp.int32(0)
    user = jnp.int32(0)
    for at in range(groups):
        place = place + jnp.where(group == at, images[at], 0)
        user = user + jnp.where(images[at] == group, at, 0)
    number_ref[0] = number
    number_ref[1] = place
    number_ref[2] = user
    iq_ref[...] = image_ref[0, :, :Q_WIDTH]
    ikv_ref[0] = image_ref[0, :, Q_WIDTH : Q_WIDTH + KV_WIDTH]
    ikv_ref[1] = image_ref[0, :, Q_WIDTH + KV_WIDTH :]
    tok_rows = kv_ref.shape[2]
    late_shard = VIS // tok_rows
    at = lax.broadcasted_iota(jnp.int32, (PROMPT, KV_WIDTH), 0)
    ahead = jnp.where(here == 0, 1, 0)
    behind = jnp.where(here == late_shard, 1, 0)
    kept = jnp.where(at < vis_ref[0], ahead, behind) == 1
    for part in range(2):
        rows = kv_ref[0, part, :PROMPT].astype(jnp.float32)
        text_ref[part] = jnp.where(kept, rows, 0.0).astype(jnp.bfloat16)
        tail_ref[part] = kv_ref[0, part, tok_rows - halo :]


def first_arrays(seq_image, vis_start, image_rows, keys_values, halo):
    rows = image_rows.shape[1]
    smem = pl.BlockSpec(memory_space=pltpu.SMEM)
    vmem = pl.BlockSpec(memory_space=pltpu.VMEM)
    tail = min(halo, keys_values.shape[2])
    return pl.pallas_call(
        functools.partial(first_kernel, tail),
        in_specs=[smem, smem, vmem, vmem],
        out_specs=[smem, vmem, vmem, vmem, vmem],
        out_shape=[
            jax.ShapeDtypeStruct((3,), jnp.int32),
            jax.ShapeDtypeStruct((2, rows, KV_WIDTH), jnp.bfloat16),
            jax.ShapeDtypeStruct((rows, Q_WIDTH), jnp.bfloat16),
            jax.ShapeDtypeStruct((2, PROMPT, KV_WIDTH), jnp.bfloat16),
            jax.ShapeDtypeStruct((2, tail, KV_WIDTH), jnp.bfloat16),
        ],
    )(seq_image, vis_start, image_rows, keys_values)


def segments(positions, length_ref):
    end = jnp.int32(PREFIX)
    segment = jnp.where(positions < PREFIX, 0, 1)
    for at in range(NCOMP):
        end = end + length_ref[0, at]
        segment = segment + jnp.where(positions >= end, 1, 0)
    return segment


def hide(visible):
    return jnp.where(visible, 0.0, HIDDEN)


def second_kernel(
    rounds, tok_rows, image_rows, halo, vis_ref, length_ref, d_ref, kv_ref, t_ref, r_ref, *out_refs
):
    *window_refs, near_ref, whole_ref, image_ref, text_ref = out_refs
    here = lax.axis_index("ctx")
    ctx_size = lax.axis_size("ctx")
    row = lax.broadcasted_iota(jnp.int32, (IMAGE_BLOCK, tok_rows), 0)
    column = lax.broadcasted_iota(jnp.int32, (IMAGE_BLOCK, tok_rows), 1)
    place = jnp.where(row < image_rows, row, 1 << 20)
    picks = []
    for pairs in [[]] + rounds:
        target = here
        for source, other in pairs:
            target = jnp.where(here == source, other, target)
        begin = vis_ref[0] + image_rows * target - tok_rows * here
        picks.append(jnp.where(column == place + begin, 1.0, 0.0).astype(jnp.bfloat16))
    picked = dot_nn(jnp.concatenate(picks, axis=0), d_ref[...]).astype(jnp.bfloat16)
    for at, window_ref in enumerate(window_refs):
        window_ref[...] = picked[at * IMAGE_BLOCK : (at + 1) * IMAGE_BLOCK]

    @pl.when(pl.program_id(0) == 0)
    def _():
        vis = vis_ref[0]
        text = t_ref[...].astype(jnp.float32) + r_ref[...].astype(jnp.float32)
        if kv_ref.shape[1] == IMAGE_BLOCK:
            text_ref[:, :IMAGE_BLOCK] = kv_ref[...]
        text_ref[:, text_ref.shape[1] - PROMPT :] = text.astype(jnp.bfloat16)
        own_at = lax.broadcasted_iota(jnp.int32, (8, tok_rows), 1) + here * tok_rows
        own_segment = segments(own_at, length_ref)[:1]
        placeholder = (own_at >= vis) & (own_at < vis + VIS)
        own_row = jnp.where(placeholder, -1, own_at)
        whole_ref[...] = hide(own_row >= vis + VIS).astype(jnp.float32)
        own_row = own_row[:1]
        image_at = lax.broadcasted_iota(jnp.int32, (1, RATIO * IMAGE_BLOCK), 1) % IMAGE_BLOCK
        image_row = jnp.where(image_at < image_rows, vis + here * image_rows + image_at, -1)
        text_at = lax.broadcasted_iota(jnp.int32, (PROMPT, tok_rows), 0)
        text_at = text_at + jnp.where(text_at < vis, 0, VIS)
        near_ref[:PROMPT] = hide(text_at <= own_row)
        near_at = lax.broadcasted_iota(jnp.int32, (halo + tok_rows, tok_rows), 0)
        near_at = near_at + (here * tok_rows - halo)
        sees = (near_at <= own_row) & (near_at >= PREFIX)
        sees = sees & (segments(near_at, length_ref) == own_segment)
        near_ref[PROMPT:] = hide(sees)
        at = 0
        for core in range(2):
            for step in range(0, ctx_size, 2):
                begin = (here ^ (step + core)) * image_rows + vis
                shape = (image_rows, RATIO * IMAGE_BLOCK)
                block_at = lax.broadcasted_iota(jnp.int32, shape, 0) + begin
                image_ref[at : at + image_rows] = hide(block_at <= image_row)
                at += image_rows
        image_ref[VIS:] = hide(text_at <= image_row)


def second_arrays(vis_start, lengths, cotangent, image_kv, text, received, halo):
    tok_rows, width = cotangent.shape
    image_rows = image_kv.shape[1]
    text_rows = PROMPT + (image_rows if image_rows == IMAGE_BLOCK else 0)
    rounds = window_rounds(lax.axis_size("ctx"), tok_rows, image_rows)
    count = len(rounds) + 1
    block = 2048
    spec = pl.BlockSpec
    smem = spec(memory_space=pltpu.SMEM)
    lanes = RATIO * IMAGE_BLOCK
    near = PROMPT + halo + tok_rows
    whole = lambda *shape: spec(shape, lambda at: (0,) * len(shape))
    out = pl.pallas_call(
        functools.partial(second_kernel, rounds, tok_rows, image_rows, halo),
        grid=(width // block,),
        in_specs=[
            smem,
            smem,
            spec((tok_rows, block), lambda at: (0, at)),
            whole(2, image_rows, KV_WIDTH),
            whole(2, PROMPT, KV_WIDTH),
            whole(2, PROMPT, KV_WIDTH),
        ],
        out_specs=[spec((IMAGE_BLOCK, block), lambda at: (0, at)) for _ in range(count)]
        + [
            whole(near, tok_rows),
            whole(8, tok_rows),
            whole(PREFIX, lanes),
            whole(2, text_rows, KV_WIDTH),
        ],
        out_shape=[jax.ShapeDtypeStruct((IMAGE_BLOCK, width), jnp.bfloat16) for _ in range(count)]
        + [
            jax.ShapeDtypeStruct((near, tok_rows), jnp.float32),
            jax.ShapeDtypeStruct((8, tok_rows), jnp.float32),
            jax.ShapeDtypeStruct((PREFIX, lanes), jnp.float32),
            jax.ShapeDtypeStruct((2, text_rows, KV_WIDTH), jnp.bfloat16),
        ],
    )(vis_start, lengths, cotangent, image_kv, text, received)
    return out[:count], rounds, out[count:]


def rows_backward(parts, q_rows, d_rows):
    scale = SCORE_SCALE * math.log2(math.e)
    scores = []
    for keys, values, bias in parts:
        raw = dot_nt(keys, q_rows) * scale
        scores.append(raw if bias.shape[0] == 1 else raw + bias)
    tops = [jnp.max(part, axis=0, keepdims=True) for part in scores]
    tops = [
        top + bias if bias.shape[0] == 1 else top for top, (_, _, bias) in zip(tops, parts)
    ]
    top = functools.reduce(jnp.maximum, tops)
    total = 0.0
    mix = 0.0
    kept = []
    for part, (keys, values, bias) in zip(scores, parts):
        shift = bias - top if bias.shape[0] == 1 else -top
        terms = jnp.exp2(part + shift)
        d_weights = dot_nt(values, d_rows)
        total = total + jnp.sum(terms, axis=0, keepdims=True)
        mix = mix + jnp.sum(terms * d_weights, axis=0, keepdims=True)
        kept.append((terms, d_weights))
    inverse = jnp.where(top > 0.5 * HIDDEN, 1.0 / total, 0.0)
    delta = mix * inverse
    outcome = []
    for terms, d_weights in kept:
        weights = terms * inverse
        d_scores = weights * (d_weights - delta)
        outcome.append((weights.astype(jnp.bfloat16), d_scores.astype(jnp.bfloat16)))
    return outcome


def total_of(values):
    if len(values) == 1:
        return values[0]
    return sum(value.astype(jnp.float32) for value in values).astype(jnp.bfloat16)


def prefix_parts(block_refs, text_refs, block_rows, lanes):
    text_refs = text_refs or [ref for ref in block_refs if ref.shape[1] > block_rows]
    visual, text = [], []
    for part in range(2):
        visual.append(
            jnp.concatenate([ref[part, :block_rows, lanes] for ref in block_refs], axis=0)
        )
        text.append(total_of([ref[part, -PROMPT:, lanes] for ref in text_refs]))
    return visual, text


def head_lanes(head):
    lanes = slice(head * HEAD_DIM, (head + 1) * HEAD_DIM)
    spans = [
        slice((head * RATIO + at) * HEAD_DIM, (head * RATIO + at + 1) * HEAD_DIM)
        for at in range(RATIO)
    ]
    return lanes, spans


def own_kernel(
    block_rows,
    block_count,
    heads,
    halo,
    own,
    near_ref,
    whole_ref,
    q_ref,
    d_ref,
    halo_ref,
    own_ref,
    *refs,
):
    *prefix_refs, dq_ref, dprefix_ref, dhalo_ref, down_ref = refs
    block_refs, text_refs = prefix_refs[:block_count], prefix_refs[block_count:]
    near_bias = jnp.concatenate([near_ref[...]] * 2, axis=1)
    whole_bias = jnp.concatenate([whole_ref[:1]] * 2, axis=1)
    for head in range(heads):
        lanes, spans = head_lanes(head)
        visual, text = prefix_parts(block_refs, text_refs, block_rows, lanes)
        near = [
            jnp.concatenate(
                [text[part], halo_ref[part, :, lanes], own_ref[0, part, :, lanes]], axis=0
            )
            for part in range(2)
        ]
        keys_across = jnp.concatenate([visual[0], near[0]], axis=0).T
        dk_sums = [0.0, 0.0]
        dv_sums = [0.0, 0.0]
        for first in range(0, RATIO, 2):
            pair = spans[first : first + 2]
            q_rows = jnp.concatenate([q_ref[:, span] for span in pair], axis=0)
            d_rows = jnp.concatenate([d_ref[:, span] for span in pair], axis=0)
            outcome = rows_backward(
                [(visual[0], visual[1], whole_bias), (near[0], near[1], near_bias)],
                q_rows,
                d_rows,
            )
            d_scores = jnp.concatenate([part[1] for part in outcome], axis=0)
            dq = (dot_nn(keys_across, d_scores) * SCORE_SCALE).astype(jnp.bfloat16)
            for at, span in enumerate(pair):
                dq_ref[:, span] = dq[:, at * own : (at + 1) * own].T
            for at, (weights, d_part) in enumerate(outcome):
                dk_sums[at] = dk_sums[at] + dot_nn(d_part, q_rows)
                dv_sums[at] = dv_sums[at] + dot_nn(weights, d_rows)
        for part, sums, scale in ((0, dk_sums, SCORE_SCALE), (1, dv_sums, 1.0)):
            dprefix_ref[part, :VIS, lanes] = sums[0] * scale
            rest = sums[1] * scale
            dprefix_ref[part, VIS:, lanes] = rest[:PROMPT]
            dhalo_ref[part, :, lanes] = rest[PROMPT : PROMPT + halo].astype(jnp.bfloat16)
            down_ref[part, :, lanes] = rest[PROMPT + halo :]


def image_kernel(
    block_rows,
    block_count,
    text_count,
    heads,
    number_ref,
    image_bias_ref,
    iq_ref,
    dprefix_ref,
    *refs,
):
    *in_refs, dq_ref, dq_more_ref, dmine_ref, dpair_ref = refs
    block_refs, in_refs = in_refs[:block_count], in_refs[block_count:]
    text_refs, window_refs = in_refs[:text_count], in_refs[text_count:]
    image_cotangent = total_of([ref[...] for ref in window_refs])
    image_queries = iq_ref[number_ref[1]]
    for head in range(heads):
        lanes, spans = head_lanes(head)
        visual, text = prefix_parts(block_refs, text_refs, block_rows, lanes)
        q_rows = jnp.concatenate([image_queries[:, span] for span in spans], axis=0)
        d_rows = jnp.concatenate([image_cotangent[:, span] for span in spans], axis=0)
        keys, values = [jnp.concatenate(pair, axis=0) for pair in zip(visual, text)]
        ((weights, d_scores),) = rows_backward(
            [(keys, values, image_bias_ref[...])], q_rows, d_rows
        )
        dq = (dot_nn(keys.T, d_scores) * SCORE_SCALE).astype(jnp.bfloat16).T
        for at, span in enumerate(spans):
            for half, out_ref in enumerate((dq_ref, dq_more_ref)):
                begin = at * IMAGE_BLOCK + half * IMAGE_HALF
                out_ref[:, span] = dq[begin : begin + IMAGE_HALF]
        for part, sums in enumerate(
            (dot_nn(d_scores, q_rows) * SCORE_SCALE, dot_nn(weights, d_rows))
        ):
            sums = (dprefix_ref[part, :, lanes] + sums).astype(jnp.bfloat16)
            dmine_ref[part, :, lanes] = sums[: VIS // 2]
            dpair_ref[part, :, lanes] = sums[VIS // 2 :]


def kv_spec(rows, heads):
    return pl.BlockSpec((2, rows, heads * HEAD_DIM), lambda at: (0, 0, at))


def q_spec(rows, heads):
    return pl.BlockSpec((rows, heads * GROUP_WIDTH), lambda at: (0, at))


def attend_own(near_bias, whole_bias, queries, cotangent, halo_kv, own_kv, blocks, texts):
    heads = 2
    own = queries.shape[0]
    halo = halo_kv.shape[1]
    columns = PREFIX + halo + own
    products = RATIO * own * columns * KV_HEADS
    spec = pl.BlockSpec
    whole = lambda rows: spec((rows, 128), lambda at: (0, 0))
    return pl.pallas_call(
        functools.partial(own_kernel, VIS // len(blocks), len(blocks), heads, halo, own),
        grid=(KV_HEADS // heads,),
        in_specs=[
            whole(columns - VIS),
            whole(8),
            q_spec(own, heads),
            q_spec(own, heads),
            kv_spec(halo, heads),
            spec((1, 2, own, heads * HEAD_DIM), lambda at: (0, 0, 0, at)),
        ]
        + [kv_spec(block.shape[1], heads) for block in [*blocks, *texts]],
        out_specs=[
            q_spec(own, heads),
            kv_spec(PREFIX, heads),
            kv_spec(halo, heads),
            kv_spec(own, heads),
        ],
        out_shape=[
            jax.ShapeDtypeStruct((own, Q_WIDTH), jnp.bfloat16),
            jax.ShapeDtypeStruct((2, PREFIX, KV_WIDTH), jnp.float32),
            jax.ShapeDtypeStruct((2, halo, KV_WIDTH), jnp.bfloat16),
            jax.ShapeDtypeStruct((2, own, KV_WIDTH), jnp.float32),
        ],
        cost_estimate=pl.CostEstimate(
            flops=20 * products * HEAD_DIM,
            bytes_accessed=16 * 1024 * 1024,
            transcendentals=products,
        ),
    )(near_bias, whole_bias, queries, cotangent, halo_kv, own_kv, *blocks, *texts)


def attend_image(number, image_bias, every_q, d_prefix, blocks, texts, windows):
    heads = 2
    groups = every_q.shape[0]
    rows = RATIO * IMAGE_BLOCK
    spec = pl.BlockSpec
    return pl.pallas_call(
        functools.partial(
            image_kernel, VIS // len(blocks), len(blocks), len(texts), heads
        ),
        grid=(KV_HEADS // heads,),
        in_specs=[
            spec(memory_space=pltpu.SMEM),
            spec((PREFIX, rows), lambda at: (0, 0)),
            spec((groups, IMAGE_BLOCK, heads * GROUP_WIDTH), lambda at: (0, 0, at)),
            kv_spec(PREFIX, heads),
        ]
        + [kv_spec(block.shape[1], heads) for block in [*blocks, *texts]]
        + [q_spec(IMAGE_BLOCK, heads) for _ in windows],
        out_specs=[
            q_spec(IMAGE_HALF, heads),
            q_spec(IMAGE_HALF, heads),
            kv_spec(VIS // 2, heads),
            kv_spec(VIS // 2 + PROMPT, heads),
        ],
        out_shape=[
            jax.ShapeDtypeStruct((IMAGE_HALF, Q_WIDTH), jnp.bfloat16),
            jax.ShapeDtypeStruct((IMAGE_HALF, Q_WIDTH), jnp.bfloat16),
            jax.ShapeDtypeStruct((2, VIS // 2, KV_WIDTH), jnp.bfloat16),
            jax.ShapeDtypeStruct((2, VIS // 2 + PROMPT, KV_WIDTH), jnp.bfloat16),
        ],
        cost_estimate=pl.CostEstimate(
            flops=10 * rows * PREFIX * KV_HEADS * HEAD_DIM,
            bytes_accessed=8 * 1024 * 1024,
            transcendentals=rows * PREFIX * KV_HEADS,
        ),
    )(number, image_bias, every_q, d_prefix, *blocks, *texts, *windows)


def route(rows, number, back, beside=()):
    groups = lax.axis_size("rollout")
    arrays = [array for array, _ in beside]

    def move_beside(arrays):
        return [lax.ppermute(array, "ctx", pairs) for array, (_, pairs) in zip(arrays, beside)]

    if groups != 4:
        every = lax.all_gather(rows, "rollout", axis=0)
        picked = lax.dynamic_index_in_dim(every, number[2 if back else 1], 0, keepdims=False)
        return [picked] + move_beside(arrays)

    def branch(images):
        pairs = [(g, i) if back else (i, g) for g, i in enumerate(images)]
        if all(source == target for source, target in pairs):
            return lambda rows, arrays: [rows] + move_beside(arrays)
        return lambda rows, arrays: [lax.ppermute(rows, "rollout", pairs)] + move_beside(arrays)

    orders = itertools.permutations(range(groups))
    return lax.switch(number[0], [branch(images) for images in orders], rows, arrays)


def window_rounds(ctx_size, tok_rows, image_rows):
    rounds = []
    for target in range(ctx_size):
        lowest = (image_rows * target + 1) // tok_rows
        highest = (image_rows * target + image_rows - 1 + PROMPT - 1) // tok_rows
        for source in range(lowest, highest + 1):
            if source == target:
                continue
            for pairs in rounds:
                if all(s != source and t != target for s, t in pairs):
                    pairs.append((source, target))
                    break
            else:
                rounds.append([(source, target)])
    return rounds


def image_windows(windows, rounds):
    parts = [windows[0]] + [
        lax.ppermute(rows, "ctx", pairs) for rows, pairs in zip(windows[1:], rounds)
    ]
    if len(parts) > 8:
        parts = [sum(part.astype(jnp.float32) for part in parts).astype(jnp.bfloat16)]
    return parts


def xor_pairs(step):
    return [(at, at ^ step) for at in range(lax.axis_size("ctx"))]


def xor_permute(rows, step):
    return lax.ppermute(rows, "ctx", xor_pairs(step))


def on_device(function, *arrays):
    if lax.axis_size("ctx") != 8:
        return function(*arrays)
    shapes = jax.eval_shape(function, *arrays)

    def kernel(*refs):
        for out_ref, value in zip(
            refs[len(arrays) :], function(*[ref[...] for ref in refs[: len(arrays)]])
        ):
            out_ref[...] = value

    def spec(array):
        *rows, width = array.shape
        return pl.BlockSpec((*rows, width // 2), lambda at: (0,) * len(rows) + (at,))

    return pl.pallas_call(
        kernel,
        grid=(2,),
        in_specs=[spec(array) for array in arrays],
        out_specs=[spec(shape) for shape in shapes],
        out_shape=[jax.ShapeDtypeStruct(shape.shape, shape.dtype) for shape in shapes],
        cost_estimate=pl.CostEstimate(flops=1, bytes_accessed=1, transcendentals=0),
    )(*arrays)


def text_strides(ctx_size, late_shard):
    strides = [1 << at for at in range(1, ctx_size.bit_length() - 1)]
    return [stride for stride in reversed(strides) if stride != late_shard]


def chip_steps(ctx_size):
    return list(range(2, ctx_size, 2))


def gather_prefix(image_kv, text, late_shard):
    ctx_size = lax.axis_size("ctx")
    steps = chip_steps(ctx_size)
    if ctx_size == 8:
        mine = [text, xor_permute(image_kv, 2), xor_permute(text, 4), xor_permute(image_kv, 6)]
        pair = [xor_permute(mine[0], 1)]
        for at, earlier in ((1, None), (3, 0), (2, 1)):
            block = mine[at]
            if earlier is not None:
                block, pair[earlier] = lax.optimization_barrier((block, pair[earlier]))
            pair.append(xor_permute(block, 1))
        blocks = mine + [pair[0], pair[1], pair[3], pair[2]]
        return blocks, [blocks[at] for at in (0, 2, 4, 6)]
    mine = jnp.concatenate(
        [image_kv] + [xor_permute(image_kv, step) for step in steps], axis=1
    )
    return [mine, xor_permute(mine, 1)], list(spread_text(text, late_shard))


def split_sums(image_rows, steps, d_mine, d_pair, other):
    half = VIS // 2
    add = lambda one, two: one.astype(jnp.float32) + two.astype(jnp.float32)
    text = add(d_pair[:, half:], other[:, half:])
    out = []
    for at in range(len(steps) + 1):
        rows = slice(at * image_rows, (at + 1) * image_rows)
        sums = add(d_mine[:, rows], other[:, rows])
        if len(steps) == 3 and steps[at - 1] == 4 and at:
            sums = jnp.concatenate([sums, text], axis=1)
        out.append(sums.astype(jnp.bfloat16) if at else sums)
    return out + [text]


def add_sums(image_rows, own, text, *parts):
    for part in parts:
        own = own + part[:, :image_rows].astype(jnp.float32)
        if part.shape[1] > image_rows:
            text = text + part[:, image_rows:].astype(jnp.float32)
    return [own.astype(jnp.bfloat16), text.astype(jnp.bfloat16)]


def spread_text(text, late_shard):
    for stride in text_strides(lax.axis_size("ctx"), late_shard):
        text = text + xor_permute(text, stride)
    return text, xor_permute(text, 1)


def collect_text(text, late_shard):
    for stride in reversed(text_strides(lax.axis_size("ctx"), late_shard)):
        moved = xor_permute(text.astype(jnp.bfloat16), stride)
        text = text.astype(jnp.float32) + moved.astype(jnp.float32)
    return text.astype(jnp.bfloat16)


def halo_cuts(tok_rows, halo):
    cuts = []
    left = halo
    while left > 0:
        cuts.append(min(left, tok_rows))
        left -= cuts[-1]
    return cuts


def halo_rows(tail, halo, tok_rows):
    ctx_size = lax.axis_size("ctx")
    parts = []
    for step, count in enumerate(halo_cuts(tok_rows, halo), 1):
        pairs = [(at, at + step) for at in range(ctx_size - step)]
        rows = tail if count == tail.shape[1] else tail[:, tail.shape[1] - count :]
        parts.insert(0, lax.ppermute(rows, "ctx", pairs))
    return jnp.concatenate(parts, axis=1) if len(parts) > 1 else parts[0]


def halo_parts(d_halo, tok_rows):
    ctx_size = lax.axis_size("ctx")
    cuts = halo_cuts(tok_rows, d_halo.shape[1])
    parts = []
    end = d_halo.shape[1]
    for step, count in enumerate(cuts, 1):
        rows = d_halo if len(cuts) == 1 else d_halo[:, end - count : end]
        parts.append((rows, [(at + step, at) for at in range(ctx_size - step)]))
        end -= count
    return parts


def last_kernel(part_count, vis_ref, dkv_ref, down_ref, text_ref, other_ref, *refs):
    part_refs = refs[:part_count]
    *dq_refs, image_ref, kv_ref = refs[part_count:]
    here = lax.axis_index("ctx")
    tok_rows = down_ref.shape[1]
    at = 0
    for dq_ref in dq_refs:
        image_ref[0, at : at + dq_ref.shape[0], :Q_WIDTH] = dq_ref[...]
        at += dq_ref.shape[0]
    image_ref[0, :, Q_WIDTH : Q_WIDTH + KV_WIDTH] = dkv_ref[0]
    image_ref[0, :, Q_WIDTH + KV_WIDTH :] = dkv_ref[1]
    at = lax.broadcasted_iota(jnp.int32, (PROMPT, KV_WIDTH), 0)
    ahead = jnp.where(here == 0, 1, 0)
    behind = jnp.where(here == VIS // tok_rows, 1, 0)
    kept = jnp.where(at < vis_ref[0], ahead, behind) == 1
    for part in range(2):
        text = text_ref[part].astype(jnp.float32) + other_ref[part].astype(jnp.float32)
        text = jnp.where(kept, text, 0.0)
        sums = down_ref[part] + jnp.concatenate(
            [text, jnp.zeros((tok_rows - PROMPT, KV_WIDTH), jnp.float32)], axis=0
        )
        for part_ref in part_refs:
            back = part_ref[part].astype(jnp.float32)
            if back.shape[0] < tok_rows:
                missing = jnp.zeros((tok_rows - back.shape[0], KV_WIDTH), jnp.float32)
                back = jnp.concatenate([missing, back], axis=0)
            sums = sums + back
        kv_ref[0, part] = sums.astype(jnp.bfloat16)


def last_arrays(vis_start, image_dq, image_dkv, d_own_kv, text, other_text, parts):
    rows = image_dkv.shape[1]
    smem = pl.BlockSpec(memory_space=pltpu.SMEM)
    vmem = pl.BlockSpec(memory_space=pltpu.VMEM)
    return pl.pallas_call(
        functools.partial(last_kernel, len(parts)),
        in_specs=[smem] + [vmem] * (4 + len(parts) + len(image_dq)),
        out_specs=[vmem, vmem],
        out_shape=[
            jax.ShapeDtypeStruct((1, rows, Q_WIDTH + 2 * KV_WIDTH), jnp.bfloat16),
            jax.ShapeDtypeStruct((1,) + d_own_kv.shape, jnp.bfloat16),
        ],
    )(vis_start, image_dkv, d_own_kv, text, other_text, *parts, *image_dq)


def gather_queries(image_q):
    every = lax.all_gather(image_q, "rollout", axis=0)
    missing = IMAGE_BLOCK - every.shape[1]
    return jnp.pad(every, ((0, 0), (0, missing), (0, 0))) if missing else every


def per_device(queries, keys_values, image_rows, cotangent, seq_image, vis_start, comp_lengths):
    tok_rows = queries.shape[1]
    image_count = image_rows.shape[1]
    ctx_size = lax.axis_size("ctx")
    seq_len = tok_rows * ctx_size
    late_shard = VIS // tok_rows
    longest = 4 * (seq_len - PREFIX) // (3 * NCOMP)
    halo = -(-(longest - 1) // 64) * 64
    q_own, d_own = queries[0], cotangent[0]

    number, image_kv, image_q, text, tail = first_arrays(
        seq_image, vis_start, image_rows, keys_values, halo
    )
    every_q = gather_queries(image_q)
    image_kv, swapped = route(image_kv, number, False, [(text, xor_pairs(late_shard))])
    image_kv, d_later = lax.optimization_barrier((image_kv, d_own))
    windows, rounds, (*masks, text) = second_arrays(
        vis_start, comp_lengths, d_later, image_kv, text, swapped, halo
    )
    blocks, texts = gather_prefix(image_kv, text, late_shard)
    windows = image_windows(windows, rounds)
    halo_kv = halo_rows(tail, halo, tok_rows)

    near_bias, whole_bias, image_bias = masks
    texts = [] if ctx_size == 8 else texts
    grad_q, d_prefix, d_halo, d_own_kv = attend_own(
        near_bias, whole_bias, q_own, d_own, halo_kv, keys_values, blocks, texts
    )
    *d_image_q, d_mine, d_pair = attend_image(
        number, image_bias, every_q, d_prefix, blocks, texts, windows
    )

    d_image_q = [
        half[: image_count - at * IMAGE_HALF]
        for at, half in enumerate(d_image_q)
        if at * IMAGE_HALF < image_count
    ]
    image_dq, other = route(d_image_q[0], number, True, [(d_pair, xor_pairs(1))])
    image_dq = [image_dq]
    steps = chip_steps(ctx_size)
    own, *sent, d_text = on_device(
        functools.partial(split_sums, image_count, steps), d_mine, d_pair, other
    )
    beside = [(rows, xor_pairs(step)) for rows, step in zip(sent, steps)]
    if len(d_image_q) > 1:
        second, *moved = route(d_image_q[1], number, True, beside)
        image_dq.append(second)
    else:
        moved = [lax.ppermute(rows, "ctx", pairs) for rows, pairs in beside]
    sums, d_text = on_device(functools.partial(add_sums, image_count), own, d_text, *moved)
    if ctx_size != 8:
        d_text = collect_text(d_text, late_shard)
    image_dkv, other_text, *halo_back = route(
        sums, number, True, [(d_text, xor_pairs(late_shard))] + halo_parts(d_halo, tok_rows)
    )
    grad_image, grad_kv = last_arrays(
        vis_start, image_dq, image_dkv, d_own_kv, d_text, other_text, halo_back
    )
    return (grad_q[None], grad_kv, grad_image)


def solution(mesh):
    placed = (
        P("rollout", "ctx", None),
        P("rollout", None, "ctx", None),
        P("rollout", "ctx", None),
        P("rollout", "ctx", None),
        P(),
        P("rollout"),
        P("rollout", None),
    )
    return jax.shard_map(
        per_device,
        mesh=mesh,
        in_specs=placed,
        out_specs=(
            P("rollout", "ctx", None),
            P("rollout", None, "ctx", None),
            P("rollout", "ctx", None),
        ),
        check_vma=False,
    )
```

```python
import functools
import itertools
import math

import jax
import jax.numpy as jnp
from jax import lax
from jax.experimental import pallas as pl
from jax.experimental.pallas import tpu as pltpu
from jax.sharding import PartitionSpec as P

HEADS = 32
KV_HEADS = 8
HEAD_DIM = 128
VIS = 256
PROMPT = 64
NCOMP = 16

RATIO = HEADS // KV_HEADS
PREFIX = VIS + PROMPT
Q_WIDTH = HEADS * HEAD_DIM
KV_WIDTH = KV_HEADS * HEAD_DIM
GROUP_WIDTH = RATIO * HEAD_DIM
IMAGE_BLOCK = 32
IMAGE_HALF = IMAGE_BLOCK // 2
KEY_CHUNK = 64
HIDDEN = -1e30
SCORE_SCALE = 1.0 / math.sqrt(HEAD_DIM)


def dot_nt(left, right):
    return lax.dot_general(
        left, right, (((1,), (1,)), ((), ())), preferred_element_type=jnp.float32
    )


def dot_nn(left, right):
    return lax.dot_general(
        left, right, (((1,), (0,)), ((), ())), preferred_element_type=jnp.float32
    )


def dot_tn(left, right):
    return lax.dot_general(
        left, right, (((0,), (0,)), ((), ())), preferred_element_type=jnp.float32
    )


def first_kernel(halo, seq_ref, vis_ref, image_ref, kv_ref, number_ref, *out_refs):
    ikv_ref, iq_ref, text_ref, tail_ref = out_refs
    groups = seq_ref.shape[0]
    group = lax.axis_index("rollout")
    here = lax.axis_index("ctx")
    images = [seq_ref[at] for at in range(groups)]
    number = jnp.int32(0)
    if groups == 4:
        for at, weight in enumerate((6, 2, 1)):
            for later in range(at + 1, groups):
                number = number + jnp.where(images[later] < images[at], weight, 0)
    place = jnp.int32(0)
    user = jnp.int32(0)
    for at in range(groups):
        place = place + jnp.where(group == at, images[at], 0)
        user = user + jnp.where(images[at] == group, at, 0)
    number_ref[0] = number
    number_ref[1] = place
    number_ref[2] = user
    iq_ref[...] = image_ref[0, :, :Q_WIDTH]
    ikv_ref[0] = image_ref[0, :, Q_WIDTH : Q_WIDTH + KV_WIDTH]
    ikv_ref[1] = image_ref[0, :, Q_WIDTH + KV_WIDTH :]
    tok_rows = kv_ref.shape[2]
    late_shard = VIS // tok_rows
    at = lax.broadcasted_iota(jnp.int32, (PROMPT, KV_WIDTH), 0)
    ahead = jnp.where(here == 0, 1, 0)
    behind = jnp.where(here == late_shard, 1, 0)
    kept = jnp.where(at < vis_ref[0], ahead, behind) == 1
    for part in range(2):
        rows = kv_ref[0, part, :PROMPT].astype(jnp.float32)
        text_ref[part] = jnp.where(kept, rows, 0.0).astype(jnp.bfloat16)
        tail_ref[part] = kv_ref[0, part, tok_rows - halo :]


def first_arrays(seq_image, vis_start, image_rows, keys_values, halo):
    rows = image_rows.shape[1]
    smem = pl.BlockSpec(memory_space=pltpu.SMEM)
    vmem = pl.BlockSpec(memory_space=pltpu.VMEM)
    tail = min(halo, keys_values.shape[2])
    return pl.pallas_call(
        functools.partial(first_kernel, tail),
        in_specs=[smem, smem, vmem, vmem],
        out_specs=[smem, vmem, vmem, vmem, vmem],
        out_shape=[
            jax.ShapeDtypeStruct((3,), jnp.int32),
            jax.ShapeDtypeStruct((2, rows, KV_WIDTH), jnp.bfloat16),
            jax.ShapeDtypeStruct((rows, Q_WIDTH), jnp.bfloat16),
            jax.ShapeDtypeStruct((2, PROMPT, KV_WIDTH), jnp.bfloat16),
            jax.ShapeDtypeStruct((2, tail, KV_WIDTH), jnp.bfloat16),
        ],
    )(seq_image, vis_start, image_rows, keys_values)


def segments(positions, length_ref):
    end = jnp.int32(PREFIX)
    segment = jnp.where(positions < PREFIX, 0, 1)
    for at in range(NCOMP):
        end = end + length_ref[0, at]
        segment = segment + jnp.where(positions >= end, 1, 0)
    return segment


def hide(visible):
    return jnp.where(visible, 0.0, HIDDEN)


def second_kernel(
    rounds, tok_rows, image_rows, halo, vis_ref, length_ref, d_ref, kv_ref, t_ref, r_ref, *out_refs
):
    *window_refs, near_ref, whole_ref, image_ref, text_ref = out_refs
    here = lax.axis_index("ctx")
    ctx_size = lax.axis_size("ctx")
    row = lax.broadcasted_iota(jnp.int32, (IMAGE_BLOCK, tok_rows), 0)
    column = lax.broadcasted_iota(jnp.int32, (IMAGE_BLOCK, tok_rows), 1)
    place = jnp.where(row < image_rows, row, 1 << 20)
    picks = []
    for pairs in [[]] + rounds:
        target = here
        for source, other in pairs:
            target = jnp.where(here == source, other, target)
        begin = vis_ref[0] + image_rows * target - tok_rows * here
        picks.append(jnp.where(column == place + begin, 1.0, 0.0).astype(jnp.bfloat16))
    picked = dot_nn(jnp.concatenate(picks, axis=0), d_ref[...]).astype(jnp.bfloat16)
    for at, window_ref in enumerate(window_refs):
        window_ref[...] = picked[at * IMAGE_BLOCK : (at + 1) * IMAGE_BLOCK]

    @pl.when(pl.program_id(0) == 0)
    def _():
        vis = vis_ref[0]
        text = t_ref[...].astype(jnp.float32) + r_ref[...].astype(jnp.float32)
        if kv_ref.shape[1] == IMAGE_BLOCK:
            text_ref[:, :IMAGE_BLOCK] = kv_ref[...]
        text_ref[:, text_ref.shape[1] - PROMPT :] = text.astype(jnp.bfloat16)
        own_at = lax.broadcasted_iota(jnp.int32, (8, tok_rows), 1) + here * tok_rows
        own_segment = segments(own_at, length_ref)[:1]
        placeholder = (own_at >= vis) & (own_at < vis + VIS)
        own_row = jnp.where(placeholder, -1, own_at)
        whole_ref[...] = hide(own_row >= vis + VIS).astype(jnp.float32)
        own_row = own_row[:1]
        image_at = lax.broadcasted_iota(jnp.int32, (1, RATIO * IMAGE_BLOCK), 1) % IMAGE_BLOCK
        image_row = jnp.where(image_at < image_rows, vis + here * image_rows + image_at, -1)
        text_at = lax.broadcasted_iota(jnp.int32, (PROMPT, tok_rows), 0)
        text_at = text_at + jnp.where(text_at < vis, 0, VIS)
        near_ref[:PROMPT] = hide(text_at <= own_row)
        near_at = lax.broadcasted_iota(jnp.int32, (halo + tok_rows, tok_rows), 0)
        near_at = near_at + (here * tok_rows - halo)
        sees = (near_at <= own_row) & (near_at >= PREFIX)
        sees = sees & (segments(near_at, length_ref) == own_segment)
        near_ref[PROMPT:] = hide(sees)
        at = 0
        for core in range(2):
            for step in range(0, ctx_size, 2):
                begin = (here ^ (step + core)) * image_rows + vis
                shape = (image_rows, RATIO * IMAGE_BLOCK)
                block_at = lax.broadcasted_iota(jnp.int32, shape, 0) + begin
                image_ref[at : at + image_rows] = hide(block_at <= image_row)
                at += image_rows
        image_ref[VIS:] = hide(text_at <= image_row)


def second_arrays(vis_start, lengths, cotangent, image_kv, text, received, halo):
    tok_rows, width = cotangent.shape
    image_rows = image_kv.shape[1]
    text_rows = PROMPT + (image_rows if image_rows == IMAGE_BLOCK else 0)
    rounds = window_rounds(lax.axis_size("ctx"), tok_rows, image_rows)
    count = len(rounds) + 1
    block = 2048
    spec = pl.BlockSpec
    smem = spec(memory_space=pltpu.SMEM)
    lanes = RATIO * IMAGE_BLOCK
    near = PROMPT + halo + tok_rows
    whole = lambda *shape: spec(shape, lambda at: (0,) * len(shape))
    out = pl.pallas_call(
        functools.partial(second_kernel, rounds, tok_rows, image_rows, halo),
        grid=(width // block,),
        in_specs=[
            smem,
            smem,
            spec((tok_rows, block), lambda at: (0, at)),
            whole(2, image_rows, KV_WIDTH),
            whole(2, PROMPT, KV_WIDTH),
            whole(2, PROMPT, KV_WIDTH),
        ],
        out_specs=[spec((IMAGE_BLOCK, block), lambda at: (0, at)) for _ in range(count)]
        + [
            whole(near, tok_rows),
            whole(8, tok_rows),
            whole(PREFIX, lanes),
            whole(2, text_rows, KV_WIDTH),
        ],
        out_shape=[jax.ShapeDtypeStruct((IMAGE_BLOCK, width), jnp.bfloat16) for _ in range(count)]
        + [
            jax.ShapeDtypeStruct((near, tok_rows), jnp.float32),
            jax.ShapeDtypeStruct((8, tok_rows), jnp.float32),
            jax.ShapeDtypeStruct((PREFIX, lanes), jnp.float32),
            jax.ShapeDtypeStruct((2, text_rows, KV_WIDTH), jnp.bfloat16),
        ],
    )(vis_start, lengths, cotangent, image_kv, text, received)
    return out[:count], rounds, out[count:]


def first_products(parts, q_rows, d_rows):
    return [(dot_nt(keys, q_rows), dot_nt(values, d_rows)) for keys, values, _ in parts]


def chunks_of(rows):
    return [rows[at : at + KEY_CHUNK] for at in range(0, rows.shape[0], KEY_CHUNK)]


def fold_rows(rows, combine):
    folded = rows[:8]
    for at in range(8, rows.shape[0], 8):
        folded = combine(folded, rows[at : at + 8])
    return folded


def rows_backward(parts, products):
    scale = SCORE_SCALE * math.log2(math.e)
    scores, tops = [], []
    for (keys, values, bias), (raw, _) in zip(parts, products):
        one_row = bias.shape[0] == 1
        top = None
        for at, chunk in enumerate(chunks_of(raw)):
            chunk = chunk * scale
            if not one_row:
                chunk = chunk + bias[at * KEY_CHUNK : (at + 1) * KEY_CHUNK]
            scores.append((chunk, bias if one_row else None))
            folded = fold_rows(chunk, jnp.maximum)
            top = folded if top is None else jnp.maximum(top, folded)
        top = jnp.max(top, axis=0, keepdims=True)
        tops.append(top + bias if one_row else top)
    top = functools.reduce(jnp.maximum, tops)
    d_weights = [chunk for _, product in products for chunk in chunks_of(product)]
    total = mix = None
    kept = []
    for (chunk, bias), d_chunk in zip(scores, d_weights):
        terms = jnp.exp2(chunk + ((bias if bias is not None else 0.0) - top))
        folded = fold_rows(terms, jnp.add)
        total = folded if total is None else total + folded
        folded = fold_rows(terms * d_chunk, jnp.add)
        mix = folded if mix is None else mix + folded
        kept.append(terms)
    total = jnp.sum(total, axis=0, keepdims=True)
    mix = jnp.sum(mix, axis=0, keepdims=True)
    inverse = jnp.where(top > 0.5 * HIDDEN, 1.0 / total, 0.0)
    delta = mix * inverse
    weights, d_scores = [], []
    for terms, d_chunk in zip(kept, d_weights):
        chunk = terms * inverse
        weights.append(chunk.astype(jnp.bfloat16))
        d_scores.append((chunk * (d_chunk - delta)).astype(jnp.bfloat16))
    outcome = []
    for raw, _ in products:
        count = raw.shape[0] // KEY_CHUNK
        outcome.append(
            (jnp.concatenate(weights[:count], axis=0), jnp.concatenate(d_scores[:count], axis=0))
        )
        weights, d_scores = weights[count:], d_scores[count:]
    return outcome


def total_of(values):
    if len(values) == 1:
        return values[0]
    return sum(value.astype(jnp.float32) for value in values).astype(jnp.bfloat16)


def attend_kernel(
    block_rows,
    block_count,
    text_count,
    window_count,
    heads,
    halo,
    own,
    number_ref,
    near_ref,
    whole_ref,
    image_bias_ref,
    q_ref,
    d_ref,
    iq_ref,
    halo_ref,
    own_ref,
    *refs,
):
    block_refs, refs = refs[:block_count], refs[block_count:]
    text_refs, refs = refs[:text_count], refs[text_count:]
    window_refs, refs = refs[:window_count], refs[window_count:]
    dq_ref, *diq_refs, dmine_ref, dpair_ref, dhalo_ref, down_ref = refs
    text_refs = text_refs or [ref for ref in block_refs if ref.shape[1] > block_rows]
    near_bias = jnp.concatenate([near_ref[...]] * 2, axis=1)
    whole_bias = jnp.concatenate([whole_ref[:1]] * 2, axis=1)
    image_cotangent = total_of([ref[...] for ref in window_refs])
    image_queries = iq_ref[number_ref[1]]
    states = []
    units = []
    for head in range(heads):
        lanes = slice(head * HEAD_DIM, (head + 1) * HEAD_DIM)
        spans = [
            slice((head * RATIO + at) * HEAD_DIM, (head * RATIO + at + 1) * HEAD_DIM)
            for at in range(RATIO)
        ]
        visual, text, near = [], [], []
        for part in range(2):
            visual.append(
                jnp.concatenate([ref[part, :block_rows, lanes] for ref in block_refs], axis=0)
            )
            text.append(total_of([ref[part, -PROMPT:, lanes] for ref in text_refs]))
            near.append(
                jnp.concatenate(
                    [text[part], halo_ref[part, :, lanes], own_ref[0, part, :, lanes]], axis=0
                )
            )
        states.append((lanes, jnp.concatenate([visual[0], near[0]], axis=0).T, {}))
        own_parts = [(visual[0], visual[1], whole_bias), (near[0], near[1], near_bias)]
        for first in range(0, RATIO, 2):
            units.append((head, own_parts, q_ref, d_ref, spans[first : first + 2]))
        image_parts = [
            (visual[0], visual[1], image_bias_ref[:VIS]),
            (text[0], text[1], image_bias_ref[VIS:]),
        ]
        units.append((head, image_parts, image_queries, image_cotangent, spans))

    def begin(unit):
        _, parts, queries, cotangents, unit_spans = unit
        q_rows = jnp.concatenate([queries[:, span] for span in unit_spans], axis=0)
        d_rows = jnp.concatenate([cotangents[:, span] for span in unit_spans], axis=0)
        return q_rows, d_rows, first_products(parts, q_rows, d_rows)

    def finish(unit, begun):
        head, parts, _, _, unit_spans = unit
        lanes, keys_across, sums = states[head]
        q_rows, d_rows, products = begun
        outcome = rows_backward(parts, products)
        d_scores = jnp.concatenate([part[1] for part in outcome], axis=0)
        dq = dot_nn(keys_across[:, : d_scores.shape[0]], d_scores) * SCORE_SCALE
        dq = dq.astype(jnp.bfloat16).T
        rows = dq.shape[0] // len(unit_spans)
        for at, span in enumerate(unit_spans):
            if len(unit_spans) == 2:
                dq_ref[:, span] = dq[at * rows : (at + 1) * rows]
            else:
                for half, out_ref in enumerate(diq_refs):
                    place = at * rows + half * IMAGE_HALF
                    out_ref[:, span] = dq[place : place + IMAGE_HALF]
        for at, (weights, d_part) in enumerate(outcome):
            for kind, rows in ((0, dot_nn(d_part, q_rows)), (1, dot_nn(weights, d_rows))):
                count = rows.shape[0]
                earlier = sums.get((kind, at))
                if earlier is not None and count < earlier.shape[0]:
                    rows = jnp.concatenate([earlier[:count] + rows, earlier[count:]], axis=0)
                elif earlier is not None:
                    rows = earlier + rows
                sums[kind, at] = rows
        if len(unit_spans) == 2:
            return
        for part, scale in ((0, SCORE_SCALE), (1, 1.0)):
            of_visual = (sums[part, 0] * scale).astype(jnp.bfloat16)
            rest = sums[part, 1] * scale
            dmine_ref[part, :, lanes] = of_visual[: VIS // 2]
            dpair_ref[part, : VIS // 2, lanes] = of_visual[VIS // 2 :]
            dpair_ref[part, VIS // 2 :, lanes] = rest[:PROMPT].astype(jnp.bfloat16)
            dhalo_ref[part, :, lanes] = rest[PROMPT : PROMPT + halo].astype(jnp.bfloat16)
            down_ref[part, :, lanes] = rest[PROMPT + halo :]

    begun = begin(units[0])
    for at, unit in enumerate(units):
        later = begin(units[at + 1]) if at + 1 < len(units) else None
        finish(unit, begun)
        begun = later


def attend(
    number, masks, queries, cotangent, every_q, halo_kv, own_kv, blocks, texts, windows
):
    heads = 2
    near_bias, whole_bias, image_bias = masks
    own = queries.shape[0]
    halo = halo_kv.shape[1]
    groups = every_q.shape[0]
    columns = PREFIX + halo + own
    products = RATIO * (own * columns + IMAGE_BLOCK * PREFIX) * KV_HEADS
    spec = pl.BlockSpec
    kv_spec = lambda rows: spec((2, rows, heads * HEAD_DIM), lambda at: (0, 0, at))
    q_spec = lambda rows: spec((rows, heads * GROUP_WIDTH), lambda at: (0, at))
    whole = lambda rows: spec((rows, 128), lambda at: (0, 0))
    return pl.pallas_call(
        functools.partial(
            attend_kernel,
            VIS // len(blocks),
            len(blocks),
            len(texts),
            len(windows),
            heads,
            halo,
            own,
        ),
        grid=(KV_HEADS // heads,),
        in_specs=[
            spec(memory_space=pltpu.SMEM),
            whole(columns - VIS),
            whole(8),
            whole(PREFIX),
            q_spec(own),
            q_spec(own),
            spec((groups, IMAGE_BLOCK, heads * GROUP_WIDTH), lambda at: (0, 0, at)),
            kv_spec(halo),
            spec((1, 2, own, heads * HEAD_DIM), lambda at: (0, 0, 0, at)),
        ]
        + [kv_spec(block.shape[1]) for block in [*blocks, *texts]]
        + [q_spec(IMAGE_BLOCK) for _ in windows],
        out_specs=[
            q_spec(own),
            q_spec(IMAGE_HALF),
            q_spec(IMAGE_HALF),
            kv_spec(VIS // 2),
            kv_spec(VIS // 2 + PROMPT),
            kv_spec(halo),
            kv_spec(own),
        ],
        out_shape=[
            jax.ShapeDtypeStruct((own, Q_WIDTH), jnp.bfloat16),
            jax.ShapeDtypeStruct((IMAGE_HALF, Q_WIDTH), jnp.bfloat16),
            jax.ShapeDtypeStruct((IMAGE_HALF, Q_WIDTH), jnp.bfloat16),
            jax.ShapeDtypeStruct((2, VIS // 2, KV_WIDTH), jnp.bfloat16),
            jax.ShapeDtypeStruct((2, VIS // 2 + PROMPT, KV_WIDTH), jnp.bfloat16),
            jax.ShapeDtypeStruct((2, halo, KV_WIDTH), jnp.bfloat16),
            jax.ShapeDtypeStruct((2, own, KV_WIDTH), jnp.float32),
        ],
        cost_estimate=pl.CostEstimate(
            flops=10 * products * HEAD_DIM,
            bytes_accessed=12 * 1024 * 1024,
            transcendentals=products,
        ),
    )(
        number,
        near_bias,
        whole_bias,
        image_bias,
        queries,
        cotangent,
        every_q,
        halo_kv,
        own_kv,
        *blocks,
        *texts,
        *windows,
    )


def route(rows, number, back, beside=()):
    groups = lax.axis_size("rollout")
    arrays = [array for array, _ in beside]

    def move_beside(arrays):
        return [lax.ppermute(array, "ctx", pairs) for array, (_, pairs) in zip(arrays, beside)]

    if groups != 4:
        every = lax.all_gather(rows, "rollout", axis=0)
        picked = lax.dynamic_index_in_dim(every, number[2 if back else 1], 0, keepdims=False)
        return [picked] + move_beside(arrays)

    def branch(images):
        pairs = [(g, i) if back else (i, g) for g, i in enumerate(images)]
        if all(source == target for source, target in pairs):
            return lambda rows, arrays: [rows] + move_beside(arrays)
        return lambda rows, arrays: [lax.ppermute(rows, "rollout", pairs)] + move_beside(arrays)

    orders = itertools.permutations(range(groups))
    return lax.switch(number[0], [branch(images) for images in orders], rows, arrays)


def window_rounds(ctx_size, tok_rows, image_rows):
    rounds = []
    for target in range(ctx_size):
        lowest = (image_rows * target + 1) // tok_rows
        highest = (image_rows * target + image_rows - 1 + PROMPT - 1) // tok_rows
        for source in range(lowest, highest + 1):
            if source == target:
                continue
            for pairs in rounds:
                if all(s != source and t != target for s, t in pairs):
                    pairs.append((source, target))
                    break
            else:
                rounds.append([(source, target)])
    return rounds


def image_windows(windows, rounds):
    parts = [windows[0]] + [
        lax.ppermute(rows, "ctx", pairs) for rows, pairs in zip(windows[1:], rounds)
    ]
    if len(parts) > 8:
        parts = [sum(part.astype(jnp.float32) for part in parts).astype(jnp.bfloat16)]
    return parts


def xor_pairs(step):
    return [(at, at ^ step) for at in range(lax.axis_size("ctx"))]


def xor_permute(rows, step):
    return lax.ppermute(rows, "ctx", xor_pairs(step))


def on_device(function, *arrays):
    if lax.axis_size("ctx") != 8:
        return function(*arrays)
    shapes = jax.eval_shape(function, *arrays)

    def kernel(*refs):
        for out_ref, value in zip(
            refs[len(arrays) :], function(*[ref[...] for ref in refs[: len(arrays)]])
        ):
            out_ref[...] = value

    def spec(array):
        *rows, width = array.shape
        return pl.BlockSpec((*rows, width // 2), lambda at: (0,) * len(rows) + (at,))

    return pl.pallas_call(
        kernel,
        grid=(2,),
        in_specs=[spec(array) for array in arrays],
        out_specs=[spec(shape) for shape in shapes],
        out_shape=[jax.ShapeDtypeStruct(shape.shape, shape.dtype) for shape in shapes],
        cost_estimate=pl.CostEstimate(flops=1, bytes_accessed=1, transcendentals=0),
    )(*arrays)


def text_strides(ctx_size, late_shard):
    strides = [1 << at for at in range(1, ctx_size.bit_length() - 1)]
    return [stride for stride in reversed(strides) if stride != late_shard]


def chip_steps(ctx_size):
    return list(range(2, ctx_size, 2))


def gather_prefix(image_kv, text, late_shard):
    ctx_size = lax.axis_size("ctx")
    steps = chip_steps(ctx_size)
    if ctx_size == 8:
        mine = [text, xor_permute(image_kv, 2), xor_permute(text, 4), xor_permute(image_kv, 6)]
        blocks = mine + [xor_permute(block, 1) for block in mine]
        return blocks, [blocks[at] for at in (0, 2, 4, 6)]
    mine = jnp.concatenate(
        [image_kv] + [xor_permute(image_kv, step) for step in steps], axis=1
    )
    return [mine, xor_permute(mine, 1)], list(spread_text(text, late_shard))


def split_sums(image_rows, steps, d_mine, d_pair, other):
    half = VIS // 2
    add = lambda one, two: one.astype(jnp.float32) + two.astype(jnp.float32)
    text = add(d_pair[:, half:], other[:, half:])
    out = []
    for at in range(len(steps) + 1):
        rows = slice(at * image_rows, (at + 1) * image_rows)
        sums = add(d_mine[:, rows], other[:, rows])
        if len(steps) == 3 and steps[at - 1] == 4 and at:
            sums = jnp.concatenate([sums, text], axis=1)
        out.append(sums.astype(jnp.bfloat16) if at else sums)
    return out + [text]


def add_sums(image_rows, own, text, *parts):
    for part in parts:
        own = own + part[:, :image_rows].astype(jnp.float32)
        if part.shape[1] > image_rows:
            text = text + part[:, image_rows:].astype(jnp.float32)
    return [own.astype(jnp.bfloat16), text.astype(jnp.bfloat16)]


def spread_text(text, late_shard):
    for stride in text_strides(lax.axis_size("ctx"), late_shard):
        text = text + xor_permute(text, stride)
    return text, xor_permute(text, 1)


def collect_text(text, late_shard):
    for stride in reversed(text_strides(lax.axis_size("ctx"), late_shard)):
        moved = xor_permute(text.astype(jnp.bfloat16), stride)
        text = text.astype(jnp.float32) + moved.astype(jnp.float32)
    return text.astype(jnp.bfloat16)


def halo_cuts(tok_rows, halo):
    cuts = []
    left = halo
    while left > 0:
        cuts.append(min(left, tok_rows))
        left -= cuts[-1]
    return cuts


def halo_rows(tail, halo, tok_rows):
    ctx_size = lax.axis_size("ctx")
    parts = []
    for step, count in enumerate(halo_cuts(tok_rows, halo), 1):
        pairs = [(at, at + step) for at in range(ctx_size - step)]
        rows = tail if count == tail.shape[1] else tail[:, tail.shape[1] - count :]
        parts.insert(0, lax.ppermute(rows, "ctx", pairs))
    return jnp.concatenate(parts, axis=1) if len(parts) > 1 else parts[0]


def halo_parts(d_halo, tok_rows):
    ctx_size = lax.axis_size("ctx")
    cuts = halo_cuts(tok_rows, d_halo.shape[1])
    parts = []
    end = d_halo.shape[1]
    for step, count in enumerate(cuts, 1):
        rows = d_halo if len(cuts) == 1 else d_halo[:, end - count : end]
        parts.append((rows, [(at + step, at) for at in range(ctx_size - step)]))
        end -= count
    return parts


def last_kernel(part_count, vis_ref, dkv_ref, down_ref, text_ref, other_ref, *refs):
    part_refs = refs[:part_count]
    *dq_refs, image_ref, kv_ref = refs[part_count:]
    here = lax.axis_index("ctx")
    tok_rows = down_ref.shape[1]
    at = 0
    for dq_ref in dq_refs:
        image_ref[0, at : at + dq_ref.shape[0], :Q_WIDTH] = dq_ref[...]
        at += dq_ref.shape[0]
    image_ref[0, :, Q_WIDTH : Q_WIDTH + KV_WIDTH] = dkv_ref[0]
    image_ref[0, :, Q_WIDTH + KV_WIDTH :] = dkv_ref[1]
    at = lax.broadcasted_iota(jnp.int32, (PROMPT, KV_WIDTH), 0)
    ahead = jnp.where(here == 0, 1, 0)
    behind = jnp.where(here == VIS // tok_rows, 1, 0)
    kept = jnp.where(at < vis_ref[0], ahead, behind) == 1
    for part in range(2):
        text = text_ref[part].astype(jnp.float32) + other_ref[part].astype(jnp.float32)
        text = jnp.where(kept, text, 0.0)
        sums = down_ref[part] + jnp.concatenate(
            [text, jnp.zeros((tok_rows - PROMPT, KV_WIDTH), jnp.float32)], axis=0
        )
        for part_ref in part_refs:
            back = part_ref[part].astype(jnp.float32)
            if back.shape[0] < tok_rows:
                missing = jnp.zeros((tok_rows - back.shape[0], KV_WIDTH), jnp.float32)
                back = jnp.concatenate([missing, back], axis=0)
            sums = sums + back
        kv_ref[0, part] = sums.astype(jnp.bfloat16)


def last_arrays(vis_start, image_dq, image_dkv, d_own_kv, text, other_text, parts):
    rows = image_dkv.shape[1]
    smem = pl.BlockSpec(memory_space=pltpu.SMEM)
    vmem = pl.BlockSpec(memory_space=pltpu.VMEM)
    return pl.pallas_call(
        functools.partial(last_kernel, len(parts)),
        in_specs=[smem] + [vmem] * (4 + len(parts) + len(image_dq)),
        out_specs=[vmem, vmem],
        out_shape=[
            jax.ShapeDtypeStruct((1, rows, Q_WIDTH + 2 * KV_WIDTH), jnp.bfloat16),
            jax.ShapeDtypeStruct((1,) + d_own_kv.shape, jnp.bfloat16),
        ],
    )(vis_start, image_dkv, d_own_kv, text, other_text, *parts, *image_dq)


def gather_queries(image_q):
    every = lax.all_gather(image_q, "rollout", axis=0)
    missing = IMAGE_BLOCK - every.shape[1]
    return jnp.pad(every, ((0, 0), (0, missing), (0, 0))) if missing else every


def per_device(queries, keys_values, image_rows, cotangent, seq_image, vis_start, comp_lengths):
    tok_rows = queries.shape[1]
    image_count = image_rows.shape[1]
    ctx_size = lax.axis_size("ctx")
    seq_len = tok_rows * ctx_size
    late_shard = VIS // tok_rows
    longest = 4 * (seq_len - PREFIX) // (3 * NCOMP)
    halo = -(-(longest - 1) // 64) * 64
    q_own, d_own = queries[0], cotangent[0]

    number, image_kv, image_q, text, tail = first_arrays(
        seq_image, vis_start, image_rows, keys_values, halo
    )
    every_q = gather_queries(image_q)
    image_kv, swapped = route(image_kv, number, False, [(text, xor_pairs(late_shard))])
    image_kv, d_later = lax.optimization_barrier((image_kv, d_own))
    windows, rounds, (*masks, text) = second_arrays(
        vis_start, comp_lengths, d_later, image_kv, text, swapped, halo
    )
    blocks, texts = gather_prefix(image_kv, text, late_shard)
    windows = image_windows(windows, rounds)
    halo_kv = halo_rows(tail, halo, tok_rows)

    grad_q, *d_image_q, d_mine, d_pair, d_halo, d_own_kv = attend(
        number,
        masks,
        q_own,
        d_own,
        every_q,
        halo_kv,
        keys_values,
        blocks,
        [] if ctx_size == 8 else texts,
        windows,
    )

    d_image_q = [
        half[: image_count - at * IMAGE_HALF]
        for at, half in enumerate(d_image_q)
        if at * IMAGE_HALF < image_count
    ]
    image_dq, other = route(d_image_q[0], number, True, [(d_pair, xor_pairs(1))])
    image_dq = [image_dq]
    steps = chip_steps(ctx_size)
    own, *sent, d_text = on_device(
        functools.partial(split_sums, image_count, steps), d_mine, d_pair, other
    )
    beside = [(rows, xor_pairs(step)) for rows, step in zip(sent, steps)]
    if len(d_image_q) > 1:
        second, *moved = route(d_image_q[1], number, True, beside)
        image_dq.append(second)
    else:
        moved = [lax.ppermute(rows, "ctx", pairs) for rows, pairs in beside]
    sums, d_text = on_device(functools.partial(add_sums, image_count), own, d_text, *moved)
    if ctx_size != 8:
        d_text = collect_text(d_text, late_shard)
    image_dkv, other_text, *halo_back = route(
        sums, number, True, [(d_text, xor_pairs(late_shard))] + halo_parts(d_halo, tok_rows)
    )
    grad_image, grad_kv = last_arrays(
        vis_start, image_dq, image_dkv, d_own_kv, d_text, other_text, halo_back
    )
    return (grad_q[None], grad_kv, grad_image)


def solution(mesh):
    placed = (
        P("rollout", "ctx", None),
        P("rollout", None, "ctx", None),
        P("rollout", "ctx", None),
        P("rollout", "ctx", None),
        P(),
        P("rollout"),
        P("rollout", None),
    )
    return jax.shard_map(
        per_device,
        mesh=mesh,
        in_specs=placed,
        out_specs=(
            P("rollout", "ctx", None),
            P("rollout", None, "ctx", None),
            P("rollout", "ctx", None),
        ),
        check_vma=False,
    )
```

```python
import functools
import itertools
import math

import jax
import jax.numpy as jnp
from jax import lax
from jax.experimental import pallas as pl
from jax.experimental.pallas import tpu as pltpu
from jax.sharding import PartitionSpec as P

HEADS = 32
KV_HEADS = 8
HEAD_DIM = 128
VIS = 256
PROMPT = 64
NCOMP = 16

RATIO = HEADS // KV_HEADS
PREFIX = VIS + PROMPT
Q_WIDTH = HEADS * HEAD_DIM
KV_WIDTH = KV_HEADS * HEAD_DIM
GROUP_WIDTH = RATIO * HEAD_DIM
IMAGE_BLOCK = 32
IMAGE_HALF = IMAGE_BLOCK // 2
KEY_CHUNK = 64
HIDDEN = -1e30
SCORE_SCALE = 1.0 / math.sqrt(HEAD_DIM)


def dot_nt(left, right):
    return lax.dot_general(
        left, right, (((1,), (1,)), ((), ())), preferred_element_type=jnp.float32
    )


def dot_nn(left, right):
    return lax.dot_general(
        left, right, (((1,), (0,)), ((), ())), preferred_element_type=jnp.float32
    )


def dot_tn(left, right):
    return lax.dot_general(
        left, right, (((0,), (0,)), ((), ())), preferred_element_type=jnp.float32
    )


def first_kernel(halo, seq_ref, vis_ref, image_ref, kv_ref, number_ref, *out_refs):
    ikv_ref, iq_ref, text_ref, tail_ref = out_refs
    groups = seq_ref.shape[0]
    group = lax.axis_index("rollout")
    here = lax.axis_index("ctx")
    images = [seq_ref[at] for at in range(groups)]
    number = jnp.int32(0)
    if groups == 4:
        for at, weight in enumerate((6, 2, 1)):
            for later in range(at + 1, groups):
                number = number + jnp.where(images[later] < images[at], weight, 0)
    place = jnp.int32(0)
    user = jnp.int32(0)
    for at in range(groups):
        place = place + jnp.where(group == at, images[at], 0)
        user = user + jnp.where(images[at] == group, at, 0)
    number_ref[0] = number
    number_ref[1] = place
    number_ref[2] = user
    iq_ref[...] = image_ref[0, :, :Q_WIDTH]
    ikv_ref[0] = image_ref[0, :, Q_WIDTH : Q_WIDTH + KV_WIDTH]
    ikv_ref[1] = image_ref[0, :, Q_WIDTH + KV_WIDTH :]
    tok_rows = kv_ref.shape[2]
    late_shard = VIS // tok_rows
    at = lax.broadcasted_iota(jnp.int32, (PROMPT, KV_WIDTH), 0)
    ahead = jnp.where(here == 0, 1, 0)
    behind = jnp.where(here == late_shard, 1, 0)
    kept = jnp.where(at < vis_ref[0], ahead, behind) == 1
    for part in range(2):
        rows = kv_ref[0, part, :PROMPT].astype(jnp.float32)
        text_ref[part] = jnp.where(kept, rows, 0.0).astype(jnp.bfloat16)
        tail_ref[part] = kv_ref[0, part, tok_rows - halo :]


def first_arrays(seq_image, vis_start, image_rows, keys_values, halo):
    rows = image_rows.shape[1]
    smem = pl.BlockSpec(memory_space=pltpu.SMEM)
    vmem = pl.BlockSpec(memory_space=pltpu.VMEM)
    tail = min(halo, keys_values.shape[2])
    return pl.pallas_call(
        functools.partial(first_kernel, tail),
        in_specs=[smem, smem, vmem, vmem],
        out_specs=[smem, vmem, vmem, vmem, vmem],
        out_shape=[
            jax.ShapeDtypeStruct((3,), jnp.int32),
            jax.ShapeDtypeStruct((2, rows, KV_WIDTH), jnp.bfloat16),
            jax.ShapeDtypeStruct((rows, Q_WIDTH), jnp.bfloat16),
            jax.ShapeDtypeStruct((2, PROMPT, KV_WIDTH), jnp.bfloat16),
            jax.ShapeDtypeStruct((2, tail, KV_WIDTH), jnp.bfloat16),
        ],
    )(seq_image, vis_start, image_rows, keys_values)


def segments(positions, length_ref):
    end = jnp.int32(PREFIX)
    segment = jnp.where(positions < PREFIX, 0, 1)
    for at in range(NCOMP):
        end = end + length_ref[0, at]
        segment = segment + jnp.where(positions >= end, 1, 0)
    return segment


def hide(visible):
    return jnp.where(visible, 0.0, HIDDEN)


def second_kernel(
    targets, tok_rows, image_rows, halo, vis_ref, length_ref, d_ref, kv_ref, t_ref, r_ref, *out_refs
):
    *window_refs, near_ref, whole_ref, image_ref, text_ref = out_refs
    here = lax.axis_index("ctx")
    ctx_size = lax.axis_size("ctx")
    row = lax.broadcasted_iota(jnp.int32, (IMAGE_BLOCK, tok_rows), 0)
    column = lax.broadcasted_iota(jnp.int32, (IMAGE_BLOCK, tok_rows), 1)
    place = jnp.where(row < image_rows, row, 1 << 20)
    picks = []
    for blocks in targets:
        for default, special in blocks:
            target = here if default is None else default
            for source, other in special:
                target = jnp.where(here == source, other, target)
            begin = vis_ref[0] + image_rows * target - tok_rows * here
            picks.append(jnp.where(column == place + begin, 1.0, 0.0).astype(jnp.bfloat16))
    picked = dot_nn(jnp.concatenate(picks, axis=0), d_ref[...]).astype(jnp.bfloat16)
    at = 0
    for window_ref in window_refs:
        window_ref[...] = picked[at : at + window_ref.shape[0]]
        at += window_ref.shape[0]

    @pl.when(pl.program_id(0) == 0)
    def _():
        vis = vis_ref[0]
        text = t_ref[...].astype(jnp.float32) + r_ref[...].astype(jnp.float32)
        if kv_ref.shape[1] == IMAGE_BLOCK:
            text_ref[:, :IMAGE_BLOCK] = kv_ref[...]
        text_ref[:, text_ref.shape[1] - PROMPT :] = text.astype(jnp.bfloat16)
        own_at = lax.broadcasted_iota(jnp.int32, (8, tok_rows), 1) + here * tok_rows
        own_segment = segments(own_at, length_ref)[:1]
        placeholder = (own_at >= vis) & (own_at < vis + VIS)
        own_row = jnp.where(placeholder, -1, own_at)
        whole_ref[...] = hide(own_row >= vis + VIS).astype(jnp.float32)
        own_row = own_row[:1]
        image_at = lax.broadcasted_iota(jnp.int32, (1, RATIO * IMAGE_BLOCK), 1) % IMAGE_BLOCK
        image_row = jnp.where(image_at < image_rows, vis + here * image_rows + image_at, -1)
        text_at = lax.broadcasted_iota(jnp.int32, (PROMPT, tok_rows), 0)
        text_at = text_at + jnp.where(text_at < vis, 0, VIS)
        near_ref[:PROMPT] = hide(text_at <= own_row)
        near_at = lax.broadcasted_iota(jnp.int32, (halo + tok_rows, tok_rows), 0)
        near_at = near_at + (here * tok_rows - halo)
        sees = (near_at <= own_row) & (near_at >= PREFIX)
        sees = sees & (segments(near_at, length_ref) == own_segment)
        near_ref[PROMPT:] = hide(sees)
        at = 0
        for core in range(2):
            for step in range(0, ctx_size, 2):
                begin = (here ^ (step + core)) * image_rows + vis
                shape = (image_rows, RATIO * IMAGE_BLOCK)
                block_at = lax.broadcasted_iota(jnp.int32, shape, 0) + begin
                image_ref[at : at + image_rows] = hide(block_at <= image_row)
                at += image_rows
        image_ref[VIS:] = hide(text_at <= image_row)


def second_arrays(vis_start, lengths, cotangent, image_kv, text, received, halo):
    tok_rows, width = cotangent.shape
    image_rows = image_kv.shape[1]
    text_rows = PROMPT + (image_rows if image_rows == IMAGE_BLOCK else 0)
    targets, rounds = window_targets(lax.axis_size("ctx"), tok_rows, image_rows)
    counts = [len(blocks) * IMAGE_BLOCK for blocks in targets]
    block = 2048
    spec = pl.BlockSpec
    smem = spec(memory_space=pltpu.SMEM)
    lanes = RATIO * IMAGE_BLOCK
    near = PROMPT + halo + tok_rows
    whole = lambda *shape: spec(shape, lambda at: (0,) * len(shape))
    out = pl.pallas_call(
        functools.partial(second_kernel, targets, tok_rows, image_rows, halo),
        grid=(width // block,),
        in_specs=[
            smem,
            smem,
            spec((tok_rows, block), lambda at: (0, at)),
            whole(2, image_rows, KV_WIDTH),
            whole(2, PROMPT, KV_WIDTH),
            whole(2, PROMPT, KV_WIDTH),
        ],
        out_specs=[spec((count, block), lambda at: (0, at)) for count in counts]
        + [
            whole(near, tok_rows),
            whole(8, tok_rows),
            whole(PREFIX, lanes),
            whole(2, text_rows, KV_WIDTH),
        ],
        out_shape=[jax.ShapeDtypeStruct((count, width), jnp.bfloat16) for count in counts]
        + [
            jax.ShapeDtypeStruct((near, tok_rows), jnp.float32),
            jax.ShapeDtypeStruct((8, tok_rows), jnp.float32),
            jax.ShapeDtypeStruct((PREFIX, lanes), jnp.float32),
            jax.ShapeDtypeStruct((2, text_rows, KV_WIDTH), jnp.bfloat16),
        ],
    )(vis_start, lengths, cotangent, image_kv, text, received)
    return out[: len(counts)], rounds, out[len(counts) :]


def first_products(parts, q_rows, d_rows):
    return [(dot_nt(keys, q_rows), dot_nt(values, d_rows)) for keys, values, _ in parts]


def chunks_of(rows):
    return [rows[at : at + KEY_CHUNK] for at in range(0, rows.shape[0], KEY_CHUNK)]


def fold_rows(rows, combine):
    folded = rows[:8]
    for at in range(8, rows.shape[0], 8):
        folded = combine(folded, rows[at : at + 8])
    return folded


def rows_backward(parts, products):
    scale = SCORE_SCALE * math.log2(math.e)
    scores, tops = [], []
    for (keys, values, bias), (raw, _) in zip(parts, products):
        one_row = bias.shape[0] == 1
        top = None
        for at, chunk in enumerate(chunks_of(raw)):
            chunk = chunk * scale
            if not one_row:
                chunk = chunk + bias[at * KEY_CHUNK : (at + 1) * KEY_CHUNK]
            scores.append((chunk, bias if one_row else None))
            folded = fold_rows(chunk, jnp.maximum)
            top = folded if top is None else jnp.maximum(top, folded)
        top = jnp.max(top, axis=0, keepdims=True)
        tops.append(top + bias if one_row else top)
    top = functools.reduce(jnp.maximum, tops)
    d_weights = [chunk for _, product in products for chunk in chunks_of(product)]
    total = mix = None
    kept = []
    for (chunk, bias), d_chunk in zip(scores, d_weights):
        terms = jnp.exp2(chunk + ((bias if bias is not None else 0.0) - top))
        folded = fold_rows(terms, jnp.add)
        total = folded if total is None else total + folded
        folded = fold_rows(terms * d_chunk, jnp.add)
        mix = folded if mix is None else mix + folded
        kept.append(terms)
    total = jnp.sum(total, axis=0, keepdims=True)
    mix = jnp.sum(mix, axis=0, keepdims=True)
    inverse = jnp.where(top > 0.5 * HIDDEN, 1.0 / total, 0.0)
    delta = mix * inverse
    weights, d_scores = [], []
    for terms, d_chunk in zip(kept, d_weights):
        chunk = terms * inverse
        weights.append(chunk.astype(jnp.bfloat16))
        d_scores.append((chunk * (d_chunk - delta)).astype(jnp.bfloat16))
    outcome = []
    for raw, _ in products:
        count = raw.shape[0] // KEY_CHUNK
        outcome.append(
            (jnp.concatenate(weights[:count], axis=0), jnp.concatenate(d_scores[:count], axis=0))
        )
        weights, d_scores = weights[count:], d_scores[count:]
    return outcome


def total_of(values):
    if len(values) == 1:
        return values[0]
    return sum(value.astype(jnp.float32) for value in values).astype(jnp.bfloat16)


def attend_kernel(
    block_rows,
    block_count,
    text_count,
    window_count,
    heads,
    halo,
    own,
    number_ref,
    near_ref,
    whole_ref,
    image_bias_ref,
    q_ref,
    d_ref,
    iq_ref,
    halo_ref,
    own_ref,
    *refs,
):
    block_refs, refs = refs[:block_count], refs[block_count:]
    text_refs, refs = refs[:text_count], refs[text_count:]
    window_refs, refs = refs[:window_count], refs[window_count:]
    dq_ref, *diq_refs, dmine_ref, dpair_ref, dhalo_ref, down_ref = refs
    text_refs = text_refs or [ref for ref in block_refs if ref.shape[1] > block_rows]
    near_bias = jnp.concatenate([near_ref[...]] * 2, axis=1)
    whole_bias = jnp.concatenate([whole_ref[:1]] * 2, axis=1)
    image_cotangent = total_of([ref[...] for ref in window_refs])
    image_queries = iq_ref[number_ref[1]]
    states = []
    units = []
    for head in range(heads):
        lanes = slice(head * HEAD_DIM, (head + 1) * HEAD_DIM)
        spans = [
            slice((head * RATIO + at) * HEAD_DIM, (head * RATIO + at + 1) * HEAD_DIM)
            for at in range(RATIO)
        ]
        visual, text, near = [], [], []
        for part in range(2):
            visual.append(
                jnp.concatenate([ref[part, :block_rows, lanes] for ref in block_refs], axis=0)
            )
            text.append(total_of([ref[part, -PROMPT:, lanes] for ref in text_refs]))
            near.append(
                jnp.concatenate(
                    [text[part], halo_ref[part, :, lanes], own_ref[0, part, :, lanes]], axis=0
                )
            )
        states.append((lanes, jnp.concatenate([visual[0], near[0]], axis=0).T, {}))
        own_parts = [(visual[0], visual[1], whole_bias), (near[0], near[1], near_bias)]
        for first in range(0, RATIO, 2):
            units.append((head, own_parts, q_ref, d_ref, spans[first : first + 2]))
        image_parts = [
            (visual[0], visual[1], image_bias_ref[:VIS]),
            (text[0], text[1], image_bias_ref[VIS:]),
        ]
        units.append((head, image_parts, image_queries, image_cotangent, spans))

    def begin(unit):
        _, parts, queries, cotangents, unit_spans = unit
        q_rows = jnp.concatenate([queries[:, span] for span in unit_spans], axis=0)
        d_rows = jnp.concatenate([cotangents[:, span] for span in unit_spans], axis=0)
        return q_rows, d_rows, first_products(parts, q_rows, d_rows)

    def finish(unit, begun):
        head, parts, _, _, unit_spans = unit
        lanes, keys_across, sums = states[head]
        q_rows, d_rows, products = begun
        outcome = rows_backward(parts, products)
        d_scores = jnp.concatenate([part[1] for part in outcome], axis=0)
        dq = dot_nn(keys_across[:, : d_scores.shape[0]], d_scores) * SCORE_SCALE
        dq = dq.astype(jnp.bfloat16).T
        rows = dq.shape[0] // len(unit_spans)
        for at, span in enumerate(unit_spans):
            if len(unit_spans) == 2:
                dq_ref[:, span] = dq[at * rows : (at + 1) * rows]
            else:
                for half, out_ref in enumerate(diq_refs):
                    place = at * rows + half * IMAGE_HALF
                    out_ref[:, span] = dq[place : place + IMAGE_HALF]
        for at, (weights, d_part) in enumerate(outcome):
            for kind, rows in ((0, dot_nn(d_part, q_rows)), (1, dot_nn(weights, d_rows))):
                count = rows.shape[0]
                earlier = sums.get((kind, at))
                if earlier is not None and count < earlier.shape[0]:
                    rows = jnp.concatenate([earlier[:count] + rows, earlier[count:]], axis=0)
                elif earlier is not None:
                    rows = earlier + rows
                sums[kind, at] = rows
        if len(unit_spans) == 2:
            return
        for part, scale in ((0, SCORE_SCALE), (1, 1.0)):
            of_visual = (sums[part, 0] * scale).astype(jnp.bfloat16)
            rest = sums[part, 1] * scale
            dmine_ref[part, :, lanes] = of_visual[: VIS // 2]
            dpair_ref[part, : VIS // 2, lanes] = of_visual[VIS // 2 :]
            dpair_ref[part, VIS // 2 :, lanes] = rest[:PROMPT].astype(jnp.bfloat16)
            dhalo_ref[part, :, lanes] = rest[PROMPT : PROMPT + halo].astype(jnp.bfloat16)
            down_ref[part, :, lanes] = rest[PROMPT + halo :]

    begun = begin(units[0])
    for at, unit in enumerate(units):
        later = begin(units[at + 1]) if at + 1 < len(units) else None
        finish(unit, begun)
        begun = later


def attend(
    number, masks, queries, cotangent, every_q, halo_kv, own_kv, blocks, texts, windows
):
    heads = 2
    near_bias, whole_bias, image_bias = masks
    own = queries.shape[0]
    halo = halo_kv.shape[1]
    groups = every_q.shape[0]
    columns = PREFIX + halo + own
    products = RATIO * (own * columns + IMAGE_BLOCK * PREFIX) * KV_HEADS
    spec = pl.BlockSpec
    kv_spec = lambda rows: spec((2, rows, heads * HEAD_DIM), lambda at: (0, 0, at))
    q_spec = lambda rows: spec((rows, heads * GROUP_WIDTH), lambda at: (0, at))
    whole = lambda rows: spec((rows, 128), lambda at: (0, 0))
    return pl.pallas_call(
        functools.partial(
            attend_kernel,
            VIS // len(blocks),
            len(blocks),
            len(texts),
            len(windows),
            heads,
            halo,
            own,
        ),
        grid=(KV_HEADS // heads,),
        in_specs=[
            spec(memory_space=pltpu.SMEM),
            whole(columns - VIS),
            whole(8),
            whole(PREFIX),
            q_spec(own),
            q_spec(own),
            spec((groups, IMAGE_BLOCK, heads * GROUP_WIDTH), lambda at: (0, 0, at)),
            kv_spec(halo),
            spec((1, 2, own, heads * HEAD_DIM), lambda at: (0, 0, 0, at)),
        ]
        + [kv_spec(block.shape[1]) for block in [*blocks, *texts]]
        + [q_spec(IMAGE_BLOCK) for _ in windows],
        out_specs=[
            q_spec(own),
            q_spec(IMAGE_HALF),
            q_spec(IMAGE_HALF),
            kv_spec(VIS // 2),
            kv_spec(VIS // 2 + PROMPT),
            kv_spec(halo),
            kv_spec(own),
        ],
        out_shape=[
            jax.ShapeDtypeStruct((own, Q_WIDTH), jnp.bfloat16),
            jax.ShapeDtypeStruct((IMAGE_HALF, Q_WIDTH), jnp.bfloat16),
            jax.ShapeDtypeStruct((IMAGE_HALF, Q_WIDTH), jnp.bfloat16),
            jax.ShapeDtypeStruct((2, VIS // 2, KV_WIDTH), jnp.bfloat16),
            jax.ShapeDtypeStruct((2, VIS // 2 + PROMPT, KV_WIDTH), jnp.bfloat16),
            jax.ShapeDtypeStruct((2, halo, KV_WIDTH), jnp.bfloat16),
            jax.ShapeDtypeStruct((2, own, KV_WIDTH), jnp.float32),
        ],
        cost_estimate=pl.CostEstimate(
            flops=10 * products * HEAD_DIM,
            bytes_accessed=12 * 1024 * 1024,
            transcendentals=products,
        ),
    )(
        number,
        near_bias,
        whole_bias,
        image_bias,
        queries,
        cotangent,
        every_q,
        halo_kv,
        own_kv,
        *blocks,
        *texts,
        *windows,
    )


def route(rows, number, back, beside=()):
    groups = lax.axis_size("rollout")
    arrays = [array for array, _ in beside]

    def move_beside(arrays):
        return [lax.ppermute(array, "ctx", pairs) for array, (_, pairs) in zip(arrays, beside)]

    if groups != 4:
        every = lax.all_gather(rows, "rollout", axis=0)
        picked = lax.dynamic_index_in_dim(every, number[2 if back else 1], 0, keepdims=False)
        return [picked] + move_beside(arrays)

    def branch(images):
        pairs = [(g, i) if back else (i, g) for g, i in enumerate(images)]
        return lambda rows, arrays: [lax.ppermute(rows, "rollout", pairs)] + move_beside(arrays)

    orders = itertools.permutations(range(groups))
    return lax.switch(number[0], [branch(images) for images in orders], rows, arrays)


def window_rounds(ctx_size, tok_rows, image_rows):
    rounds = []
    for target in range(ctx_size):
        lowest = (image_rows * target + 1) // tok_rows
        highest = (image_rows * target + image_rows - 1 + PROMPT - 1) // tok_rows
        for source in range(lowest, highest + 1):
            if source == target:
                continue
            for pairs in rounds:
                if all(s != source and t != target for s, t in pairs):
                    pairs.append((source, target))
                    break
            else:
                rounds.append([(source, target)])
    return rounds


def window_targets(ctx_size, tok_rows, image_rows):
    rounds = window_rounds(ctx_size, tok_rows, image_rows)
    if ctx_size != 8:
        return [[(None, [])]] + [[(None, pairs)] for pairs in rounds], rounds
    rounds = [[(0, 2), (1, 4), (2, 6)], [(0, 3), (1, 5), (2, 7)], [(1, 6)], [(1, 7)]]
    swapped = [(2, [(0, 1)]), (3, [])]
    return [[(None, [])]] + [[(None, pairs)] for pairs in rounds] + [swapped], rounds


def join_windows(own, one, two, swapped):
    here = lax.axis_index("ctx")
    wide = lambda rows: rows.astype(jnp.float32)
    near, far = swapped[:IMAGE_BLOCK], swapped[IMAGE_BLOCK:]
    sums = [
        jnp.where(here == 1, wide(own) + wide(near), wide(own)),
        jnp.where(here == 0, wide(one) + wide(near), wide(one)),
        jnp.where(here == 0, wide(two) + wide(far), wide(two)),
    ]
    return [part.astype(jnp.bfloat16) for part in sums]


def image_windows(windows, rounds):
    own, *sent = windows
    if lax.axis_size("ctx") == 8:
        one, two, three, four, swapped = sent
        late = [lax.ppermute(rows, "ctx", pairs) for rows, pairs in zip((three, four), rounds[2:])]
        own, one, two = on_device(join_windows, own, one, two, xor_permute(swapped, 1))
        return [own] + late + [
            lax.ppermute(rows, "ctx", pairs) for rows, pairs in zip((one, two), rounds)
        ]
    parts = [own] + [lax.ppermute(rows, "ctx", pairs) for rows, pairs in zip(sent, rounds)]
    return [sum(part.astype(jnp.float32) for part in parts).astype(jnp.bfloat16)]


def xor_pairs(step):
    return [(at, at ^ step) for at in range(lax.axis_size("ctx"))]


def xor_permute(rows, step):
    return lax.ppermute(rows, "ctx", xor_pairs(step))


def on_device(function, *arrays):
    if lax.axis_size("ctx") != 8:
        return function(*arrays)
    shapes = jax.eval_shape(function, *arrays)

    def kernel(*refs):
        for out_ref, value in zip(
            refs[len(arrays) :], function(*[ref[...] for ref in refs[: len(arrays)]])
        ):
            out_ref[...] = value

    def spec(array):
        *rows, width = array.shape
        return pl.BlockSpec((*rows, width // 2), lambda at: (0,) * len(rows) + (at,))

    return pl.pallas_call(
        kernel,
        grid=(2,),
        in_specs=[spec(array) for array in arrays],
        out_specs=[spec(shape) for shape in shapes],
        out_shape=[jax.ShapeDtypeStruct(shape.shape, shape.dtype) for shape in shapes],
        cost_estimate=pl.CostEstimate(flops=1, bytes_accessed=1, transcendentals=0),
    )(*arrays)


def text_strides(ctx_size, late_shard):
    strides = [1 << at for at in range(1, ctx_size.bit_length() - 1)]
    return [stride for stride in reversed(strides) if stride != late_shard]


def chip_steps(ctx_size):
    return list(range(2, ctx_size, 2))


def gather_prefix(image_kv, text, late_shard):
    ctx_size = lax.axis_size("ctx")
    steps = chip_steps(ctx_size)
    if ctx_size == 8:
        mine = [text, xor_permute(image_kv, 2), xor_permute(text, 4), xor_permute(image_kv, 6)]
        blocks = mine + [xor_permute(block, 1) for block in mine]
        return blocks, [blocks[at] for at in (0, 2, 4, 6)]
    mine = jnp.concatenate(
        [image_kv] + [xor_permute(image_kv, step) for step in steps], axis=1
    )
    return [mine, xor_permute(mine, 1)], list(spread_text(text, late_shard))


def split_sums(image_rows, steps, d_mine, d_pair, other):
    half = VIS // 2
    add = lambda one, two: one.astype(jnp.float32) + two.astype(jnp.float32)
    text = add(d_pair[:, half:], other[:, half:])
    out = []
    for at in range(len(steps) + 1):
        rows = slice(at * image_rows, (at + 1) * image_rows)
        sums = add(d_mine[:, rows], other[:, rows])
        if len(steps) == 3 and at in (1, 2):
            halves = text[2 - at]
            halves = jnp.stack([halves[: PROMPT // 2], halves[PROMPT // 2 :]])
            sums = jnp.concatenate([sums, halves], axis=1)
        out.append(sums.astype(jnp.bfloat16) if at else sums)
    return out + [text[0], text[1]]


def add_sums(image_rows, own, keys_text, values_text, *parts):
    texts = [values_text, keys_text]
    for at, part in enumerate(parts):
        own = own + part[:, :image_rows].astype(jnp.float32)
        if part.shape[1] > image_rows:
            rows = part[:, image_rows:].astype(jnp.float32)
            texts[at] = texts[at] + jnp.concatenate([rows[0], rows[1]], axis=0)
    return [part.astype(jnp.bfloat16) for part in (own, texts[1], texts[0])]


def spread_text(text, late_shard):
    for stride in text_strides(lax.axis_size("ctx"), late_shard):
        text = text + xor_permute(text, stride)
    return text, xor_permute(text, 1)


def collect_text(text, late_shard):
    for stride in reversed(text_strides(lax.axis_size("ctx"), late_shard)):
        moved = xor_permute(text.astype(jnp.bfloat16), stride)
        text = text.astype(jnp.float32) + moved.astype(jnp.float32)
    return text.astype(jnp.bfloat16)


def halo_cuts(tok_rows, halo):
    cuts = []
    left = halo
    while left > 0:
        cuts.append(min(left, tok_rows))
        left -= cuts[-1]
    return cuts


def halo_rows(tail, halo, tok_rows):
    ctx_size = lax.axis_size("ctx")
    parts = []
    for step, count in enumerate(halo_cuts(tok_rows, halo), 1):
        pairs = [(at, at + step) for at in range(ctx_size - step)]
        rows = tail if count == tail.shape[1] else tail[:, tail.shape[1] - count :]
        parts.insert(0, lax.ppermute(rows, "ctx", pairs))
    return jnp.concatenate(parts, axis=1) if len(parts) > 1 else parts[0]


def halo_parts(d_halo, tok_rows):
    ctx_size = lax.axis_size("ctx")
    cuts = halo_cuts(tok_rows, d_halo.shape[1])
    parts = []
    end = d_halo.shape[1]
    for step, count in enumerate(cuts, 1):
        rows = d_halo if len(cuts) == 1 else d_halo[:, end - count : end]
        parts.append((rows, [(at + step, at) for at in range(ctx_size - step)]))
        end -= count
    return parts


def last_kernel(part_count, vis_ref, dkv_ref, down_ref, *refs):
    text_refs, refs = refs[:4], refs[4:]
    part_refs = refs[:part_count]
    *dq_refs, image_ref, kv_ref = refs[part_count:]
    here = lax.axis_index("ctx")
    tok_rows = down_ref.shape[1]
    at = 0
    for dq_ref in dq_refs:
        image_ref[0, at : at + dq_ref.shape[0], :Q_WIDTH] = dq_ref[...]
        at += dq_ref.shape[0]
    image_ref[0, :, Q_WIDTH : Q_WIDTH + KV_WIDTH] = dkv_ref[0]
    image_ref[0, :, Q_WIDTH + KV_WIDTH :] = dkv_ref[1]
    at = lax.broadcasted_iota(jnp.int32, (PROMPT, KV_WIDTH), 0)
    ahead = jnp.where(here == 0, 1, 0)
    behind = jnp.where(here == VIS // tok_rows, 1, 0)
    kept = jnp.where(at < vis_ref[0], ahead, behind) == 1
    for part in range(2):
        text = text_refs[part][...].astype(jnp.float32)
        text = text + text_refs[2 + part][...].astype(jnp.float32)
        text = jnp.where(kept, text, 0.0)
        sums = down_ref[part] + jnp.concatenate(
            [text, jnp.zeros((tok_rows - PROMPT, KV_WIDTH), jnp.float32)], axis=0
        )
        for part_ref in part_refs:
            back = part_ref[part].astype(jnp.float32)
            if back.shape[0] < tok_rows:
                missing = jnp.zeros((tok_rows - back.shape[0], KV_WIDTH), jnp.float32)
                back = jnp.concatenate([missing, back], axis=0)
            sums = sums + back
        kv_ref[0, part] = sums.astype(jnp.bfloat16)


def last_arrays(vis_start, image_dq, image_dkv, d_own_kv, texts, parts):
    rows = image_dkv.shape[1]
    smem = pl.BlockSpec(memory_space=pltpu.SMEM)
    vmem = pl.BlockSpec(memory_space=pltpu.VMEM)
    return pl.pallas_call(
        functools.partial(last_kernel, len(parts)),
        in_specs=[smem] + [vmem] * (6 + len(parts) + len(image_dq)),
        out_specs=[vmem, vmem],
        out_shape=[
            jax.ShapeDtypeStruct((1, rows, Q_WIDTH + 2 * KV_WIDTH), jnp.bfloat16),
            jax.ShapeDtypeStruct((1,) + d_own_kv.shape, jnp.bfloat16),
        ],
    )(vis_start, image_dkv, d_own_kv, *texts, *parts, *image_dq)


def gather_queries(image_q):
    every = lax.all_gather(image_q, "rollout", axis=0)
    missing = IMAGE_BLOCK - every.shape[1]
    return jnp.pad(every, ((0, 0), (0, missing), (0, 0))) if missing else every


def per_device(queries, keys_values, image_rows, cotangent, seq_image, vis_start, comp_lengths):
    tok_rows = queries.shape[1]
    image_count = image_rows.shape[1]
    ctx_size = lax.axis_size("ctx")
    seq_len = tok_rows * ctx_size
    late_shard = VIS // tok_rows
    longest = 4 * (seq_len - PREFIX) // (3 * NCOMP)
    halo = -(-(longest - 1) // 64) * 64
    q_own, d_own = queries[0], cotangent[0]

    number, image_kv, image_q, text, tail = first_arrays(
        seq_image, vis_start, image_rows, keys_values, halo
    )
    every_q = gather_queries(image_q)
    image_kv, swapped = route(image_kv, number, False, [(text, xor_pairs(late_shard))])
    image_kv, d_later = lax.optimization_barrier((image_kv, d_own))
    windows, rounds, (*masks, text) = second_arrays(
        vis_start, comp_lengths, d_later, image_kv, text, swapped, halo
    )
    blocks, texts = gather_prefix(image_kv, text, late_shard)
    windows = image_windows(windows, rounds)
    halo_kv = halo_rows(tail, halo, tok_rows)

    grad_q, *d_image_q, d_mine, d_pair, d_halo, d_own_kv = attend(
        number,
        masks,
        q_own,
        d_own,
        every_q,
        halo_kv,
        keys_values,
        blocks,
        [] if ctx_size == 8 else texts,
        windows,
    )

    d_image_q = [
        half[: image_count - at * IMAGE_HALF]
        for at, half in enumerate(d_image_q)
        if at * IMAGE_HALF < image_count
    ]
    image_dq, other, *halo_back = route(
        d_image_q[0], number, True, [(d_pair, xor_pairs(1))] + halo_parts(d_halo, tok_rows)
    )
    image_dq = [image_dq]
    steps = chip_steps(ctx_size)
    own, *sent, keys_text, values_text = on_device(
        functools.partial(split_sums, image_count, steps), d_mine, d_pair, other
    )
    beside = [(rows, xor_pairs(step)) for rows, step in zip(sent, steps)]
    if len(d_image_q) > 1:
        second, *moved = route(d_image_q[1], number, True, beside)
        image_dq.append(second)
    else:
        moved = [lax.ppermute(rows, "ctx", pairs) for rows, pairs in beside]
    sums, keys_text, values_text = on_device(
        functools.partial(add_sums, image_count), own, keys_text, values_text, *moved
    )
    if ctx_size != 8:
        keys_text = collect_text(keys_text, late_shard)
        values_text = collect_text(values_text, late_shard)
    keys_step = late_shard
    values_step = 4 if ctx_size == 8 else late_shard
    image_dkv, *other_texts = route(
        sums,
        number,
        True,
        [(keys_text, xor_pairs(keys_step)), (values_text, xor_pairs(values_step))],
    )
    grad_image, grad_kv = last_arrays(
        vis_start,
        image_dq,
        image_dkv,
        d_own_kv,
        [keys_text, values_text, *other_texts],
        halo_back,
    )
    return (grad_q[None], grad_kv, grad_image)


def solution(mesh):
    placed = (
        P("rollout", "ctx", None),
        P("rollout", None, "ctx", None),
        P("rollout", "ctx", None),
        P("rollout", "ctx", None),
        P(),
        P("rollout"),
        P("rollout", None),
    )
    return jax.shard_map(
        per_device,
        mesh=mesh,
        in_specs=placed,
        out_specs=(
            P("rollout", "ctx", None),
            P("rollout", None, "ctx", None),
            P("rollout", "ctx", None),
        ),
        check_vma=False,
    )
```

```python
import functools
import itertools
import math

import jax
import jax.numpy as jnp
from jax import lax
from jax.experimental import pallas as pl
from jax.experimental.pallas import tpu as pltpu
from jax.sharding import PartitionSpec as P

HEADS = 32
KV_HEADS = 8
HEAD_DIM = 128
VIS = 256
PROMPT = 64
NCOMP = 16

RATIO = HEADS // KV_HEADS
PREFIX = VIS + PROMPT
Q_WIDTH = HEADS * HEAD_DIM
KV_WIDTH = KV_HEADS * HEAD_DIM
GROUP_WIDTH = RATIO * HEAD_DIM
IMAGE_BLOCK = 32
IMAGE_HALF = IMAGE_BLOCK // 2
KEY_CHUNK = 64
HIDDEN = -1e30
SCORE_SCALE = 1.0 / math.sqrt(HEAD_DIM)


def dot_nt(left, right):
    return lax.dot_general(
        left, right, (((1,), (1,)), ((), ())), preferred_element_type=jnp.float32
    )


def dot_nn(left, right):
    return lax.dot_general(
        left, right, (((1,), (0,)), ((), ())), preferred_element_type=jnp.float32
    )


def dot_tn(left, right):
    return lax.dot_general(
        left, right, (((0,), (0,)), ((), ())), preferred_element_type=jnp.float32
    )


def send_first(halo, seq_ref, vis_ref, image_ref, kv_ref, number_ref, *out_refs):
    ikv_ref, iq_ref, text_ref, tail_ref = out_refs
    groups = seq_ref.shape[0]
    group = lax.axis_index("rollout")
    here = lax.axis_index("ctx")
    images = [seq_ref[at] for at in range(groups)]
    number = jnp.int32(0)
    if groups == 4:
        for at, weight in enumerate((6, 2, 1)):
            for later in range(at + 1, groups):
                number = number + jnp.where(images[later] < images[at], weight, 0)
    place = jnp.int32(0)
    user = jnp.int32(0)
    for at in range(groups):
        place = place + jnp.where(group == at, images[at], 0)
        user = user + jnp.where(images[at] == group, at, 0)
    number_ref[0] = number
    number_ref[1] = place
    number_ref[2] = user
    iq_ref[...] = image_ref[0, :, :Q_WIDTH]
    ikv_ref[0] = image_ref[0, :, Q_WIDTH : Q_WIDTH + KV_WIDTH]
    ikv_ref[1] = image_ref[0, :, Q_WIDTH + KV_WIDTH :]
    tok_rows = kv_ref.shape[2]
    late_shard = VIS // tok_rows
    at = lax.broadcasted_iota(jnp.int32, (PROMPT, KV_WIDTH), 0)
    ahead = jnp.where(here == 0, 1, 0)
    behind = jnp.where(here == late_shard, 1, 0)
    kept = jnp.where(at < vis_ref[0], ahead, behind) == 1
    for part in range(2):
        rows = kv_ref[0, part, :PROMPT].astype(jnp.float32)
        text_ref[part] = jnp.where(kept, rows, 0.0).astype(jnp.bfloat16)
        tail_ref[part] = kv_ref[0, part, tok_rows - halo :]


def segments(positions, length_ref):
    end = jnp.int32(PREFIX)
    segment = jnp.where(positions < PREFIX, 0, 1)
    for at in range(NCOMP):
        end = end + length_ref[0, at]
        segment = segment + jnp.where(positions >= end, 1, 0)
    return segment


def hide(visible):
    return jnp.where(visible, 0.0, HIDDEN)


def first_kernel(halo, tail, seq_ref, vis_ref, length_ref, *refs):
    image_in_ref, kv_ref, d_ref, *out_refs = refs
    first_refs, window_ref, mask_refs = out_refs[:5], out_refs[5], out_refs[6:]
    near_ref, whole_ref, image_ref = mask_refs
    here = lax.axis_index("ctx")
    ctx_size = lax.axis_size("ctx")
    tok_rows = d_ref.shape[0]
    image_rows = image_in_ref.shape[1]
    row = lax.broadcasted_iota(jnp.int32, (VIS, tok_rows), 0)
    column = lax.broadcasted_iota(jnp.int32, (VIS, tok_rows), 1)
    pick = column == row + (vis_ref[0] - tok_rows * here)
    pick = jnp.where(pick, 1.0, 0.0).astype(jnp.bfloat16)
    window_ref[...] = dot_nn(pick, d_ref[...]).astype(jnp.bfloat16)

    @pl.when(pl.program_id(0) == 0)
    def _():
        send_first(tail, seq_ref, vis_ref, image_in_ref, kv_ref, *first_refs)
        vis = vis_ref[0]
        own_at = lax.broadcasted_iota(jnp.int32, (8, tok_rows), 1) + here * tok_rows
        own_segment = segments(own_at, length_ref)[:1]
        placeholder = (own_at >= vis) & (own_at < vis + VIS)
        own_row = jnp.where(placeholder, -1, own_at)
        whole_ref[...] = hide(own_row >= vis + VIS).astype(jnp.float32)
        own_row = own_row[:1]
        image_at = lax.broadcasted_iota(jnp.int32, (1, RATIO * IMAGE_BLOCK), 1) % IMAGE_BLOCK
        image_row = jnp.where(image_at < image_rows, vis + here * image_rows + image_at, -1)
        text_at = lax.broadcasted_iota(jnp.int32, (PROMPT, tok_rows), 0)
        text_at = text_at + jnp.where(text_at < vis, 0, VIS)
        near_ref[:PROMPT] = hide(text_at <= own_row)
        near_at = lax.broadcasted_iota(jnp.int32, (halo + tok_rows, tok_rows), 0)
        near_at = near_at + (here * tok_rows - halo)
        sees = (near_at <= own_row) & (near_at >= PREFIX)
        sees = sees & (segments(near_at, length_ref) == own_segment)
        near_ref[PROMPT:] = hide(sees)
        at = 0
        for core in range(2):
            for step in range(0, ctx_size, 2):
                begin = (here ^ (step + core)) * image_rows + vis
                shape = (image_rows, RATIO * IMAGE_BLOCK)
                block_at = lax.broadcasted_iota(jnp.int32, shape, 0) + begin
                image_ref[at : at + image_rows] = hide(block_at <= image_row)
                at += image_rows
        image_ref[VIS:] = hide(text_at <= image_row)


def first_arrays(seq_image, vis_start, lengths, image_rows, keys_values, cotangent, halo):
    rows = image_rows.shape[1]
    tok_rows, width = cotangent.shape
    tail = min(halo, tok_rows)
    block = 2048
    spec = pl.BlockSpec
    smem = spec(memory_space=pltpu.SMEM)
    lanes = RATIO * IMAGE_BLOCK
    near = PROMPT + halo + tok_rows
    whole = lambda *shape: spec(shape, lambda at: (0,) * len(shape))
    kept = [
        ((2, rows, KV_WIDTH), jnp.bfloat16),
        ((rows, Q_WIDTH), jnp.bfloat16),
        ((2, PROMPT, KV_WIDTH), jnp.bfloat16),
        ((2, tail, KV_WIDTH), jnp.bfloat16),
    ]
    masks = [
        ((near, tok_rows), jnp.float32),
        ((8, tok_rows), jnp.float32),
        ((PREFIX, lanes), jnp.float32),
    ]
    number, *out = pl.pallas_call(
        functools.partial(first_kernel, halo, tail),
        grid=(width // block,),
        in_specs=[
            smem,
            smem,
            smem,
            whole(*image_rows.shape),
            whole(*keys_values.shape),
            spec((tok_rows, block), lambda at: (0, at)),
        ],
        out_specs=[smem]
        + [whole(*shape) for shape, _ in kept]
        + [spec((VIS, block), lambda at: (0, at))]
        + [whole(*shape) for shape, _ in masks],
        out_shape=[jax.ShapeDtypeStruct((3,), jnp.int32)]
        + [jax.ShapeDtypeStruct(*pair) for pair in kept]
        + [jax.ShapeDtypeStruct((VIS, width), jnp.bfloat16)]
        + [jax.ShapeDtypeStruct(*pair) for pair in masks],
    )(seq_image, vis_start, lengths, image_rows, keys_values, cotangent)
    return number, out[:4], out[4], out[5:]


def first_products(parts, q_rows, d_rows):
    return [(dot_nt(keys, q_rows), dot_nt(values, d_rows)) for keys, values, _ in parts]


def chunks_of(rows):
    return [rows[at : at + KEY_CHUNK] for at in range(0, rows.shape[0], KEY_CHUNK)]


def fold_rows(rows, combine):
    folded = rows[:8]
    for at in range(8, rows.shape[0], 8):
        folded = combine(folded, rows[at : at + 8])
    return folded


def rows_backward(parts, products):
    scale = SCORE_SCALE * math.log2(math.e)
    scores, tops = [], []
    for (keys, values, bias), (raw, _) in zip(parts, products):
        one_row = bias.shape[0] == 1
        top = None
        for at, chunk in enumerate(chunks_of(raw)):
            chunk = chunk * scale
            if not one_row:
                chunk = chunk + bias[at * KEY_CHUNK : (at + 1) * KEY_CHUNK]
            scores.append((chunk, bias if one_row else None))
            folded = fold_rows(chunk, jnp.maximum)
            top = folded if top is None else jnp.maximum(top, folded)
        top = jnp.max(top, axis=0, keepdims=True)
        tops.append(top + bias if one_row else top)
    top = functools.reduce(jnp.maximum, tops)
    d_weights = [chunk for _, product in products for chunk in chunks_of(product)]
    total = mix = None
    kept = []
    for (chunk, bias), d_chunk in zip(scores, d_weights):
        terms = jnp.exp2(chunk + ((bias if bias is not None else 0.0) - top))
        folded = fold_rows(terms, jnp.add)
        total = folded if total is None else total + folded
        folded = fold_rows(terms * d_chunk, jnp.add)
        mix = folded if mix is None else mix + folded
        kept.append(terms)
    total = jnp.sum(total, axis=0, keepdims=True)
    mix = jnp.sum(mix, axis=0, keepdims=True)
    inverse = jnp.where(top > 0.5 * HIDDEN, 1.0 / total, 0.0)
    delta = mix * inverse
    weights, d_scores = [], []
    for terms, d_chunk in zip(kept, d_weights):
        chunk = terms * inverse
        weights.append(chunk.astype(jnp.bfloat16))
        d_scores.append((chunk * (d_chunk - delta)).astype(jnp.bfloat16))
    outcome = []
    for raw, _ in products:
        count = raw.shape[0] // KEY_CHUNK
        outcome.append(
            (jnp.concatenate(weights[:count], axis=0), jnp.concatenate(d_scores[:count], axis=0))
        )
        weights, d_scores = weights[count:], d_scores[count:]
    return outcome


def total_of(values):
    if len(values) == 1:
        return values[0]
    return sum(value.astype(jnp.float32) for value in values).astype(jnp.bfloat16)


def attend_kernel(
    block_rows,
    block_count,
    text_count,
    window_count,
    heads,
    halo,
    own,
    number_ref,
    near_ref,
    whole_ref,
    image_bias_ref,
    q_ref,
    d_ref,
    iq_ref,
    halo_ref,
    own_ref,
    *refs,
):
    block_refs, refs = refs[:block_count], refs[block_count:]
    text_refs, refs = refs[:text_count], refs[text_count:]
    window_refs, refs = refs[:window_count], refs[window_count:]
    dq_ref, *diq_refs, dmine_ref, dpair_ref, dhalo_ref, down_ref = refs
    text_refs = text_refs or [ref for ref in block_refs if ref.shape[1] > block_rows]
    near_bias = jnp.concatenate([near_ref[...]] * 2, axis=1)
    whole_bias = jnp.concatenate([whole_ref[:1]] * 2, axis=1)
    image_cotangent = total_of([ref[...] for ref in window_refs])
    image_queries = iq_ref[number_ref[1]]
    states = []
    units = []
    for head in range(heads):
        lanes = slice(head * HEAD_DIM, (head + 1) * HEAD_DIM)
        spans = [
            slice((head * RATIO + at) * HEAD_DIM, (head * RATIO + at + 1) * HEAD_DIM)
            for at in range(RATIO)
        ]
        visual, text, near = [], [], []
        for part in range(2):
            visual.append(
                jnp.concatenate([ref[part, :block_rows, lanes] for ref in block_refs], axis=0)
            )
            text.append(total_of([ref[part, -PROMPT:, lanes] for ref in text_refs]))
            near.append(
                jnp.concatenate(
                    [text[part], halo_ref[part, :, lanes], own_ref[0, part, :, lanes]], axis=0
                )
            )
        states.append((lanes, jnp.concatenate([visual[0], near[0]], axis=0).T, {}))
        own_parts = [(visual[0], visual[1], whole_bias), (near[0], near[1], near_bias)]
        for first in range(0, RATIO, 2):
            units.append((head, own_parts, q_ref, d_ref, spans[first : first + 2]))
        image_parts = [
            (visual[0], visual[1], image_bias_ref[:VIS]),
            (text[0], text[1], image_bias_ref[VIS:]),
        ]
        units.append((head, image_parts, image_queries, image_cotangent, spans))

    def begin(unit):
        _, parts, queries, cotangents, unit_spans = unit
        q_rows = jnp.concatenate([queries[:, span] for span in unit_spans], axis=0)
        d_rows = jnp.concatenate([cotangents[:, span] for span in unit_spans], axis=0)
        return q_rows, d_rows, first_products(parts, q_rows, d_rows)

    def finish(unit, begun):
        head, parts, _, _, unit_spans = unit
        lanes, keys_across, sums = states[head]
        q_rows, d_rows, products = begun
        outcome = rows_backward(parts, products)
        d_scores = jnp.concatenate([part[1] for part in outcome], axis=0)
        dq = dot_nn(keys_across[:, : d_scores.shape[0]], d_scores) * SCORE_SCALE
        dq = dq.astype(jnp.bfloat16).T
        rows = dq.shape[0] // len(unit_spans)
        for at, span in enumerate(unit_spans):
            if len(unit_spans) == 2:
                dq_ref[:, span] = dq[at * rows : (at + 1) * rows]
            else:
                for half, out_ref in enumerate(diq_refs):
                    place = at * rows + half * IMAGE_HALF
                    out_ref[:, span] = dq[place : place + IMAGE_HALF]
        for at, (weights, d_part) in enumerate(outcome):
            for kind, rows in ((0, dot_nn(d_part, q_rows)), (1, dot_nn(weights, d_rows))):
                count = rows.shape[0]
                earlier = sums.get((kind, at))
                if earlier is not None and count < earlier.shape[0]:
                    rows = jnp.concatenate([earlier[:count] + rows, earlier[count:]], axis=0)
                elif earlier is not None:
                    rows = earlier + rows
                sums[kind, at] = rows
        if len(unit_spans) == 2:
            return
        for part, scale in ((0, SCORE_SCALE), (1, 1.0)):
            of_visual = (sums[part, 0] * scale).astype(jnp.bfloat16)
            rest = sums[part, 1] * scale
            dmine_ref[part, :, lanes] = of_visual[: VIS // 2]
            dpair_ref[part, : VIS // 2, lanes] = of_visual[VIS // 2 :]
            dpair_ref[part, VIS // 2 :, lanes] = rest[:PROMPT].astype(jnp.bfloat16)
            dhalo_ref[part, :, lanes] = rest[PROMPT : PROMPT + halo].astype(jnp.bfloat16)
            down_ref[part, :, lanes] = rest[PROMPT + halo :]

    begun = begin(units[0])
    for at, unit in enumerate(units):
        later = begin(units[at + 1]) if at + 1 < len(units) else None
        finish(unit, begun)
        begun = later


def attend(
    number, masks, queries, cotangent, every_q, halo_kv, own_kv, blocks, texts, windows
):
    heads = 2
    near_bias, whole_bias, image_bias = masks
    sources = range(windows.shape[0] // IMAGE_BLOCK)[: (VIS + PROMPT - 1) // queries.shape[0] + 1]
    own = queries.shape[0]
    halo = halo_kv.shape[1]
    groups = every_q.shape[0]
    columns = PREFIX + halo + own
    products = RATIO * (own * columns + IMAGE_BLOCK * PREFIX) * KV_HEADS
    spec = pl.BlockSpec
    kv_spec = lambda rows: spec((2, rows, heads * HEAD_DIM), lambda at: (0, 0, at))
    q_spec = lambda rows: spec((rows, heads * GROUP_WIDTH), lambda at: (0, at))
    whole = lambda rows: spec((rows, 128), lambda at: (0, 0))
    return pl.pallas_call(
        functools.partial(
            attend_kernel,
            VIS // len(blocks),
            len(blocks),
            len(texts),
            len(sources),
            heads,
            halo,
            own,
        ),
        grid=(KV_HEADS // heads,),
        in_specs=[
            spec(memory_space=pltpu.SMEM),
            whole(columns - VIS),
            whole(8),
            whole(PREFIX),
            q_spec(own),
            q_spec(own),
            spec((groups, IMAGE_BLOCK, heads * GROUP_WIDTH), lambda at: (0, 0, at)),
            kv_spec(halo),
            spec((1, 2, own, heads * HEAD_DIM), lambda at: (0, 0, 0, at)),
        ]
        + [kv_spec(block.shape[1]) for block in [*blocks, *texts]]
        + [
            spec((IMAGE_BLOCK, heads * GROUP_WIDTH), lambda at, source=source: (source, at))
            for source in sources
        ],
        out_specs=[
            q_spec(own),
            q_spec(IMAGE_HALF),
            q_spec(IMAGE_HALF),
            kv_spec(VIS // 2),
            kv_spec(VIS // 2 + PROMPT),
            kv_spec(halo),
            kv_spec(own),
        ],
        out_shape=[
            jax.ShapeDtypeStruct((own, Q_WIDTH), jnp.bfloat16),
            jax.ShapeDtypeStruct((IMAGE_HALF, Q_WIDTH), jnp.bfloat16),
            jax.ShapeDtypeStruct((IMAGE_HALF, Q_WIDTH), jnp.bfloat16),
            jax.ShapeDtypeStruct((2, VIS // 2, KV_WIDTH), jnp.bfloat16),
            jax.ShapeDtypeStruct((2, VIS // 2 + PROMPT, KV_WIDTH), jnp.bfloat16),
            jax.ShapeDtypeStruct((2, halo, KV_WIDTH), jnp.bfloat16),
            jax.ShapeDtypeStruct((2, own, KV_WIDTH), jnp.float32),
        ],
        cost_estimate=pl.CostEstimate(
            flops=10 * products * HEAD_DIM,
            bytes_accessed=12 * 1024 * 1024,
            transcendentals=products,
        ),
    )(
        number,
        near_bias,
        whole_bias,
        image_bias,
        queries,
        cotangent,
        every_q,
        halo_kv,
        own_kv,
        *blocks,
        *texts,
        *[windows for _ in sources],
    )


def route(rows, number, back, beside=()):
    groups = lax.axis_size("rollout")
    arrays = [array for array, _ in beside]

    def move_beside(arrays):
        return [lax.ppermute(array, "ctx", pairs) for array, (_, pairs) in zip(arrays, beside)]

    if groups != 4:
        every = lax.all_gather(rows, "rollout", axis=0)
        picked = lax.dynamic_index_in_dim(every, number[2 if back else 1], 0, keepdims=False)
        return [picked] + move_beside(arrays)

    def branch(images):
        pairs = [(g, i) if back else (i, g) for g, i in enumerate(images)]
        return lambda rows, arrays: [lax.ppermute(rows, "rollout", pairs)] + move_beside(arrays)

    orders = itertools.permutations(range(groups))
    return lax.switch(number[0], [branch(images) for images in orders], rows, arrays)


def xor_pairs(step):
    return [(at, at ^ step) for at in range(lax.axis_size("ctx"))]


def xor_permute(rows, step):
    return lax.ppermute(rows, "ctx", xor_pairs(step))


def on_device(function, *arrays):
    if lax.axis_size("ctx") != 8:
        return function(*arrays)
    shapes = jax.eval_shape(function, *arrays)

    def kernel(*refs):
        for out_ref, value in zip(
            refs[len(arrays) :], function(*[ref[...] for ref in refs[: len(arrays)]])
        ):
            out_ref[...] = value

    def spec(array):
        *rows, width = array.shape
        return pl.BlockSpec((*rows, width // 2), lambda at: (0,) * len(rows) + (at,))

    return pl.pallas_call(
        kernel,
        grid=(2,),
        in_specs=[spec(array) for array in arrays],
        out_specs=[spec(shape) for shape in shapes],
        out_shape=[jax.ShapeDtypeStruct(shape.shape, shape.dtype) for shape in shapes],
        cost_estimate=pl.CostEstimate(flops=1, bytes_accessed=1, transcendentals=0),
    )(*arrays)


def text_strides(ctx_size, late_shard):
    strides = [1 << at for at in range(1, ctx_size.bit_length() - 1)]
    return [stride for stride in reversed(strides) if stride != late_shard]


def chip_steps(ctx_size):
    return list(range(2, ctx_size, 2))


def join_text(image_kv, text, received):
    return [jnp.concatenate([image_kv, add_text(text, received)], axis=1)]


def add_text(text, received):
    return (text.astype(jnp.float32) + received.astype(jnp.float32)).astype(jnp.bfloat16)


def gather_prefix(image_kv, text, received, late_shard):
    ctx_size = lax.axis_size("ctx")
    steps = chip_steps(ctx_size)
    if ctx_size == 8:
        (text,) = on_device(join_text, image_kv, text, received)
        mine = [text, xor_permute(image_kv, 2), xor_permute(text, 4), xor_permute(image_kv, 6)]
        blocks = mine + [xor_permute(block, 1) for block in mine]
        return blocks, [blocks[at] for at in (0, 2, 4, 6)]
    mine = jnp.concatenate(
        [image_kv] + [xor_permute(image_kv, step) for step in steps], axis=1
    )
    return [mine, xor_permute(mine, 1)], list(spread_text(add_text(text, received), late_shard))


def split_sums(image_rows, steps, d_mine, d_pair, other):
    half = VIS // 2
    add = lambda one, two: one.astype(jnp.float32) + two.astype(jnp.float32)
    text = add(d_pair[:, half:], other[:, half:])
    out = []
    for at in range(len(steps) + 1):
        rows = slice(at * image_rows, (at + 1) * image_rows)
        sums = add(d_mine[:, rows], other[:, rows])
        if len(steps) == 3 and at in (1, 2):
            halves = text[2 - at]
            halves = jnp.stack([halves[: PROMPT // 2], halves[PROMPT // 2 :]])
            sums = jnp.concatenate([sums, halves], axis=1)
        out.append(sums.astype(jnp.bfloat16) if at else sums)
    return out + [text[0], text[1]]


def add_sums(image_rows, own, keys_text, values_text, *parts):
    texts = [values_text, keys_text]
    for at, part in enumerate(parts):
        own = own + part[:, :image_rows].astype(jnp.float32)
        if part.shape[1] > image_rows:
            rows = part[:, image_rows:].astype(jnp.float32)
            texts[at] = texts[at] + jnp.concatenate([rows[0], rows[1]], axis=0)
    return [part.astype(jnp.bfloat16) for part in (own, texts[1], texts[0])]


def spread_text(text, late_shard):
    for stride in text_strides(lax.axis_size("ctx"), late_shard):
        text = text + xor_permute(text, stride)
    return text, xor_permute(text, 1)


def collect_text(text, late_shard):
    for stride in reversed(text_strides(lax.axis_size("ctx"), late_shard)):
        moved = xor_permute(text.astype(jnp.bfloat16), stride)
        text = text.astype(jnp.float32) + moved.astype(jnp.float32)
    return text.astype(jnp.bfloat16)


def halo_cuts(tok_rows, halo):
    cuts = []
    left = halo
    while left > 0:
        cuts.append(min(left, tok_rows))
        left -= cuts[-1]
    return cuts


def halo_rows(tail, halo, tok_rows):
    ctx_size = lax.axis_size("ctx")
    parts = []
    for step, count in enumerate(halo_cuts(tok_rows, halo), 1):
        pairs = [(at, at + step) for at in range(ctx_size - step)]
        rows = tail if count == tail.shape[1] else tail[:, tail.shape[1] - count :]
        parts.insert(0, lax.ppermute(rows, "ctx", pairs))
    return jnp.concatenate(parts, axis=1) if len(parts) > 1 else parts[0]


def halo_parts(d_halo, tok_rows):
    ctx_size = lax.axis_size("ctx")
    cuts = halo_cuts(tok_rows, d_halo.shape[1])
    parts = []
    end = d_halo.shape[1]
    for step, count in enumerate(cuts, 1):
        rows = d_halo if len(cuts) == 1 else d_halo[:, end - count : end]
        parts.append((rows, [(at + step, at) for at in range(ctx_size - step)]))
        end -= count
    return parts


def last_kernel(part_count, vis_ref, dkv_ref, down_ref, *refs):
    text_refs, refs = refs[:4], refs[4:]
    part_refs = refs[:part_count]
    *dq_refs, image_ref, kv_ref = refs[part_count:]
    here = lax.axis_index("ctx")
    tok_rows = down_ref.shape[1]
    at = 0
    for dq_ref in dq_refs:
        image_ref[0, at : at + dq_ref.shape[0], :Q_WIDTH] = dq_ref[...]
        at += dq_ref.shape[0]
    image_ref[0, :, Q_WIDTH : Q_WIDTH + KV_WIDTH] = dkv_ref[0]
    image_ref[0, :, Q_WIDTH + KV_WIDTH :] = dkv_ref[1]
    at = lax.broadcasted_iota(jnp.int32, (PROMPT, KV_WIDTH), 0)
    ahead = jnp.where(here == 0, 1, 0)
    behind = jnp.where(here == VIS // tok_rows, 1, 0)
    kept = jnp.where(at < vis_ref[0], ahead, behind) == 1
    for part in range(2):
        text = text_refs[part][...].astype(jnp.float32)
        text = text + text_refs[2 + part][...].astype(jnp.float32)
        text = jnp.where(kept, text, 0.0)
        sums = down_ref[part] + jnp.concatenate(
            [text, jnp.zeros((tok_rows - PROMPT, KV_WIDTH), jnp.float32)], axis=0
        )
        for part_ref in part_refs:
            back = part_ref[part].astype(jnp.float32)
            if back.shape[0] < tok_rows:
                missing = jnp.zeros((tok_rows - back.shape[0], KV_WIDTH), jnp.float32)
                back = jnp.concatenate([missing, back], axis=0)
            sums = sums + back
        kv_ref[0, part] = sums.astype(jnp.bfloat16)


def last_arrays(vis_start, image_dq, image_dkv, d_own_kv, texts, parts):
    rows = image_dkv.shape[1]
    smem = pl.BlockSpec(memory_space=pltpu.SMEM)
    vmem = pl.BlockSpec(memory_space=pltpu.VMEM)
    return pl.pallas_call(
        functools.partial(last_kernel, len(parts)),
        in_specs=[smem] + [vmem] * (6 + len(parts) + len(image_dq)),
        out_specs=[vmem, vmem],
        out_shape=[
            jax.ShapeDtypeStruct((1, rows, Q_WIDTH + 2 * KV_WIDTH), jnp.bfloat16),
            jax.ShapeDtypeStruct((1,) + d_own_kv.shape, jnp.bfloat16),
        ],
    )(vis_start, image_dkv, d_own_kv, *texts, *parts, *image_dq)


def gather_queries(image_q):
    every = lax.all_gather(image_q, "rollout", axis=0)
    missing = IMAGE_BLOCK - every.shape[1]
    return jnp.pad(every, ((0, 0), (0, missing), (0, 0))) if missing else every


def per_device(queries, keys_values, image_rows, cotangent, seq_image, vis_start, comp_lengths):
    tok_rows = queries.shape[1]
    image_count = image_rows.shape[1]
    ctx_size = lax.axis_size("ctx")
    seq_len = tok_rows * ctx_size
    late_shard = VIS // tok_rows
    longest = 4 * (seq_len - PREFIX) // (3 * NCOMP)
    halo = -(-(longest - 1) // 64) * 64
    q_own, d_own = queries[0], cotangent[0]

    number, (image_kv, image_q, text, tail), windows, masks = first_arrays(
        seq_image, vis_start, comp_lengths, image_rows, keys_values, d_own, halo
    )
    windows = lax.all_to_all(windows, "ctx", split_axis=0, concat_axis=0, tiled=True)
    if image_count < IMAGE_BLOCK:
        windows = windows.reshape(ctx_size, image_count, -1)[: (VIS + PROMPT - 1) // tok_rows + 1]
        windows = jnp.sum(windows.astype(jnp.float32), axis=0).astype(jnp.bfloat16)
        windows = jnp.pad(windows, ((0, IMAGE_BLOCK - image_count), (0, 0)))
    every_q = gather_queries(image_q)
    image_kv, received = route(image_kv, number, False, [(text, xor_pairs(late_shard))])
    blocks, texts = gather_prefix(image_kv, text, received, late_shard)
    halo_kv = halo_rows(tail, halo, tok_rows)

    grad_q, *d_image_q, d_mine, d_pair, d_halo, d_own_kv = attend(
        number,
        masks,
        q_own,
        d_own,
        every_q,
        halo_kv,
        keys_values,
        blocks,
        [] if ctx_size == 8 else texts,
        windows,
    )

    d_image_q = [
        half[: image_count - at * IMAGE_HALF]
        for at, half in enumerate(d_image_q)
        if at * IMAGE_HALF < image_count
    ]
    image_dq, other, *halo_back = route(
        d_image_q[0], number, True, [(d_pair, xor_pairs(1))] + halo_parts(d_halo, tok_rows)
    )
    image_dq = [image_dq]
    steps = chip_steps(ctx_size)
    own, *sent, keys_text, values_text = on_device(
        functools.partial(split_sums, image_count, steps), d_mine, d_pair, other
    )
    beside = [(rows, xor_pairs(step)) for rows, step in zip(sent, steps)]
    if len(d_image_q) > 1:
        second, *moved = route(d_image_q[1], number, True, beside)
        image_dq.append(second)
    else:
        moved = [lax.ppermute(rows, "ctx", pairs) for rows, pairs in beside]
    sums, keys_text, values_text = on_device(
        functools.partial(add_sums, image_count), own, keys_text, values_text, *moved
    )
    if ctx_size != 8:
        keys_text = collect_text(keys_text, late_shard)
        values_text = collect_text(values_text, late_shard)
    keys_step = late_shard
    values_step = 4 if ctx_size == 8 else late_shard
    image_dkv, *other_texts = route(
        sums,
        number,
        True,
        [(keys_text, xor_pairs(keys_step)), (values_text, xor_pairs(values_step))],
    )
    grad_image, grad_kv = last_arrays(
        vis_start,
        image_dq,
        image_dkv,
        d_own_kv,
        [keys_text, values_text, *other_texts],
        halo_back,
    )
    return (grad_q[None], grad_kv, grad_image)


def solution(mesh):
    placed = (
        P("rollout", "ctx", None),
        P("rollout", None, "ctx", None),
        P("rollout", "ctx", None),
        P("rollout", "ctx", None),
        P(),
        P("rollout"),
        P("rollout", None),
    )
    return jax.shard_map(
        per_device,
        mesh=mesh,
        in_specs=placed,
        out_specs=(
            P("rollout", "ctx", None),
            P("rollout", None, "ctx", None),
            P("rollout", "ctx", None),
        ),
        check_vma=False,
    )
```

```python
import functools
import itertools
import math

import jax
import jax.numpy as jnp
from jax import lax
from jax.experimental import pallas as pl
from jax.experimental.pallas import tpu as pltpu
from jax.sharding import PartitionSpec as P

HEADS = 32
KV_HEADS = 8
HEAD_DIM = 128
VIS = 256
PROMPT = 64
NCOMP = 16

RATIO = HEADS // KV_HEADS
PREFIX = VIS + PROMPT
Q_WIDTH = HEADS * HEAD_DIM
KV_WIDTH = KV_HEADS * HEAD_DIM
GROUP_WIDTH = RATIO * HEAD_DIM
IMAGE_BLOCK = 32
IMAGE_HALF = IMAGE_BLOCK // 2
KEY_CHUNK = 64
HIDDEN = -1e30
SCORE_SCALE = 1.0 / math.sqrt(HEAD_DIM)


def dot_nt(left, right):
    return lax.dot_general(
        left, right, (((1,), (1,)), ((), ())), preferred_element_type=jnp.float32
    )


def dot_nn(left, right):
    return lax.dot_general(
        left, right, (((1,), (0,)), ((), ())), preferred_element_type=jnp.float32
    )


def dot_tn(left, right):
    return lax.dot_general(
        left, right, (((0,), (0,)), ((), ())), preferred_element_type=jnp.float32
    )


def first_kernel(halo, seq_ref, vis_ref, image_ref, kv_ref, number_ref, *out_refs):
    ikv_ref, iq_ref, text_ref, tail_ref = out_refs
    groups = seq_ref.shape[0]
    group = lax.axis_index("rollout")
    here = lax.axis_index("ctx")
    images = [seq_ref[at] for at in range(groups)]
    number = jnp.int32(0)
    if groups == 4:
        for at, weight in enumerate((6, 2, 1)):
            for later in range(at + 1, groups):
                number = number + jnp.where(images[later] < images[at], weight, 0)
    place = jnp.int32(0)
    user = jnp.int32(0)
    for at in range(groups):
        place = place + jnp.where(group == at, images[at], 0)
        user = user + jnp.where(images[at] == group, at, 0)
    number_ref[0] = number
    number_ref[1] = place
    number_ref[2] = user
    iq_ref[...] = image_ref[0, :, :Q_WIDTH]
    ikv_ref[0] = image_ref[0, :, Q_WIDTH : Q_WIDTH + KV_WIDTH]
    ikv_ref[1] = image_ref[0, :, Q_WIDTH + KV_WIDTH :]
    tok_rows = kv_ref.shape[2]
    late_shard = VIS // tok_rows
    at = lax.broadcasted_iota(jnp.int32, (PROMPT, KV_WIDTH), 0)
    ahead = jnp.where(here == 0, 1, 0)
    behind = jnp.where(here == late_shard, 1, 0)
    kept = jnp.where(at < vis_ref[0], ahead, behind) == 1
    for part in range(2):
        rows = kv_ref[0, part, :PROMPT].astype(jnp.float32)
        text_ref[part] = jnp.where(kept, rows, 0.0).astype(jnp.bfloat16)
        tail_ref[part] = kv_ref[0, part, tok_rows - halo :]


def first_arrays(seq_image, vis_start, image_rows, keys_values, halo):
    rows = image_rows.shape[1]
    smem = pl.BlockSpec(memory_space=pltpu.SMEM)
    vmem = pl.BlockSpec(memory_space=pltpu.VMEM)
    tail = min(halo, keys_values.shape[2])
    return pl.pallas_call(
        functools.partial(first_kernel, tail),
        in_specs=[smem, smem, vmem, vmem],
        out_specs=[smem, vmem, vmem, vmem, vmem],
        out_shape=[
            jax.ShapeDtypeStruct((3,), jnp.int32),
            jax.ShapeDtypeStruct((2, rows, KV_WIDTH), jnp.bfloat16),
            jax.ShapeDtypeStruct((rows, Q_WIDTH), jnp.bfloat16),
            jax.ShapeDtypeStruct((2, PROMPT, KV_WIDTH), jnp.bfloat16),
            jax.ShapeDtypeStruct((2, tail, KV_WIDTH), jnp.bfloat16),
        ],
    )(seq_image, vis_start, image_rows, keys_values)


def segments(positions, length_ref):
    end = jnp.int32(PREFIX)
    segment = jnp.where(positions < PREFIX, 0, 1)
    for at in range(NCOMP):
        end = end + length_ref[0, at]
        segment = segment + jnp.where(positions >= end, 1, 0)
    return segment


def hide(visible):
    return jnp.where(visible, 0.0, HIDDEN)


def second_kernel(
    rounds, tok_rows, image_rows, halo, vis_ref, length_ref, d_ref, kv_ref, t_ref, r_ref, *out_refs
):
    *window_refs, near_ref, whole_ref, image_ref, text_ref = out_refs
    here = lax.axis_index("ctx")
    ctx_size = lax.axis_size("ctx")
    row = lax.broadcasted_iota(jnp.int32, (IMAGE_BLOCK, tok_rows), 0)
    column = lax.broadcasted_iota(jnp.int32, (IMAGE_BLOCK, tok_rows), 1)
    place = jnp.where(row < image_rows, row, 1 << 20)
    picks = []
    for pairs in [[]] + rounds:
        target = here
        for source, other in pairs:
            target = jnp.where(here == source, other, target)
        begin = vis_ref[0] + image_rows * target - tok_rows * here
        picks.append(jnp.where(column == place + begin, 1.0, 0.0).astype(jnp.bfloat16))
    picked = dot_nn(jnp.concatenate(picks, axis=0), d_ref[...]).astype(jnp.bfloat16)
    for at, window_ref in enumerate(window_refs):
        window_ref[...] = picked[at * IMAGE_BLOCK : (at + 1) * IMAGE_BLOCK]

    @pl.when(pl.program_id(0) == 0)
    def _():
        vis = vis_ref[0]
        text = t_ref[...].astype(jnp.float32) + r_ref[...].astype(jnp.float32)
        if kv_ref.shape[1] == IMAGE_BLOCK:
            text_ref[:, :IMAGE_BLOCK] = kv_ref[...]
        text_ref[:, text_ref.shape[1] - PROMPT :] = text.astype(jnp.bfloat16)
        own_at = lax.broadcasted_iota(jnp.int32, (8, tok_rows), 1) + here * tok_rows
        own_segment = segments(own_at, length_ref)[:1]
        placeholder = (own_at >= vis) & (own_at < vis + VIS)
        own_row = jnp.where(placeholder, -1, own_at)
        whole_ref[...] = hide(own_row >= vis + VIS).astype(jnp.float32)
        own_row = own_row[:1]
        image_at = lax.broadcasted_iota(jnp.int32, (1, RATIO * IMAGE_BLOCK), 1) % IMAGE_BLOCK
        image_row = jnp.where(image_at < image_rows, vis + here * image_rows + image_at, -1)
        text_at = lax.broadcasted_iota(jnp.int32, (PROMPT, tok_rows), 0)
        text_at = text_at + jnp.where(text_at < vis, 0, VIS)
        near_ref[:PROMPT] = hide(text_at <= own_row)
        near_at = lax.broadcasted_iota(jnp.int32, (halo + tok_rows, tok_rows), 0)
        near_at = near_at + (here * tok_rows - halo)
        sees = (near_at <= own_row) & (near_at >= PREFIX)
        sees = sees & (segments(near_at, length_ref) == own_segment)
        near_ref[PROMPT:] = hide(sees)
        at = 0
        for core in range(2):
            for step in range(0, ctx_size, 2):
                begin = (here ^ (step + core)) * image_rows + vis
                shape = (image_rows, RATIO * IMAGE_BLOCK)
                block_at = lax.broadcasted_iota(jnp.int32, shape, 0) + begin
                image_ref[at : at + image_rows] = hide(block_at <= image_row)
                at += image_rows
        image_ref[VIS:] = hide(text_at <= image_row)


def second_arrays(vis_start, lengths, cotangent, image_kv, text, received, halo):
    tok_rows, width = cotangent.shape
    image_rows = image_kv.shape[1]
    text_rows = PROMPT + (image_rows if image_rows == IMAGE_BLOCK else 0)
    rounds = window_rounds(lax.axis_size("ctx"), tok_rows, image_rows)
    count = len(rounds) + 1
    block = 2048
    spec = pl.BlockSpec
    smem = spec(memory_space=pltpu.SMEM)
    lanes = RATIO * IMAGE_BLOCK
    near = PROMPT + halo + tok_rows
    whole = lambda *shape: spec(shape, lambda at: (0,) * len(shape))
    out = pl.pallas_call(
        functools.partial(second_kernel, rounds, tok_rows, image_rows, halo),
        grid=(width // block,),
        in_specs=[
            smem,
            smem,
            spec((tok_rows, block), lambda at: (0, at)),
            whole(2, image_rows, KV_WIDTH),
            whole(2, PROMPT, KV_WIDTH),
            whole(2, PROMPT, KV_WIDTH),
        ],
        out_specs=[spec((IMAGE_BLOCK, block), lambda at: (0, at)) for _ in range(count)]
        + [
            whole(near, tok_rows),
            whole(8, tok_rows),
            whole(PREFIX, lanes),
            whole(2, text_rows, KV_WIDTH),
        ],
        out_shape=[jax.ShapeDtypeStruct((IMAGE_BLOCK, width), jnp.bfloat16) for _ in range(count)]
        + [
            jax.ShapeDtypeStruct((near, tok_rows), jnp.float32),
            jax.ShapeDtypeStruct((8, tok_rows), jnp.float32),
            jax.ShapeDtypeStruct((PREFIX, lanes), jnp.float32),
            jax.ShapeDtypeStruct((2, text_rows, KV_WIDTH), jnp.bfloat16),
        ],
    )(vis_start, lengths, cotangent, image_kv, text, received)
    return out[:count], rounds, out[count:]


def first_products(parts, q_rows, d_rows):
    return [(dot_nt(keys, q_rows), dot_nt(values, d_rows)) for keys, values, _ in parts]


def chunks_of(rows):
    return [rows[at : at + KEY_CHUNK] for at in range(0, rows.shape[0], KEY_CHUNK)]


def fold_rows(rows, combine):
    folded = rows[:8]
    for at in range(8, rows.shape[0], 8):
        folded = combine(folded, rows[at : at + 8])
    return folded


def rows_backward(parts, products):
    scale = SCORE_SCALE * math.log2(math.e)
    scores, tops = [], []
    for (keys, values, bias), (raw, _) in zip(parts, products):
        one_row = bias.shape[0] == 1
        top = None
        for at, chunk in enumerate(chunks_of(raw)):
            chunk = chunk * scale
            if not one_row:
                chunk = chunk + bias[at * KEY_CHUNK : (at + 1) * KEY_CHUNK]
            scores.append((chunk, bias if one_row else None))
            folded = fold_rows(chunk, jnp.maximum)
            top = folded if top is None else jnp.maximum(top, folded)
        top = jnp.max(top, axis=0, keepdims=True)
        tops.append(top + bias if one_row else top)
    top = functools.reduce(jnp.maximum, tops)
    d_weights = [chunk for _, product in products for chunk in chunks_of(product)]
    total = mix = None
    kept = []
    for (chunk, bias), d_chunk in zip(scores, d_weights):
        terms = jnp.exp2(chunk + ((bias if bias is not None else 0.0) - top))
        folded = fold_rows(terms, jnp.add)
        total = folded if total is None else total + folded
        folded = fold_rows(terms * d_chunk, jnp.add)
        mix = folded if mix is None else mix + folded
        kept.append(terms)
    total = jnp.sum(total, axis=0, keepdims=True)
    mix = jnp.sum(mix, axis=0, keepdims=True)
    inverse = jnp.where(top > 0.5 * HIDDEN, 1.0 / total, 0.0)
    delta = mix * inverse
    weights, d_scores = [], []
    for terms, d_chunk in zip(kept, d_weights):
        chunk = terms * inverse
        weights.append(chunk.astype(jnp.bfloat16))
        d_scores.append((chunk * (d_chunk - delta)).astype(jnp.bfloat16))
    outcome = []
    for raw, _ in products:
        count = raw.shape[0] // KEY_CHUNK
        outcome.append(
            (jnp.concatenate(weights[:count], axis=0), jnp.concatenate(d_scores[:count], axis=0))
        )
        weights, d_scores = weights[count:], d_scores[count:]
    return outcome


def total_of(values):
    if len(values) == 1:
        return values[0]
    return sum(value.astype(jnp.float32) for value in values).astype(jnp.bfloat16)


def attend_kernel(
    block_rows,
    block_count,
    text_count,
    window_count,
    heads,
    halo,
    own,
    number_ref,
    near_ref,
    whole_ref,
    image_bias_ref,
    q_ref,
    d_ref,
    iq_ref,
    halo_ref,
    own_ref,
    *refs,
):
    block_refs, refs = refs[:block_count], refs[block_count:]
    text_refs, refs = refs[:text_count], refs[text_count:]
    window_refs, refs = refs[:window_count], refs[window_count:]
    dq_ref, *diq_refs, dmine_ref, dpair_ref, dhalo_ref, down_ref = refs
    text_refs = text_refs or [ref for ref in block_refs if ref.shape[1] > block_rows]
    near_bias = jnp.concatenate([near_ref[...]] * 2, axis=1)
    whole_bias = jnp.concatenate([whole_ref[:1]] * 2, axis=1)
    image_cotangent = total_of([ref[...] for ref in window_refs])
    image_queries = iq_ref[number_ref[1]]
    states = []
    units = []
    for head in range(heads):
        lanes = slice(head * HEAD_DIM, (head + 1) * HEAD_DIM)
        spans = [
            slice((head * RATIO + at) * HEAD_DIM, (head * RATIO + at + 1) * HEAD_DIM)
            for at in range(RATIO)
        ]
        visual, text, near = [], [], []
        for part in range(2):
            visual.append(
                jnp.concatenate([ref[part, :block_rows, lanes] for ref in block_refs], axis=0)
            )
            text.append(total_of([ref[part, -PROMPT:, lanes] for ref in text_refs]))
            near.append(
                jnp.concatenate(
                    [text[part], halo_ref[part, :, lanes], own_ref[0, part, :, lanes]], axis=0
                )
            )
        states.append((lanes, jnp.concatenate([visual[0], near[0]], axis=0).T, {}))
        own_parts = [(visual[0], visual[1], whole_bias), (near[0], near[1], near_bias)]
        for first in range(0, RATIO, 2):
            units.append((head, own_parts, q_ref, d_ref, spans[first : first + 2]))
        image_parts = [
            (visual[0], visual[1], image_bias_ref[:VIS]),
            (text[0], text[1], image_bias_ref[VIS:]),
        ]
        units.append((head, image_parts, image_queries, image_cotangent, spans))

    def begin(unit):
        _, parts, queries, cotangents, unit_spans = unit
        q_rows = jnp.concatenate([queries[:, span] for span in unit_spans], axis=0)
        d_rows = jnp.concatenate([cotangents[:, span] for span in unit_spans], axis=0)
        return q_rows, d_rows, first_products(parts, q_rows, d_rows)

    def finish(unit, begun):
        head, parts, _, _, unit_spans = unit
        lanes, keys_across, sums = states[head]
        q_rows, d_rows, products = begun
        outcome = rows_backward(parts, products)
        d_scores = jnp.concatenate([part[1] for part in outcome], axis=0)
        dq = dot_nn(keys_across[:, : d_scores.shape[0]], d_scores) * SCORE_SCALE
        dq = dq.astype(jnp.bfloat16).T
        rows = dq.shape[0] // len(unit_spans)
        for at, span in enumerate(unit_spans):
            if len(unit_spans) == 2:
                dq_ref[:, span] = dq[at * rows : (at + 1) * rows]
            else:
                for half, out_ref in enumerate(diq_refs):
                    place = at * rows + half * IMAGE_HALF
                    out_ref[:, span] = dq[place : place + IMAGE_HALF]
        for at, (weights, d_part) in enumerate(outcome):
            for kind, rows in ((0, dot_nn(d_part, q_rows)), (1, dot_nn(weights, d_rows))):
                count = rows.shape[0]
                earlier = sums.get((kind, at))
                if earlier is not None and count < earlier.shape[0]:
                    rows = jnp.concatenate([earlier[:count] + rows, earlier[count:]], axis=0)
                elif earlier is not None:
                    rows = earlier + rows
                sums[kind, at] = rows
        if len(unit_spans) == 2:
            return
        for part, scale in ((0, SCORE_SCALE), (1, 1.0)):
            of_visual = (sums[part, 0] * scale).astype(jnp.bfloat16)
            rest = sums[part, 1] * scale
            dmine_ref[part, :, lanes] = of_visual[: VIS // 2]
            dpair_ref[part, : VIS // 2, lanes] = of_visual[VIS // 2 :]
            dpair_ref[part, VIS // 2 :, lanes] = rest[:PROMPT].astype(jnp.bfloat16)
            dhalo_ref[part, :, lanes] = rest[PROMPT : PROMPT + halo].astype(jnp.bfloat16)
            down_ref[part, :, lanes] = rest[PROMPT + halo :]

    begun = begin(units[0])
    for at, unit in enumerate(units):
        later = begin(units[at + 1]) if at + 1 < len(units) else None
        finish(unit, begun)
        begun = later


def attend(
    number, masks, queries, cotangent, every_q, halo_kv, own_kv, blocks, texts, windows
):
    heads = 2
    near_bias, whole_bias, image_bias = masks
    own = queries.shape[0]
    halo = halo_kv.shape[1]
    groups = every_q.shape[0]
    columns = PREFIX + halo + own
    products = RATIO * (own * columns + IMAGE_BLOCK * PREFIX) * KV_HEADS
    spec = pl.BlockSpec
    kv_spec = lambda rows: spec((2, rows, heads * HEAD_DIM), lambda at: (0, 0, at))
    q_spec = lambda rows: spec((rows, heads * GROUP_WIDTH), lambda at: (0, at))
    whole = lambda rows: spec((rows, 128), lambda at: (0, 0))
    return pl.pallas_call(
        functools.partial(
            attend_kernel,
            VIS // len(blocks),
            len(blocks),
            len(texts),
            len(windows),
            heads,
            halo,
            own,
        ),
        grid=(KV_HEADS // heads,),
        in_specs=[
            spec(memory_space=pltpu.SMEM),
            whole(columns - VIS),
            whole(8),
            whole(PREFIX),
            q_spec(own),
            q_spec(own),
            spec((groups, IMAGE_BLOCK, heads * GROUP_WIDTH), lambda at: (0, 0, at)),
            kv_spec(halo),
            spec((1, 2, own, heads * HEAD_DIM), lambda at: (0, 0, 0, at)),
        ]
        + [kv_spec(block.shape[1]) for block in [*blocks, *texts]]
        + [q_spec(IMAGE_BLOCK) for _ in windows],
        out_specs=[
            q_spec(own),
            q_spec(IMAGE_HALF),
            q_spec(IMAGE_HALF),
            kv_spec(VIS // 2),
            kv_spec(VIS // 2 + PROMPT),
            kv_spec(halo),
            kv_spec(own),
        ],
        out_shape=[
            jax.ShapeDtypeStruct((own, Q_WIDTH), jnp.bfloat16),
            jax.ShapeDtypeStruct((IMAGE_HALF, Q_WIDTH), jnp.bfloat16),
            jax.ShapeDtypeStruct((IMAGE_HALF, Q_WIDTH), jnp.bfloat16),
            jax.ShapeDtypeStruct((2, VIS // 2, KV_WIDTH), jnp.bfloat16),
            jax.ShapeDtypeStruct((2, VIS // 2 + PROMPT, KV_WIDTH), jnp.bfloat16),
            jax.ShapeDtypeStruct((2, halo, KV_WIDTH), jnp.bfloat16),
            jax.ShapeDtypeStruct((2, own, KV_WIDTH), jnp.float32),
        ],
        cost_estimate=pl.CostEstimate(
            flops=10 * products * HEAD_DIM,
            bytes_accessed=12 * 1024 * 1024,
            transcendentals=products,
        ),
    )(
        number,
        near_bias,
        whole_bias,
        image_bias,
        queries,
        cotangent,
        every_q,
        halo_kv,
        own_kv,
        *blocks,
        *texts,
        *windows,
    )


def route(rows, number, back, beside=()):
    groups = lax.axis_size("rollout")
    arrays = [array for array, _ in beside]

    def move_beside(arrays):
        return [lax.ppermute(array, "ctx", pairs) for array, (_, pairs) in zip(arrays, beside)]

    if groups != 4:
        every = lax.all_gather(rows, "rollout", axis=0)
        picked = lax.dynamic_index_in_dim(every, number[2 if back else 1], 0, keepdims=False)
        return [picked] + move_beside(arrays)

    def branch(images):
        pairs = [(g, i) if back else (i, g) for g, i in enumerate(images)]
        if all(source == target for source, target in pairs):
            return lambda rows, arrays: [rows] + move_beside(arrays)
        return lambda rows, arrays: [lax.ppermute(rows, "rollout", pairs)] + move_beside(arrays)

    orders = itertools.permutations(range(groups))
    return lax.switch(number[0], [branch(images) for images in orders], rows, arrays)


def window_rounds(ctx_size, tok_rows, image_rows):
    rounds = []
    for target in range(ctx_size):
        lowest = (image_rows * target + 1) // tok_rows
        highest = (image_rows * target + image_rows - 1 + PROMPT - 1) // tok_rows
        for source in range(lowest, highest + 1):
            if source == target:
                continue
            for pairs in rounds:
                if all(s != source and t != target for s, t in pairs):
                    pairs.append((source, target))
                    break
            else:
                rounds.append([(source, target)])
    return rounds


def image_windows(windows, rounds):
    parts = [windows[0]] + [
        lax.ppermute(rows, "ctx", pairs) for rows, pairs in zip(windows[1:], rounds)
    ]
    if len(parts) > 8:
        parts = [sum(part.astype(jnp.float32) for part in parts).astype(jnp.bfloat16)]
    return parts


def xor_pairs(step):
    return [(at, at ^ step) for at in range(lax.axis_size("ctx"))]


def xor_permute(rows, step):
    return lax.ppermute(rows, "ctx", xor_pairs(step))


def on_device(function, *arrays):
    if lax.axis_size("ctx") != 8:
        return function(*arrays)
    shapes = jax.eval_shape(function, *arrays)

    def kernel(*refs):
        for out_ref, value in zip(
            refs[len(arrays) :], function(*[ref[...] for ref in refs[: len(arrays)]])
        ):
            out_ref[...] = value

    def spec(array):
        *rows, width = array.shape
        return pl.BlockSpec((*rows, width // 2), lambda at: (0,) * len(rows) + (at,))

    return pl.pallas_call(
        kernel,
        grid=(2,),
        in_specs=[spec(array) for array in arrays],
        out_specs=[spec(shape) for shape in shapes],
        out_shape=[jax.ShapeDtypeStruct(shape.shape, shape.dtype) for shape in shapes],
        cost_estimate=pl.CostEstimate(flops=1, bytes_accessed=1, transcendentals=0),
    )(*arrays)


def text_strides(ctx_size, late_shard):
    strides = [1 << at for at in range(1, ctx_size.bit_length() - 1)]
    return [stride for stride in reversed(strides) if stride != late_shard]


def chip_steps(ctx_size):
    return list(range(2, ctx_size, 2))


def gather_prefix(image_kv, text, late_shard):
    ctx_size = lax.axis_size("ctx")
    steps = chip_steps(ctx_size)
    if ctx_size == 8:
        mine = [text, xor_permute(image_kv, 2), xor_permute(text, 4), xor_permute(image_kv, 6)]
        blocks = mine + [xor_permute(block, 1) for block in mine]
        return blocks, [blocks[at] for at in (0, 2, 4, 6)]
    mine = jnp.concatenate(
        [image_kv] + [xor_permute(image_kv, step) for step in steps], axis=1
    )
    return [mine, xor_permute(mine, 1)], list(spread_text(text, late_shard))


def split_sums(image_rows, steps, d_mine, d_pair, other):
    half = VIS // 2
    add = lambda one, two: one.astype(jnp.float32) + two.astype(jnp.float32)
    text = add(d_pair[:, half:], other[:, half:])
    out = []
    for at in range(len(steps) + 1):
        rows = slice(at * image_rows, (at + 1) * image_rows)
        sums = add(d_mine[:, rows], other[:, rows])
        if len(steps) == 3 and at in (1, 2):
            halves = text[2 - at]
            halves = jnp.stack([halves[: PROMPT // 2], halves[PROMPT // 2 :]])
            sums = jnp.concatenate([sums, halves], axis=1)
        out.append(sums.astype(jnp.bfloat16) if at else sums)
    return out + [text[0], text[1]]


def add_sums(image_rows, own, keys_text, values_text, *parts):
    texts = [values_text, keys_text]
    for at, part in enumerate(parts):
        own = own + part[:, :image_rows].astype(jnp.float32)
        if part.shape[1] > image_rows:
            rows = part[:, image_rows:].astype(jnp.float32)
            texts[at] = texts[at] + jnp.concatenate([rows[0], rows[1]], axis=0)
    return [part.astype(jnp.bfloat16) for part in (own, texts[1], texts[0])]


def spread_text(text, late_shard):
    for stride in text_strides(lax.axis_size("ctx"), late_shard):
        text = text + xor_permute(text, stride)
    return text, xor_permute(text, 1)


def collect_text(text, late_shard):
    for stride in reversed(text_strides(lax.axis_size("ctx"), late_shard)):
        moved = xor_permute(text.astype(jnp.bfloat16), stride)
        text = text.astype(jnp.float32) + moved.astype(jnp.float32)
    return text.astype(jnp.bfloat16)


def halo_cuts(tok_rows, halo):
    cuts = []
    left = halo
    while left > 0:
        cuts.append(min(left, tok_rows))
        left -= cuts[-1]
    return cuts


def halo_pairs(step, tok_rows):
    first = PREFIX // tok_rows
    return [(at, at + step) for at in range(first, lax.axis_size("ctx") - step)]


def halo_rows(tail, halo, tok_rows):
    parts = []
    for step, count in enumerate(halo_cuts(tok_rows, halo), 1):
        pairs = halo_pairs(step, tok_rows)
        rows = tail if count == tail.shape[1] else tail[:, tail.shape[1] - count :]
        parts.insert(0, lax.ppermute(rows, "ctx", pairs))
    return jnp.concatenate(parts, axis=1) if len(parts) > 1 else parts[0]


def halo_parts(d_halo, tok_rows):
    cuts = halo_cuts(tok_rows, d_halo.shape[1])
    parts = []
    end = d_halo.shape[1]
    for step, count in enumerate(cuts, 1):
        rows = d_halo if len(cuts) == 1 else d_halo[:, end - count : end]
        parts.append((rows, [(target, at) for at, target in halo_pairs(step, tok_rows)]))
        end -= count
    return parts


def last_kernel(part_count, vis_ref, dkv_ref, down_ref, *refs):
    text_refs, refs = refs[:4], refs[4:]
    part_refs = refs[:part_count]
    *dq_refs, image_ref, kv_ref = refs[part_count:]
    here = lax.axis_index("ctx")
    tok_rows = down_ref.shape[1]
    at = 0
    for dq_ref in dq_refs:
        image_ref[0, at : at + dq_ref.shape[0], :Q_WIDTH] = dq_ref[...]
        at += dq_ref.shape[0]
    image_ref[0, :, Q_WIDTH : Q_WIDTH + KV_WIDTH] = dkv_ref[0]
    image_ref[0, :, Q_WIDTH + KV_WIDTH :] = dkv_ref[1]
    at = lax.broadcasted_iota(jnp.int32, (PROMPT, KV_WIDTH), 0)
    ahead = jnp.where(here == 0, 1, 0)
    behind = jnp.where(here == VIS // tok_rows, 1, 0)
    kept = jnp.where(at < vis_ref[0], ahead, behind) == 1
    for part in range(2):
        text = text_refs[part][...].astype(jnp.float32)
        text = text + text_refs[2 + part][...].astype(jnp.float32)
        text = jnp.where(kept, text, 0.0)
        sums = down_ref[part] + jnp.concatenate(
            [text, jnp.zeros((tok_rows - PROMPT, KV_WIDTH), jnp.float32)], axis=0
        )
        for part_ref in part_refs:
            back = part_ref[part].astype(jnp.float32)
            if back.shape[0] < tok_rows:
                missing = jnp.zeros((tok_rows - back.shape[0], KV_WIDTH), jnp.float32)
                back = jnp.concatenate([missing, back], axis=0)
            sums = sums + back
        kv_ref[0, part] = sums.astype(jnp.bfloat16)


def last_arrays(vis_start, image_dq, image_dkv, d_own_kv, texts, parts):
    rows = image_dkv.shape[1]
    smem = pl.BlockSpec(memory_space=pltpu.SMEM)
    vmem = pl.BlockSpec(memory_space=pltpu.VMEM)
    return pl.pallas_call(
        functools.partial(last_kernel, len(parts)),
        in_specs=[smem] + [vmem] * (6 + len(parts) + len(image_dq)),
        out_specs=[vmem, vmem],
        out_shape=[
            jax.ShapeDtypeStruct((1, rows, Q_WIDTH + 2 * KV_WIDTH), jnp.bfloat16),
            jax.ShapeDtypeStruct((1,) + d_own_kv.shape, jnp.bfloat16),
        ],
    )(vis_start, image_dkv, d_own_kv, *texts, *parts, *image_dq)


def gather_queries(image_q):
    every = lax.all_gather(image_q, "rollout", axis=0)
    missing = IMAGE_BLOCK - every.shape[1]
    return jnp.pad(every, ((0, 0), (0, missing), (0, 0))) if missing else every


def per_device(queries, keys_values, image_rows, cotangent, seq_image, vis_start, comp_lengths):
    tok_rows = queries.shape[1]
    image_count = image_rows.shape[1]
    ctx_size = lax.axis_size("ctx")
    seq_len = tok_rows * ctx_size
    late_shard = VIS // tok_rows
    longest = 4 * (seq_len - PREFIX) // (3 * NCOMP)
    halo = -(-(longest - 1) // 64) * 64
    q_own, d_own = queries[0], cotangent[0]

    number, image_kv, image_q, text, tail = first_arrays(
        seq_image, vis_start, image_rows, keys_values, halo
    )
    every_q = gather_queries(image_q)
    image_kv, swapped = route(image_kv, number, False, [(text, xor_pairs(late_shard))])
    image_kv, d_later = lax.optimization_barrier((image_kv, d_own))
    windows, rounds, (*masks, text) = second_arrays(
        vis_start, comp_lengths, d_later, image_kv, text, swapped, halo
    )
    blocks, texts = gather_prefix(image_kv, text, late_shard)
    windows = image_windows(windows, rounds)
    halo_kv = halo_rows(tail, halo, tok_rows)

    grad_q, *d_image_q, d_mine, d_pair, d_halo, d_own_kv = attend(
        number,
        masks,
        q_own,
        d_own,
        every_q,
        halo_kv,
        keys_values,
        blocks,
        [] if ctx_size == 8 else texts,
        windows,
    )

    d_image_q = [
        half[: image_count - at * IMAGE_HALF]
        for at, half in enumerate(d_image_q)
        if at * IMAGE_HALF < image_count
    ]
    image_dq, other, *halo_back = route(
        d_image_q[0], number, True, [(d_pair, xor_pairs(1))] + halo_parts(d_halo, tok_rows)
    )
    image_dq = [image_dq]
    steps = chip_steps(ctx_size)
    own, *sent, keys_text, values_text = on_device(
        functools.partial(split_sums, image_count, steps), d_mine, d_pair, other
    )
    beside = [(rows, xor_pairs(step)) for rows, step in zip(sent, steps)]
    if len(d_image_q) > 1:
        second, *moved = route(d_image_q[1], number, True, beside)
        image_dq.append(second)
    else:
        moved = [lax.ppermute(rows, "ctx", pairs) for rows, pairs in beside]
    sums, keys_text, values_text = on_device(
        functools.partial(add_sums, image_count), own, keys_text, values_text, *moved
    )
    if ctx_size != 8:
        keys_text = collect_text(keys_text, late_shard)
        values_text = collect_text(values_text, late_shard)
    keys_step = late_shard
    values_step = 4 if ctx_size == 8 else late_shard
    image_dkv, *other_texts = route(
        sums,
        number,
        True,
        [(keys_text, xor_pairs(keys_step)), (values_text, xor_pairs(values_step))],
    )
    grad_image, grad_kv = last_arrays(
        vis_start,
        image_dq,
        image_dkv,
        d_own_kv,
        [keys_text, values_text, *other_texts],
        halo_back,
    )
    return (grad_q[None], grad_kv, grad_image)


def solution(mesh):
    placed = (
        P("rollout", "ctx", None),
        P("rollout", None, "ctx", None),
        P("rollout", "ctx", None),
        P("rollout", "ctx", None),
        P(),
        P("rollout"),
        P("rollout", None),
    )
    return jax.shard_map(
        per_device,
        mesh=mesh,
        in_specs=placed,
        out_specs=(
            P("rollout", "ctx", None),
            P("rollout", None, "ctx", None),
            P("rollout", "ctx", None),
        ),
        check_vma=False,
    )
```

```python
import functools
import itertools
import math

import jax
import jax.numpy as jnp
from jax import lax
from jax.experimental import pallas as pl
from jax.experimental.pallas import tpu as pltpu
from jax.sharding import PartitionSpec as P

HEADS = 32
KV_HEADS = 8
HEAD_DIM = 128
VIS = 256
PROMPT = 64
NCOMP = 16

RATIO = HEADS // KV_HEADS
PREFIX = VIS + PROMPT
Q_WIDTH = HEADS * HEAD_DIM
KV_WIDTH = KV_HEADS * HEAD_DIM
GROUP_WIDTH = RATIO * HEAD_DIM
IMAGE_BLOCK = 32
IMAGE_HALF = IMAGE_BLOCK // 2
KEY_CHUNK = 64
HIDDEN = -1e30
SCORE_SCALE = 1.0 / math.sqrt(HEAD_DIM)


def dot_nt(left, right):
    return lax.dot_general(
        left, right, (((1,), (1,)), ((), ())), preferred_element_type=jnp.float32
    )


def dot_nn(left, right):
    return lax.dot_general(
        left, right, (((1,), (0,)), ((), ())), preferred_element_type=jnp.float32
    )


def dot_tn(left, right):
    return lax.dot_general(
        left, right, (((0,), (0,)), ((), ())), preferred_element_type=jnp.float32
    )


def first_kernel(halo, seq_ref, vis_ref, image_ref, kv_ref, number_ref, *out_refs):
    ikv_ref, iq_ref, text_ref, tail_ref = out_refs
    groups = seq_ref.shape[0]
    group = lax.axis_index("rollout")
    here = lax.axis_index("ctx")
    images = [seq_ref[at] for at in range(groups)]
    number = jnp.int32(0)
    if groups == 4:
        for at, weight in enumerate((6, 2, 1)):
            for later in range(at + 1, groups):
                number = number + jnp.where(images[later] < images[at], weight, 0)
    place = jnp.int32(0)
    user = jnp.int32(0)
    for at in range(groups):
        place = place + jnp.where(group == at, images[at], 0)
        user = user + jnp.where(images[at] == group, at, 0)
    number_ref[0] = number
    number_ref[1] = place
    number_ref[2] = user
    iq_ref[...] = image_ref[0, :, :Q_WIDTH]
    ikv_ref[0] = image_ref[0, :, Q_WIDTH : Q_WIDTH + KV_WIDTH]
    ikv_ref[1] = image_ref[0, :, Q_WIDTH + KV_WIDTH :]
    tok_rows = kv_ref.shape[2]
    late_shard = VIS // tok_rows
    at = lax.broadcasted_iota(jnp.int32, (PROMPT, KV_WIDTH), 0)
    ahead = jnp.where(here == 0, 1, 0)
    behind = jnp.where(here == late_shard, 1, 0)
    kept = jnp.where(at < vis_ref[0], ahead, behind) == 1
    for part in range(2):
        rows = kv_ref[0, part, :PROMPT].astype(jnp.float32)
        text_ref[part] = jnp.where(kept, rows, 0.0).astype(jnp.bfloat16)
        tail_ref[part] = kv_ref[0, part, tok_rows - halo :]


def first_arrays(seq_image, vis_start, image_rows, keys_values, halo):
    rows = image_rows.shape[1]
    smem = pl.BlockSpec(memory_space=pltpu.SMEM)
    vmem = pl.BlockSpec(memory_space=pltpu.VMEM)
    tail = min(halo, keys_values.shape[2])
    return pl.pallas_call(
        functools.partial(first_kernel, tail),
        in_specs=[smem, smem, vmem, vmem],
        out_specs=[smem, vmem, vmem, vmem, vmem],
        out_shape=[
            jax.ShapeDtypeStruct((3,), jnp.int32),
            jax.ShapeDtypeStruct((2, rows, KV_WIDTH), jnp.bfloat16),
            jax.ShapeDtypeStruct((rows, Q_WIDTH), jnp.bfloat16),
            jax.ShapeDtypeStruct((2, PROMPT, KV_WIDTH), jnp.bfloat16),
            jax.ShapeDtypeStruct((2, tail, KV_WIDTH), jnp.bfloat16),
        ],
    )(seq_image, vis_start, image_rows, keys_values)


def segments(positions, length_ref):
    end = jnp.int32(PREFIX)
    segment = jnp.where(positions < PREFIX, 0, 1)
    for at in range(NCOMP):
        end = end + length_ref[0, at]
        segment = segment + jnp.where(positions >= end, 1, 0)
    return segment


def hide(visible):
    return jnp.where(visible, 0.0, HIDDEN)


def second_kernel(
    rounds, tok_rows, image_rows, halo, vis_ref, length_ref, d_ref, kv_ref, t_ref, r_ref, *out_refs
):
    *window_refs, near_ref, whole_ref, image_ref, text_ref = out_refs
    here = lax.axis_index("ctx")
    ctx_size = lax.axis_size("ctx")
    row = lax.broadcasted_iota(jnp.int32, (IMAGE_BLOCK, tok_rows), 0)
    column = lax.broadcasted_iota(jnp.int32, (IMAGE_BLOCK, tok_rows), 1)
    place = jnp.where(row < image_rows, row, 1 << 20)
    picks = []
    for pairs in [[]] + rounds:
        target = here
        for source, other in pairs:
            target = jnp.where(here == source, other, target)
        begin = vis_ref[0] + image_rows * target - tok_rows * here
        picks.append(jnp.where(column == place + begin, 1.0, 0.0).astype(jnp.bfloat16))
    picked = dot_nn(jnp.concatenate(picks, axis=0), d_ref[...]).astype(jnp.bfloat16)
    for at, window_ref in enumerate(window_refs):
        window_ref[...] = picked[at * IMAGE_BLOCK : (at + 1) * IMAGE_BLOCK]

    @pl.when(pl.program_id(0) == 0)
    def _():
        vis = vis_ref[0]
        text = t_ref[...].astype(jnp.float32) + r_ref[...].astype(jnp.float32)
        if kv_ref.shape[1] == IMAGE_BLOCK:
            text_ref[:, :IMAGE_BLOCK] = kv_ref[...]
        text_ref[:, text_ref.shape[1] - PROMPT :] = text.astype(jnp.bfloat16)
        own_at = lax.broadcasted_iota(jnp.int32, (8, tok_rows), 1) + here * tok_rows
        own_segment = segments(own_at, length_ref)[:1]
        placeholder = (own_at >= vis) & (own_at < vis + VIS)
        own_row = jnp.where(placeholder, -1, own_at)
        whole_ref[...] = hide(own_row >= vis + VIS).astype(jnp.float32)
        own_row = own_row[:1]
        image_at = lax.broadcasted_iota(jnp.int32, (1, RATIO * IMAGE_BLOCK), 1) % IMAGE_BLOCK
        image_row = jnp.where(image_at < image_rows, vis + here * image_rows + image_at, -1)
        text_at = lax.broadcasted_iota(jnp.int32, (PROMPT, tok_rows), 0)
        text_at = text_at + jnp.where(text_at < vis, 0, VIS)
        near_ref[:PROMPT] = hide(text_at <= own_row)
        near_at = lax.broadcasted_iota(jnp.int32, (halo + tok_rows, tok_rows), 0)
        near_at = near_at + (here * tok_rows - halo)
        sees = (near_at <= own_row) & (near_at >= PREFIX)
        sees = sees & (segments(near_at, length_ref) == own_segment)
        near_ref[PROMPT:] = hide(sees)
        at = 0
        for core in range(2):
            for step in range(0, ctx_size, 2):
                begin = (here ^ (step + core)) * image_rows + vis
                shape = (image_rows, RATIO * IMAGE_BLOCK)
                block_at = lax.broadcasted_iota(jnp.int32, shape, 0) + begin
                image_ref[at : at + image_rows] = hide(block_at <= image_row)
                at += image_rows
        image_ref[VIS:] = hide(text_at <= image_row)


def second_arrays(vis_start, lengths, cotangent, image_kv, text, received, halo):
    tok_rows, width = cotangent.shape
    image_rows = image_kv.shape[1]
    text_rows = PROMPT + (image_rows if image_rows == IMAGE_BLOCK else 0)
    rounds = window_rounds(lax.axis_size("ctx"), tok_rows, image_rows)
    count = len(rounds) + 1
    block = 2048
    spec = pl.BlockSpec
    smem = spec(memory_space=pltpu.SMEM)
    lanes = RATIO * IMAGE_BLOCK
    near = PROMPT + halo + tok_rows
    whole = lambda *shape: spec(shape, lambda at: (0,) * len(shape))
    out = pl.pallas_call(
        functools.partial(second_kernel, rounds, tok_rows, image_rows, halo),
        grid=(width // block,),
        in_specs=[
            smem,
            smem,
            spec((tok_rows, block), lambda at: (0, at)),
            whole(2, image_rows, KV_WIDTH),
            whole(2, PROMPT, KV_WIDTH),
            whole(2, PROMPT, KV_WIDTH),
        ],
        out_specs=[spec((IMAGE_BLOCK, block), lambda at: (0, at)) for _ in range(count)]
        + [
            whole(near, tok_rows),
            whole(8, tok_rows),
            whole(PREFIX, lanes),
            whole(2, text_rows, KV_WIDTH),
        ],
        out_shape=[jax.ShapeDtypeStruct((IMAGE_BLOCK, width), jnp.bfloat16) for _ in range(count)]
        + [
            jax.ShapeDtypeStruct((near, tok_rows), jnp.float32),
            jax.ShapeDtypeStruct((8, tok_rows), jnp.float32),
            jax.ShapeDtypeStruct((PREFIX, lanes), jnp.float32),
            jax.ShapeDtypeStruct((2, text_rows, KV_WIDTH), jnp.bfloat16),
        ],
    )(vis_start, lengths, cotangent, image_kv, text, received)
    return out[:count], rounds, out[count:]


def first_products(parts, q_rows, d_rows):
    return [(dot_nt(keys, q_rows), dot_nt(values, d_rows)) for keys, values, _ in parts]


def chunks_of(rows):
    return [rows[at : at + KEY_CHUNK] for at in range(0, rows.shape[0], KEY_CHUNK)]


def fold_rows(rows, combine):
    folded = rows[:8]
    for at in range(8, rows.shape[0], 8):
        folded = combine(folded, rows[at : at + 8])
    return folded


def rows_backward(parts, products):
    scale = SCORE_SCALE * math.log2(math.e)
    scores, tops = [], []
    for (keys, values, bias), (raw, _) in zip(parts, products):
        one_row = bias.shape[0] == 1
        top = None
        for at, chunk in enumerate(chunks_of(raw)):
            chunk = chunk * scale
            if not one_row:
                chunk = chunk + bias[at * KEY_CHUNK : (at + 1) * KEY_CHUNK]
            scores.append((chunk, bias if one_row else None))
            folded = fold_rows(chunk, jnp.maximum)
            top = folded if top is None else jnp.maximum(top, folded)
        top = jnp.max(top, axis=0, keepdims=True)
        tops.append(top + bias if one_row else top)
    top = functools.reduce(jnp.maximum, tops)
    d_weights = [chunk for _, product in products for chunk in chunks_of(product)]
    total = mix = None
    kept = []
    for (chunk, bias), d_chunk in zip(scores, d_weights):
        terms = jnp.exp2(chunk + ((bias if bias is not None else 0.0) - top))
        folded = fold_rows(terms, jnp.add)
        total = folded if total is None else total + folded
        folded = fold_rows(terms * d_chunk, jnp.add)
        mix = folded if mix is None else mix + folded
        kept.append(terms)
    total = jnp.sum(total, axis=0, keepdims=True)
    mix = jnp.sum(mix, axis=0, keepdims=True)
    inverse = jnp.where(top > 0.5 * HIDDEN, 1.0 / total, 0.0)
    delta = mix * inverse
    weights, d_scores = [], []
    for terms, d_chunk in zip(kept, d_weights):
        chunk = terms * inverse
        weights.append(chunk.astype(jnp.bfloat16))
        d_scores.append((chunk * (d_chunk - delta)).astype(jnp.bfloat16))
    outcome = []
    for raw, _ in products:
        count = raw.shape[0] // KEY_CHUNK
        outcome.append(
            (jnp.concatenate(weights[:count], axis=0), jnp.concatenate(d_scores[:count], axis=0))
        )
        weights, d_scores = weights[count:], d_scores[count:]
    return outcome


def total_of(values):
    if len(values) == 1:
        return values[0]
    return sum(value.astype(jnp.float32) for value in values).astype(jnp.bfloat16)


def attend_kernel(
    block_rows,
    block_count,
    text_count,
    window_count,
    heads,
    halo,
    own,
    number_ref,
    near_ref,
    whole_ref,
    image_bias_ref,
    q_ref,
    d_ref,
    iq_ref,
    halo_ref,
    own_ref,
    *refs,
):
    block_refs, refs = refs[:block_count], refs[block_count:]
    text_refs, refs = refs[:text_count], refs[text_count:]
    window_refs, refs = refs[:window_count], refs[window_count:]
    dq_ref, *diq_refs, dmine_ref, dpair_ref, dhalo_ref, down_ref = refs
    text_refs = text_refs or [ref for ref in block_refs if ref.shape[1] > block_rows]
    near_bias = jnp.concatenate([near_ref[...]] * 2, axis=1)
    whole_bias = jnp.concatenate([whole_ref[:1]] * 2, axis=1)
    image_cotangent = total_of([ref[...] for ref in window_refs])
    image_queries = iq_ref[number_ref[1]]
    states = []
    units = []
    for head in range(heads):
        lanes = slice(head * HEAD_DIM, (head + 1) * HEAD_DIM)
        spans = [
            slice((head * RATIO + at) * HEAD_DIM, (head * RATIO + at + 1) * HEAD_DIM)
            for at in range(RATIO)
        ]
        visual, text, near = [], [], []
        for part in range(2):
            visual.append(
                jnp.concatenate([ref[part, :block_rows, lanes] for ref in block_refs], axis=0)
            )
            text.append(total_of([ref[part, -PROMPT:, lanes] for ref in text_refs]))
            near.append(
                jnp.concatenate(
                    [text[part], halo_ref[part, :, lanes], own_ref[0, part, :, lanes]], axis=0
                )
            )
        states.append((lanes, jnp.concatenate([visual[0], near[0]], axis=0).T, {}))
        own_parts = [(visual[0], visual[1], whole_bias), (near[0], near[1], near_bias)]
        for first in range(0, RATIO, 2):
            units.append((head, own_parts, q_ref, d_ref, spans[first : first + 2]))
        image_parts = [
            (visual[0], visual[1], image_bias_ref[:VIS]),
            (text[0], text[1], image_bias_ref[VIS:]),
        ]
        units.append((head, image_parts, image_queries, image_cotangent, spans))

    def begin(unit):
        _, parts, queries, cotangents, unit_spans = unit
        q_rows = jnp.concatenate([queries[:, span] for span in unit_spans], axis=0)
        d_rows = jnp.concatenate([cotangents[:, span] for span in unit_spans], axis=0)
        return q_rows, d_rows, first_products(parts, q_rows, d_rows)

    def finish(unit, begun):
        head, parts, _, _, unit_spans = unit
        lanes, keys_across, sums = states[head]
        q_rows, d_rows, products = begun
        outcome = rows_backward(parts, products)
        d_scores = jnp.concatenate([part[1] for part in outcome], axis=0)
        dq = dot_nn(keys_across[:, : d_scores.shape[0]], d_scores) * SCORE_SCALE
        dq = dq.astype(jnp.bfloat16).T
        rows = dq.shape[0] // len(unit_spans)
        for at, span in enumerate(unit_spans):
            if len(unit_spans) == 2:
                dq_ref[:, span] = dq[at * rows : (at + 1) * rows]
            else:
                for half, out_ref in enumerate(diq_refs):
                    place = at * rows + half * IMAGE_HALF
                    out_ref[:, span] = dq[place : place + IMAGE_HALF]
        for at, (weights, d_part) in enumerate(outcome):
            for kind, rows in ((0, dot_nn(d_part, q_rows)), (1, dot_nn(weights, d_rows))):
                count = rows.shape[0]
                earlier = sums.get((kind, at))
                if earlier is not None and count < earlier.shape[0]:
                    rows = jnp.concatenate([earlier[:count] + rows, earlier[count:]], axis=0)
                elif earlier is not None:
                    rows = earlier + rows
                sums[kind, at] = rows
        if len(unit_spans) == 2:
            return
        for part, scale in ((0, SCORE_SCALE), (1, 1.0)):
            of_visual = (sums[part, 0] * scale).astype(jnp.bfloat16)
            rest = sums[part, 1] * scale
            dmine_ref[part, :, lanes] = of_visual[: VIS // 2]
            dpair_ref[part, : VIS // 2, lanes] = of_visual[VIS // 2 :]
            dpair_ref[part, VIS // 2 :, lanes] = rest[:PROMPT].astype(jnp.bfloat16)
            dhalo_ref[part, :, lanes] = rest[PROMPT : PROMPT + halo].astype(jnp.bfloat16)
            down_ref[part, :, lanes] = rest[PROMPT + halo :]

    begun = begin(units[0])
    for at, unit in enumerate(units):
        later = begin(units[at + 1]) if at + 1 < len(units) else None
        finish(unit, begun)
        begun = later


def attend(
    number, masks, queries, cotangent, every_q, halo_kv, own_kv, blocks, texts, windows
):
    heads = 2
    near_bias, whole_bias, image_bias = masks
    own = queries.shape[0]
    halo = halo_kv.shape[1]
    groups = every_q.shape[0]
    columns = PREFIX + halo + own
    products = RATIO * (own * columns + IMAGE_BLOCK * PREFIX) * KV_HEADS
    spec = pl.BlockSpec
    kv_spec = lambda rows: spec((2, rows, heads * HEAD_DIM), lambda at: (0, 0, at))
    q_spec = lambda rows: spec((rows, heads * GROUP_WIDTH), lambda at: (0, at))
    whole = lambda rows: spec((rows, 128), lambda at: (0, 0))
    return pl.pallas_call(
        functools.partial(
            attend_kernel,
            VIS // len(blocks),
            len(blocks),
            len(texts),
            len(windows),
            heads,
            halo,
            own,
        ),
        grid=(KV_HEADS // heads,),
        in_specs=[
            spec(memory_space=pltpu.SMEM),
            whole(columns - VIS),
            whole(8),
            whole(PREFIX),
            q_spec(own),
            q_spec(own),
            spec((groups, IMAGE_BLOCK, heads * GROUP_WIDTH), lambda at: (0, 0, at)),
            kv_spec(halo),
            spec((1, 2, own, heads * HEAD_DIM), lambda at: (0, 0, 0, at)),
        ]
        + [kv_spec(block.shape[1]) for block in [*blocks, *texts]]
        + [q_spec(IMAGE_BLOCK) for _ in windows],
        out_specs=[
            q_spec(own),
            q_spec(IMAGE_HALF),
            q_spec(IMAGE_HALF),
            kv_spec(VIS // 2),
            kv_spec(VIS // 2 + PROMPT),
            kv_spec(halo),
            kv_spec(own),
        ],
        out_shape=[
            jax.ShapeDtypeStruct((own, Q_WIDTH), jnp.bfloat16),
            jax.ShapeDtypeStruct((IMAGE_HALF, Q_WIDTH), jnp.bfloat16),
            jax.ShapeDtypeStruct((IMAGE_HALF, Q_WIDTH), jnp.bfloat16),
            jax.ShapeDtypeStruct((2, VIS // 2, KV_WIDTH), jnp.bfloat16),
            jax.ShapeDtypeStruct((2, VIS // 2 + PROMPT, KV_WIDTH), jnp.bfloat16),
            jax.ShapeDtypeStruct((2, halo, KV_WIDTH), jnp.bfloat16),
            jax.ShapeDtypeStruct((2, own, KV_WIDTH), jnp.float32),
        ],
        cost_estimate=pl.CostEstimate(
            flops=10 * products * HEAD_DIM,
            bytes_accessed=12 * 1024 * 1024,
            transcendentals=products,
        ),
    )(
        number,
        near_bias,
        whole_bias,
        image_bias,
        queries,
        cotangent,
        every_q,
        halo_kv,
        own_kv,
        *blocks,
        *texts,
        *windows,
    )


def route(rows, number, back, beside=()):
    groups = lax.axis_size("rollout")
    arrays = [array for array, _ in beside]

    def move_beside(arrays):
        return [lax.ppermute(array, "ctx", pairs) for array, (_, pairs) in zip(arrays, beside)]

    if groups != 4:
        every = lax.all_gather(rows, "rollout", axis=0)
        picked = lax.dynamic_index_in_dim(every, number[2 if back else 1], 0, keepdims=False)
        return [picked] + move_beside(arrays)

    def branch(images):
        pairs = [(g, i) if back else (i, g) for g, i in enumerate(images)]
        if all(source == target for source, target in pairs):
            return lambda rows, arrays: [rows] + move_beside(arrays)
        return lambda rows, arrays: [lax.ppermute(rows, "rollout", pairs)] + move_beside(arrays)

    orders = itertools.permutations(range(groups))
    return lax.switch(number[0], [branch(images) for images in orders], rows, arrays)


def window_rounds(ctx_size, tok_rows, image_rows):
    rounds = []
    for target in range(ctx_size):
        lowest = (image_rows * target + 1) // tok_rows
        highest = (image_rows * target + image_rows - 1 + PROMPT - 1) // tok_rows
        for source in range(lowest, highest + 1):
            if source == target:
                continue
            for pairs in rounds:
                if all(s != source and t != target for s, t in pairs):
                    pairs.append((source, target))
                    break
            else:
                rounds.append([(source, target)])
    if ctx_size != 8:
        return rounds
    order = [
        [(0, 1), (1, 6)],
        [(0, 2), (1, 4), (2, 6)],
        [(1, 7)],
        [(0, 3), (1, 5), (2, 7)],
        [(1, 2)],
        [(1, 3)],
    ]
    assert sorted(sum(order, [])) == sorted(sum(rounds, []))
    return order


def image_windows(windows, rounds):
    parts = [windows[0]] + [
        lax.ppermute(rows, "ctx", pairs) for rows, pairs in zip(windows[1:], rounds)
    ]
    if len(parts) > 8:
        parts = [sum(part.astype(jnp.float32) for part in parts).astype(jnp.bfloat16)]
    return parts


def xor_pairs(step):
    return [(at, at ^ step) for at in range(lax.axis_size("ctx"))]


def xor_permute(rows, step):
    return lax.ppermute(rows, "ctx", xor_pairs(step))


def on_device(function, *arrays):
    if lax.axis_size("ctx") != 8:
        return function(*arrays)
    shapes = jax.eval_shape(function, *arrays)

    def kernel(*refs):
        for out_ref, value in zip(
            refs[len(arrays) :], function(*[ref[...] for ref in refs[: len(arrays)]])
        ):
            out_ref[...] = value

    def spec(array):
        *rows, width = array.shape
        return pl.BlockSpec((*rows, width // 2), lambda at: (0,) * len(rows) + (at,))

    return pl.pallas_call(
        kernel,
        grid=(2,),
        in_specs=[spec(array) for array in arrays],
        out_specs=[spec(shape) for shape in shapes],
        out_shape=[jax.ShapeDtypeStruct(shape.shape, shape.dtype) for shape in shapes],
        cost_estimate=pl.CostEstimate(flops=1, bytes_accessed=1, transcendentals=0),
    )(*arrays)


def text_strides(ctx_size, late_shard):
    strides = [1 << at for at in range(1, ctx_size.bit_length() - 1)]
    return [stride for stride in reversed(strides) if stride != late_shard]


def chip_steps(ctx_size):
    return list(range(2, ctx_size, 2))


def gather_prefix(image_kv, text, late_shard):
    ctx_size = lax.axis_size("ctx")
    steps = chip_steps(ctx_size)
    if ctx_size == 8:
        mine = [text, xor_permute(image_kv, 2), xor_permute(text, 4), xor_permute(image_kv, 6)]
        blocks = mine + [xor_permute(block, 1) for block in mine]
        return blocks, [blocks[at] for at in (0, 2, 4, 6)]
    mine = jnp.concatenate(
        [image_kv] + [xor_permute(image_kv, step) for step in steps], axis=1
    )
    return [mine, xor_permute(mine, 1)], list(spread_text(text, late_shard))


def split_sums(image_rows, steps, d_mine, d_pair, other):
    half = VIS // 2
    add = lambda one, two: one.astype(jnp.float32) + two.astype(jnp.float32)
    text = add(d_pair[:, half:], other[:, half:])
    out = []
    for at in range(len(steps) + 1):
        rows = slice(at * image_rows, (at + 1) * image_rows)
        sums = add(d_mine[:, rows], other[:, rows])
        if len(steps) == 3 and at in (1, 2):
            halves = text[2 - at]
            halves = jnp.stack([halves[: PROMPT // 2], halves[PROMPT // 2 :]])
            sums = jnp.concatenate([sums, halves], axis=1)
        out.append(sums.astype(jnp.bfloat16) if at else sums)
    return out + [text[0], text[1]]


def add_sums(image_rows, own, keys_text, values_text, *parts):
    texts = [values_text, keys_text]
    for at, part in enumerate(parts):
        own = own + part[:, :image_rows].astype(jnp.float32)
        if part.shape[1] > image_rows:
            rows = part[:, image_rows:].astype(jnp.float32)
            texts[at] = texts[at] + jnp.concatenate([rows[0], rows[1]], axis=0)
    return [part.astype(jnp.bfloat16) for part in (own, texts[1], texts[0])]


def spread_text(text, late_shard):
    for stride in text_strides(lax.axis_size("ctx"), late_shard):
        text = text + xor_permute(text, stride)
    return text, xor_permute(text, 1)


def collect_text(text, late_shard):
    for stride in reversed(text_strides(lax.axis_size("ctx"), late_shard)):
        moved = xor_permute(text.astype(jnp.bfloat16), stride)
        text = text.astype(jnp.float32) + moved.astype(jnp.float32)
    return text.astype(jnp.bfloat16)


def halo_cuts(tok_rows, halo):
    cuts = []
    left = halo
    while left > 0:
        cuts.append(min(left, tok_rows))
        left -= cuts[-1]
    return cuts


def halo_pairs(step, tok_rows):
    first = PREFIX // tok_rows
    return [(at, at + step) for at in range(first, lax.axis_size("ctx") - step)]


def halo_rows(tail, halo, tok_rows):
    parts = []
    for step, count in enumerate(halo_cuts(tok_rows, halo), 1):
        pairs = halo_pairs(step, tok_rows)
        rows = tail if count == tail.shape[1] else tail[:, tail.shape[1] - count :]
        parts.insert(0, lax.ppermute(rows, "ctx", pairs))
    return jnp.concatenate(parts, axis=1) if len(parts) > 1 else parts[0]


def halo_parts(d_halo, tok_rows):
    cuts = halo_cuts(tok_rows, d_halo.shape[1])
    parts = []
    end = d_halo.shape[1]
    for step, count in enumerate(cuts, 1):
        rows = d_halo if len(cuts) == 1 else d_halo[:, end - count : end]
        parts.append((rows, [(target, at) for at, target in halo_pairs(step, tok_rows)]))
        end -= count
    return parts


def last_kernel(part_count, vis_ref, dkv_ref, down_ref, *refs):
    text_refs, refs = refs[:4], refs[4:]
    part_refs = refs[:part_count]
    *dq_refs, image_ref, kv_ref = refs[part_count:]
    here = lax.axis_index("ctx")
    tok_rows = down_ref.shape[1]
    at = 0
    for dq_ref in dq_refs:
        image_ref[0, at : at + dq_ref.shape[0], :Q_WIDTH] = dq_ref[...]
        at += dq_ref.shape[0]
    image_ref[0, :, Q_WIDTH : Q_WIDTH + KV_WIDTH] = dkv_ref[0]
    image_ref[0, :, Q_WIDTH + KV_WIDTH :] = dkv_ref[1]
    at = lax.broadcasted_iota(jnp.int32, (PROMPT, KV_WIDTH), 0)
    ahead = jnp.where(here == 0, 1, 0)
    behind = jnp.where(here == VIS // tok_rows, 1, 0)
    kept = jnp.where(at < vis_ref[0], ahead, behind) == 1
    for part in range(2):
        text = text_refs[part][...].astype(jnp.float32)
        text = text + text_refs[2 + part][...].astype(jnp.float32)
        text = jnp.where(kept, text, 0.0)
        sums = down_ref[part] + jnp.concatenate(
            [text, jnp.zeros((tok_rows - PROMPT, KV_WIDTH), jnp.float32)], axis=0
        )
        for part_ref in part_refs:
            back = part_ref[part].astype(jnp.float32)
            if back.shape[0] < tok_rows:
                missing = jnp.zeros((tok_rows - back.shape[0], KV_WIDTH), jnp.float32)
                back = jnp.concatenate([missing, back], axis=0)
            sums = sums + back
        kv_ref[0, part] = sums.astype(jnp.bfloat16)


def last_arrays(vis_start, image_dq, image_dkv, d_own_kv, texts, parts):
    rows = image_dkv.shape[1]
    smem = pl.BlockSpec(memory_space=pltpu.SMEM)
    vmem = pl.BlockSpec(memory_space=pltpu.VMEM)
    return pl.pallas_call(
        functools.partial(last_kernel, len(parts)),
        in_specs=[smem] + [vmem] * (6 + len(parts) + len(image_dq)),
        out_specs=[vmem, vmem],
        out_shape=[
            jax.ShapeDtypeStruct((1, rows, Q_WIDTH + 2 * KV_WIDTH), jnp.bfloat16),
            jax.ShapeDtypeStruct((1,) + d_own_kv.shape, jnp.bfloat16),
        ],
    )(vis_start, image_dkv, d_own_kv, *texts, *parts, *image_dq)


def gather_queries(image_q):
    every = lax.all_gather(image_q, "rollout", axis=0)
    missing = IMAGE_BLOCK - every.shape[1]
    return jnp.pad(every, ((0, 0), (0, missing), (0, 0))) if missing else every


def per_device(queries, keys_values, image_rows, cotangent, seq_image, vis_start, comp_lengths):
    tok_rows = queries.shape[1]
    image_count = image_rows.shape[1]
    ctx_size = lax.axis_size("ctx")
    seq_len = tok_rows * ctx_size
    late_shard = VIS // tok_rows
    longest = 4 * (seq_len - PREFIX) // (3 * NCOMP)
    halo = -(-(longest - 1) // 64) * 64
    q_own, d_own = queries[0], cotangent[0]

    number, image_kv, image_q, text, tail = first_arrays(
        seq_image, vis_start, image_rows, keys_values, halo
    )
    every_q = gather_queries(image_q)
    image_kv, swapped = route(image_kv, number, False, [(text, xor_pairs(late_shard))])
    image_kv, d_later = lax.optimization_barrier((image_kv, d_own))
    windows, rounds, (*masks, text) = second_arrays(
        vis_start, comp_lengths, d_later, image_kv, text, swapped, halo
    )
    blocks, texts = gather_prefix(image_kv, text, late_shard)
    windows = image_windows(windows, rounds)
    halo_kv = halo_rows(tail, halo, tok_rows)

    grad_q, *d_image_q, d_mine, d_pair, d_halo, d_own_kv = attend(
        number,
        masks,
        q_own,
        d_own,
        every_q,
        halo_kv,
        keys_values,
        blocks,
        [] if ctx_size == 8 else texts,
        windows,
    )

    d_image_q = [
        half[: image_count - at * IMAGE_HALF]
        for at, half in enumerate(d_image_q)
        if at * IMAGE_HALF < image_count
    ]
    image_dq, other, *halo_back = route(
        d_image_q[0], number, True, [(d_pair, xor_pairs(1))] + halo_parts(d_halo, tok_rows)
    )
    image_dq = [image_dq]
    steps = chip_steps(ctx_size)
    own, *sent, keys_text, values_text = on_device(
        functools.partial(split_sums, image_count, steps), d_mine, d_pair, other
    )
    beside = [(rows, xor_pairs(step)) for rows, step in zip(sent, steps)]
    if len(d_image_q) > 1:
        second, *moved = route(d_image_q[1], number, True, beside)
        image_dq.append(second)
    else:
        moved = [lax.ppermute(rows, "ctx", pairs) for rows, pairs in beside]
    sums, keys_text, values_text = on_device(
        functools.partial(add_sums, image_count), own, keys_text, values_text, *moved
    )
    if ctx_size != 8:
        keys_text = collect_text(keys_text, late_shard)
        values_text = collect_text(values_text, late_shard)
    keys_step = late_shard
    values_step = 4 if ctx_size == 8 else late_shard
    image_dkv, *other_texts = route(
        sums,
        number,
        True,
        [(keys_text, xor_pairs(keys_step)), (values_text, xor_pairs(values_step))],
    )
    grad_image, grad_kv = last_arrays(
        vis_start,
        image_dq,
        image_dkv,
        d_own_kv,
        [keys_text, values_text, *other_texts],
        halo_back,
    )
    return (grad_q[None], grad_kv, grad_image)


def solution(mesh):
    placed = (
        P("rollout", "ctx", None),
        P("rollout", None, "ctx", None),
        P("rollout", "ctx", None),
        P("rollout", "ctx", None),
        P(),
        P("rollout"),
        P("rollout", None),
    )
    return jax.shard_map(
        per_device,
        mesh=mesh,
        in_specs=placed,
        out_specs=(
            P("rollout", "ctx", None),
            P("rollout", None, "ctx", None),
            P("rollout", "ctx", None),
        ),
        check_vma=False,
    )
```

```python
import functools
import itertools
import math

import jax
import jax.numpy as jnp
from jax import lax
from jax.experimental import pallas as pl
from jax.experimental.pallas import tpu as pltpu
from jax.sharding import PartitionSpec as P

HEADS = 32
KV_HEADS = 8
HEAD_DIM = 128
VIS = 256
PROMPT = 64
NCOMP = 16

RATIO = HEADS // KV_HEADS
PREFIX = VIS + PROMPT
Q_WIDTH = HEADS * HEAD_DIM
KV_WIDTH = KV_HEADS * HEAD_DIM
GROUP_WIDTH = RATIO * HEAD_DIM
IMAGE_BLOCK = 32
IMAGE_HALF = IMAGE_BLOCK // 2
KEY_CHUNK = 32
HIDDEN = -1e30
SCORE_SCALE = 1.0 / math.sqrt(HEAD_DIM)


def dot_nt(left, right):
    return lax.dot_general(
        left, right, (((1,), (1,)), ((), ())), preferred_element_type=jnp.float32
    )


def dot_nn(left, right):
    return lax.dot_general(
        left, right, (((1,), (0,)), ((), ())), preferred_element_type=jnp.float32
    )


def dot_tn(left, right):
    return lax.dot_general(
        left, right, (((0,), (0,)), ((), ())), preferred_element_type=jnp.float32
    )


def first_kernel(halo, seq_ref, vis_ref, image_ref, kv_ref, number_ref, *out_refs):
    ikv_ref, iq_ref, text_ref, tail_ref = out_refs
    groups = seq_ref.shape[0]
    group = lax.axis_index("rollout")
    here = lax.axis_index("ctx")
    images = [seq_ref[at] for at in range(groups)]
    number = jnp.int32(0)
    if groups == 4:
        for at, weight in enumerate((6, 2, 1)):
            for later in range(at + 1, groups):
                number = number + jnp.where(images[later] < images[at], weight, 0)
    place = jnp.int32(0)
    user = jnp.int32(0)
    for at in range(groups):
        place = place + jnp.where(group == at, images[at], 0)
        user = user + jnp.where(images[at] == group, at, 0)
    number_ref[0] = number
    number_ref[1] = place
    number_ref[2] = user
    iq_ref[...] = image_ref[0, :, :Q_WIDTH]
    ikv_ref[0] = image_ref[0, :, Q_WIDTH : Q_WIDTH + KV_WIDTH]
    ikv_ref[1] = image_ref[0, :, Q_WIDTH + KV_WIDTH :]
    tok_rows = kv_ref.shape[2]
    late_shard = VIS // tok_rows
    at = lax.broadcasted_iota(jnp.int32, (PROMPT, KV_WIDTH), 0)
    ahead = jnp.where(here == 0, 1, 0)
    behind = jnp.where(here == late_shard, 1, 0)
    kept = jnp.where(at < vis_ref[0], ahead, behind) == 1
    for part in range(2):
        rows = kv_ref[0, part, :PROMPT].astype(jnp.float32)
        text_ref[part] = jnp.where(kept, rows, 0.0).astype(jnp.bfloat16)
        tail_ref[part] = kv_ref[0, part, tok_rows - halo :]


def first_arrays(seq_image, vis_start, image_rows, keys_values, halo):
    rows = image_rows.shape[1]
    smem = pl.BlockSpec(memory_space=pltpu.SMEM)
    vmem = pl.BlockSpec(memory_space=pltpu.VMEM)
    tail = min(halo, keys_values.shape[2])
    return pl.pallas_call(
        functools.partial(first_kernel, tail),
        in_specs=[smem, smem, vmem, vmem],
        out_specs=[smem, vmem, vmem, vmem, vmem],
        out_shape=[
            jax.ShapeDtypeStruct((3,), jnp.int32),
            jax.ShapeDtypeStruct((2, rows, KV_WIDTH), jnp.bfloat16),
            jax.ShapeDtypeStruct((rows, Q_WIDTH), jnp.bfloat16),
            jax.ShapeDtypeStruct((2, PROMPT, KV_WIDTH), jnp.bfloat16),
            jax.ShapeDtypeStruct((2, tail, KV_WIDTH), jnp.bfloat16),
        ],
    )(seq_image, vis_start, image_rows, keys_values)


def segments(positions, length_ref):
    end = jnp.int32(PREFIX)
    segment = jnp.where(positions < PREFIX, 0, 1)
    for at in range(NCOMP):
        end = end + length_ref[0, at]
        segment = segment + jnp.where(positions >= end, 1, 0)
    return segment


def hide(visible):
    return jnp.where(visible, 0.0, HIDDEN)


def second_kernel(
    rounds, tok_rows, image_rows, halo, vis_ref, length_ref, d_ref, kv_ref, t_ref, r_ref, *out_refs
):
    *window_refs, near_ref, whole_ref, image_ref, text_ref = out_refs
    here = lax.axis_index("ctx")
    ctx_size = lax.axis_size("ctx")
    row = lax.broadcasted_iota(jnp.int32, (IMAGE_BLOCK, tok_rows), 0)
    column = lax.broadcasted_iota(jnp.int32, (IMAGE_BLOCK, tok_rows), 1)
    place = jnp.where(row < image_rows, row, 1 << 20)
    picks = []
    for pairs in [[]] + rounds:
        target = here
        for source, other in pairs:
            target = jnp.where(here == source, other, target)
        begin = vis_ref[0] + image_rows * target - tok_rows * here
        picks.append(jnp.where(column == place + begin, 1.0, 0.0).astype(jnp.bfloat16))
    picked = dot_nn(jnp.concatenate(picks, axis=0), d_ref[...]).astype(jnp.bfloat16)
    for at, window_ref in enumerate(window_refs):
        window_ref[...] = picked[at * IMAGE_BLOCK : (at + 1) * IMAGE_BLOCK]

    @pl.when(pl.program_id(0) == 0)
    def _():
        vis = vis_ref[0]
        text = t_ref[...].astype(jnp.float32) + r_ref[...].astype(jnp.float32)
        if kv_ref.shape[1] == IMAGE_BLOCK:
            text_ref[:, :IMAGE_BLOCK] = kv_ref[...]
        text_ref[:, text_ref.shape[1] - PROMPT :] = text.astype(jnp.bfloat16)
        own_at = lax.broadcasted_iota(jnp.int32, (8, tok_rows), 1) + here * tok_rows
        own_segment = segments(own_at, length_ref)[:1]
        placeholder = (own_at >= vis) & (own_at < vis + VIS)
        own_row = jnp.where(placeholder, -1, own_at)
        whole_ref[...] = hide(own_row >= vis + VIS).astype(jnp.float32)
        own_row = own_row[:1]
        image_at = lax.broadcasted_iota(jnp.int32, (1, RATIO * IMAGE_BLOCK), 1) % IMAGE_BLOCK
        image_row = jnp.where(image_at < image_rows, vis + here * image_rows + image_at, -1)
        text_at = lax.broadcasted_iota(jnp.int32, (PROMPT, tok_rows), 0)
        text_at = text_at + jnp.where(text_at < vis, 0, VIS)
        near_ref[:PROMPT] = hide(text_at <= own_row)
        near_at = lax.broadcasted_iota(jnp.int32, (halo + tok_rows, tok_rows), 0)
        near_at = near_at + (here * tok_rows - halo)
        sees = (near_at <= own_row) & (near_at >= PREFIX)
        sees = sees & (segments(near_at, length_ref) == own_segment)
        near_ref[PROMPT:] = hide(sees)
        at = 0
        for core in range(2):
            for step in range(0, ctx_size, 2):
                begin = (here ^ (step + core)) * image_rows + vis
                shape = (image_rows, RATIO * IMAGE_BLOCK)
                block_at = lax.broadcasted_iota(jnp.int32, shape, 0) + begin
                image_ref[at : at + image_rows] = hide(block_at <= image_row)
                at += image_rows
        image_ref[VIS:] = hide(text_at <= image_row)


def second_arrays(vis_start, lengths, cotangent, image_kv, text, received, halo):
    tok_rows, width = cotangent.shape
    image_rows = image_kv.shape[1]
    text_rows = PROMPT + (image_rows if image_rows == IMAGE_BLOCK else 0)
    rounds = window_rounds(lax.axis_size("ctx"), tok_rows, image_rows)
    count = len(rounds) + 1
    block = 2048
    spec = pl.BlockSpec
    smem = spec(memory_space=pltpu.SMEM)
    lanes = RATIO * IMAGE_BLOCK
    near = PROMPT + halo + tok_rows
    whole = lambda *shape: spec(shape, lambda at: (0,) * len(shape))
    out = pl.pallas_call(
        functools.partial(second_kernel, rounds, tok_rows, image_rows, halo),
        grid=(width // block,),
        in_specs=[
            smem,
            smem,
            spec((tok_rows, block), lambda at: (0, at)),
            whole(2, image_rows, KV_WIDTH),
            whole(2, PROMPT, KV_WIDTH),
            whole(2, PROMPT, KV_WIDTH),
        ],
        out_specs=[spec((IMAGE_BLOCK, block), lambda at: (0, at)) for _ in range(count)]
        + [
            whole(near, tok_rows),
            whole(8, tok_rows),
            whole(PREFIX, lanes),
            whole(2, text_rows, KV_WIDTH),
        ],
        out_shape=[jax.ShapeDtypeStruct((IMAGE_BLOCK, width), jnp.bfloat16) for _ in range(count)]
        + [
            jax.ShapeDtypeStruct((near, tok_rows), jnp.float32),
            jax.ShapeDtypeStruct((8, tok_rows), jnp.float32),
            jax.ShapeDtypeStruct((PREFIX, lanes), jnp.float32),
            jax.ShapeDtypeStruct((2, text_rows, KV_WIDTH), jnp.bfloat16),
        ],
    )(vis_start, lengths, cotangent, image_kv, text, received)
    return out[:count], rounds, out[count:]


def first_products(parts, q_rows, d_rows):
    return [(dot_nt(keys, q_rows), dot_nt(values, d_rows)) for keys, values, _ in parts]


def chunks_of(rows):
    return [rows[at : at + KEY_CHUNK] for at in range(0, rows.shape[0], KEY_CHUNK)]


def fold_rows(rows, combine):
    folded = rows[:8]
    for at in range(8, rows.shape[0], 8):
        folded = combine(folded, rows[at : at + 8])
    return folded


def rows_backward(parts, products):
    scale = SCORE_SCALE * math.log2(math.e)
    scores, tops = [], []
    for (keys, values, bias), (raw, _) in zip(parts, products):
        one_row = bias.shape[0] == 1
        top = None
        for at, chunk in enumerate(chunks_of(raw)):
            chunk = chunk * scale
            if not one_row:
                chunk = chunk + bias[at * KEY_CHUNK : (at + 1) * KEY_CHUNK]
            scores.append((chunk, bias if one_row else None))
            folded = fold_rows(chunk, jnp.maximum)
            top = folded if top is None else jnp.maximum(top, folded)
        top = jnp.max(top, axis=0, keepdims=True)
        tops.append(top + bias if one_row else top)
    top = functools.reduce(jnp.maximum, tops)
    d_weights = [chunk for _, product in products for chunk in chunks_of(product)]
    total = mix = None
    kept = []
    for (chunk, bias), d_chunk in zip(scores, d_weights):
        terms = jnp.exp2(chunk + ((bias if bias is not None else 0.0) - top))
        folded = fold_rows(terms, jnp.add)
        total = folded if total is None else total + folded
        folded = fold_rows(terms * d_chunk, jnp.add)
        mix = folded if mix is None else mix + folded
        kept.append(terms)
    total = jnp.sum(total, axis=0, keepdims=True)
    mix = jnp.sum(mix, axis=0, keepdims=True)
    inverse = jnp.where(top > 0.5 * HIDDEN, 1.0 / total, 0.0)
    delta = mix * inverse
    weights, d_scores = [], []
    for terms, d_chunk in zip(kept, d_weights):
        chunk = terms * inverse
        weights.append(chunk.astype(jnp.bfloat16))
        d_scores.append((chunk * (d_chunk - delta)).astype(jnp.bfloat16))
    outcome = []
    for raw, _ in products:
        count = raw.shape[0] // KEY_CHUNK
        outcome.append(
            (jnp.concatenate(weights[:count], axis=0), jnp.concatenate(d_scores[:count], axis=0))
        )
        weights, d_scores = weights[count:], d_scores[count:]
    return outcome


def total_of(values):
    if len(values) == 1:
        return values[0]
    return sum(value.astype(jnp.float32) for value in values).astype(jnp.bfloat16)


def attend_kernel(
    block_rows,
    block_count,
    text_count,
    window_count,
    heads,
    halo,
    own,
    number_ref,
    near_ref,
    whole_ref,
    image_bias_ref,
    q_ref,
    d_ref,
    iq_ref,
    halo_ref,
    own_ref,
    *refs,
):
    block_refs, refs = refs[:block_count], refs[block_count:]
    text_refs, refs = refs[:text_count], refs[text_count:]
    window_refs, refs = refs[:window_count], refs[window_count:]
    dq_ref, *diq_refs, dmine_ref, dpair_ref, dhalo_ref, down_ref = refs
    text_refs = text_refs or [ref for ref in block_refs if ref.shape[1] > block_rows]
    near_bias = jnp.concatenate([near_ref[...]] * 2, axis=1)
    whole_bias = jnp.concatenate([whole_ref[:1]] * 2, axis=1)
    image_cotangent = total_of([ref[...] for ref in window_refs])
    image_queries = iq_ref[number_ref[1]]
    states = []
    units = []
    for head in range(heads):
        lanes = slice(head * HEAD_DIM, (head + 1) * HEAD_DIM)
        spans = [
            slice((head * RATIO + at) * HEAD_DIM, (head * RATIO + at + 1) * HEAD_DIM)
            for at in range(RATIO)
        ]
        visual, text, near = [], [], []
        for part in range(2):
            visual.append(
                jnp.concatenate([ref[part, :block_rows, lanes] for ref in block_refs], axis=0)
            )
            text.append(total_of([ref[part, -PROMPT:, lanes] for ref in text_refs]))
            near.append(
                jnp.concatenate(
                    [text[part], halo_ref[part, :, lanes], own_ref[0, part, :, lanes]], axis=0
                )
            )
        states.append((lanes, jnp.concatenate([visual[0], near[0]], axis=0).T, {}))
        own_parts = [(visual[0], visual[1], whole_bias), (near[0], near[1], near_bias)]
        for first in range(0, RATIO, 2):
            units.append((head, own_parts, q_ref, d_ref, spans[first : first + 2]))
        image_parts = [
            (visual[0], visual[1], image_bias_ref[:VIS]),
            (text[0], text[1], image_bias_ref[VIS:]),
        ]
        units.append((head, image_parts, image_queries, image_cotangent, spans))

    def begin(unit):
        _, parts, queries, cotangents, unit_spans = unit
        q_rows = jnp.concatenate([queries[:, span] for span in unit_spans], axis=0)
        d_rows = jnp.concatenate([cotangents[:, span] for span in unit_spans], axis=0)
        return q_rows, d_rows, first_products(parts, q_rows, d_rows)

    def finish(unit, begun):
        head, parts, _, _, unit_spans = unit
        lanes, keys_across, sums = states[head]
        q_rows, d_rows, products = begun
        outcome = rows_backward(parts, products)
        d_scores = jnp.concatenate([part[1] for part in outcome], axis=0)
        dq = dot_nn(keys_across[:, : d_scores.shape[0]], d_scores) * SCORE_SCALE
        dq = dq.astype(jnp.bfloat16).T
        rows = dq.shape[0] // len(unit_spans)
        for at, span in enumerate(unit_spans):
            if len(unit_spans) == 2:
                dq_ref[:, span] = dq[at * rows : (at + 1) * rows]
            else:
                for half, out_ref in enumerate(diq_refs):
                    place = at * rows + half * IMAGE_HALF
                    out_ref[:, span] = dq[place : place + IMAGE_HALF]
        for at, (weights, d_part) in enumerate(outcome):
            for kind, rows in ((0, dot_nn(d_part, q_rows)), (1, dot_nn(weights, d_rows))):
                count = rows.shape[0]
                earlier = sums.get((kind, at))
                if earlier is not None and count < earlier.shape[0]:
                    rows = jnp.concatenate([earlier[:count] + rows, earlier[count:]], axis=0)
                elif earlier is not None:
                    rows = earlier + rows
                sums[kind, at] = rows
        if len(unit_spans) == 2:
            return
        for part, scale in ((0, SCORE_SCALE), (1, 1.0)):
            of_visual = (sums[part, 0] * scale).astype(jnp.bfloat16)
            rest = sums[part, 1] * scale
            dmine_ref[part, :, lanes] = of_visual[: VIS // 2]
            dpair_ref[part, : VIS // 2, lanes] = of_visual[VIS // 2 :]
            dpair_ref[part, VIS // 2 :, lanes] = rest[:PROMPT].astype(jnp.bfloat16)
            dhalo_ref[part, :, lanes] = rest[PROMPT : PROMPT + halo].astype(jnp.bfloat16)
            down_ref[part, :, lanes] = rest[PROMPT + halo :]

    begun = begin(units[0])
    for at, unit in enumerate(units):
        later = begin(units[at + 1]) if at + 1 < len(units) else None
        finish(unit, begun)
        begun = later


def attend(
    number, masks, queries, cotangent, every_q, halo_kv, own_kv, blocks, texts, windows
):
    heads = 2
    near_bias, whole_bias, image_bias = masks
    own = queries.shape[0]
    halo = halo_kv.shape[1]
    groups = every_q.shape[0]
    columns = PREFIX + halo + own
    products = RATIO * (own * columns + IMAGE_BLOCK * PREFIX) * KV_HEADS
    spec = pl.BlockSpec
    kv_spec = lambda rows: spec((2, rows, heads * HEAD_DIM), lambda at: (0, 0, at))
    q_spec = lambda rows: spec((rows, heads * GROUP_WIDTH), lambda at: (0, at))
    whole = lambda rows: spec((rows, 128), lambda at: (0, 0))
    return pl.pallas_call(
        functools.partial(
            attend_kernel,
            VIS // len(blocks),
            len(blocks),
            len(texts),
            len(windows),
            heads,
            halo,
            own,
        ),
        grid=(KV_HEADS // heads,),
        in_specs=[
            spec(memory_space=pltpu.SMEM),
            whole(columns - VIS),
            whole(8),
            whole(PREFIX),
            q_spec(own),
            q_spec(own),
            spec((groups, IMAGE_BLOCK, heads * GROUP_WIDTH), lambda at: (0, 0, at)),
            kv_spec(halo),
            spec((1, 2, own, heads * HEAD_DIM), lambda at: (0, 0, 0, at)),
        ]
        + [kv_spec(block.shape[1]) for block in [*blocks, *texts]]
        + [q_spec(IMAGE_BLOCK) for _ in windows],
        out_specs=[
            q_spec(own),
            q_spec(IMAGE_HALF),
            q_spec(IMAGE_HALF),
            kv_spec(VIS // 2),
            kv_spec(VIS // 2 + PROMPT),
            kv_spec(halo),
            kv_spec(own),
        ],
        out_shape=[
            jax.ShapeDtypeStruct((own, Q_WIDTH), jnp.bfloat16),
            jax.ShapeDtypeStruct((IMAGE_HALF, Q_WIDTH), jnp.bfloat16),
            jax.ShapeDtypeStruct((IMAGE_HALF, Q_WIDTH), jnp.bfloat16),
            jax.ShapeDtypeStruct((2, VIS // 2, KV_WIDTH), jnp.bfloat16),
            jax.ShapeDtypeStruct((2, VIS // 2 + PROMPT, KV_WIDTH), jnp.bfloat16),
            jax.ShapeDtypeStruct((2, halo, KV_WIDTH), jnp.bfloat16),
            jax.ShapeDtypeStruct((2, own, KV_WIDTH), jnp.float32),
        ],
        cost_estimate=pl.CostEstimate(
            flops=10 * products * HEAD_DIM,
            bytes_accessed=12 * 1024 * 1024,
            transcendentals=products,
        ),
    )(
        number,
        near_bias,
        whole_bias,
        image_bias,
        queries,
        cotangent,
        every_q,
        halo_kv,
        own_kv,
        *blocks,
        *texts,
        *windows,
    )


def route(rows, number, back, beside=()):
    groups = lax.axis_size("rollout")
    arrays = [array for array, _ in beside]

    def move_beside(arrays):
        return [lax.ppermute(array, "ctx", pairs) for array, (_, pairs) in zip(arrays, beside)]

    if groups != 4:
        every = lax.all_gather(rows, "rollout", axis=0)
        picked = lax.dynamic_index_in_dim(every, number[2 if back else 1], 0, keepdims=False)
        return [picked] + move_beside(arrays)

    def branch(images):
        pairs = [(g, i) if back else (i, g) for g, i in enumerate(images)]
        if all(source == target for source, target in pairs):
            return lambda rows, arrays: [rows] + move_beside(arrays)
        return lambda rows, arrays: [lax.ppermute(rows, "rollout", pairs)] + move_beside(arrays)

    orders = itertools.permutations(range(groups))
    return lax.switch(number[0], [branch(images) for images in orders], rows, arrays)


def window_rounds(ctx_size, tok_rows, image_rows):
    rounds = []
    for target in range(ctx_size):
        lowest = (image_rows * target + 1) // tok_rows
        highest = (image_rows * target + image_rows - 1 + PROMPT - 1) // tok_rows
        for source in range(lowest, highest + 1):
            if source == target:
                continue
            for pairs in rounds:
                if all(s != source and t != target for s, t in pairs):
                    pairs.append((source, target))
                    break
            else:
                rounds.append([(source, target)])
    return rounds


def image_windows(windows, rounds):
    parts = [windows[0]] + [
        lax.ppermute(rows, "ctx", pairs) for rows, pairs in zip(windows[1:], rounds)
    ]
    if len(parts) > 8:
        parts = [sum(part.astype(jnp.float32) for part in parts).astype(jnp.bfloat16)]
    return parts


def xor_pairs(step):
    return [(at, at ^ step) for at in range(lax.axis_size("ctx"))]


def xor_permute(rows, step):
    return lax.ppermute(rows, "ctx", xor_pairs(step))


def on_device(function, *arrays):
    if lax.axis_size("ctx") != 8:
        return function(*arrays)
    shapes = jax.eval_shape(function, *arrays)

    def kernel(*refs):
        for out_ref, value in zip(
            refs[len(arrays) :], function(*[ref[...] for ref in refs[: len(arrays)]])
        ):
            out_ref[...] = value

    def spec(array):
        *rows, width = array.shape
        return pl.BlockSpec((*rows, width // 2), lambda at: (0,) * len(rows) + (at,))

    return pl.pallas_call(
        kernel,
        grid=(2,),
        in_specs=[spec(array) for array in arrays],
        out_specs=[spec(shape) for shape in shapes],
        out_shape=[jax.ShapeDtypeStruct(shape.shape, shape.dtype) for shape in shapes],
        cost_estimate=pl.CostEstimate(flops=1, bytes_accessed=1, transcendentals=0),
    )(*arrays)


def text_strides(ctx_size, late_shard):
    strides = [1 << at for at in range(1, ctx_size.bit_length() - 1)]
    return [stride for stride in reversed(strides) if stride != late_shard]


def chip_steps(ctx_size):
    return list(range(2, ctx_size, 2))


def gather_prefix(image_kv, text, late_shard):
    ctx_size = lax.axis_size("ctx")
    steps = chip_steps(ctx_size)
    if ctx_size == 8:
        mine = [text, xor_permute(image_kv, 2), xor_permute(text, 4), xor_permute(image_kv, 6)]
        blocks = mine + [xor_permute(block, 1) for block in mine]
        return blocks, [blocks[at] for at in (0, 2, 4, 6)]
    mine = jnp.concatenate(
        [image_kv] + [xor_permute(image_kv, step) for step in steps], axis=1
    )
    return [mine, xor_permute(mine, 1)], list(spread_text(text, late_shard))


def split_sums(image_rows, steps, d_mine, d_pair, other):
    half = VIS // 2
    add = lambda one, two: one.astype(jnp.float32) + two.astype(jnp.float32)
    text = add(d_pair[:, half:], other[:, half:])
    out = []
    for at in range(len(steps) + 1):
        rows = slice(at * image_rows, (at + 1) * image_rows)
        sums = add(d_mine[:, rows], other[:, rows])
        if len(steps) == 3 and at in (1, 2):
            halves = text[2 - at]
            halves = jnp.stack([halves[: PROMPT // 2], halves[PROMPT // 2 :]])
            sums = jnp.concatenate([sums, halves], axis=1)
        out.append(sums.astype(jnp.bfloat16) if at else sums)
    return out + [text[0], text[1]]


def add_sums(image_rows, own, keys_text, values_text, *parts):
    texts = [values_text, keys_text]
    for at, part in enumerate(parts):
        own = own + part[:, :image_rows].astype(jnp.float32)
        if part.shape[1] > image_rows:
            rows = part[:, image_rows:].astype(jnp.float32)
            texts[at] = texts[at] + jnp.concatenate([rows[0], rows[1]], axis=0)
    return [part.astype(jnp.bfloat16) for part in (own, texts[1], texts[0])]


def spread_text(text, late_shard):
    for stride in text_strides(lax.axis_size("ctx"), late_shard):
        text = text + xor_permute(text, stride)
    return text, xor_permute(text, 1)


def collect_text(text, late_shard):
    for stride in reversed(text_strides(lax.axis_size("ctx"), late_shard)):
        moved = xor_permute(text.astype(jnp.bfloat16), stride)
        text = text.astype(jnp.float32) + moved.astype(jnp.float32)
    return text.astype(jnp.bfloat16)


def halo_cuts(tok_rows, halo):
    cuts = []
    left = halo
    while left > 0:
        cuts.append(min(left, tok_rows))
        left -= cuts[-1]
    return cuts


def halo_pairs(step, tok_rows):
    first = PREFIX // tok_rows
    return [(at, at + step) for at in range(first, lax.axis_size("ctx") - step)]


def halo_rows(tail, halo, tok_rows):
    parts = []
    for step, count in enumerate(halo_cuts(tok_rows, halo), 1):
        pairs = halo_pairs(step, tok_rows)
        rows = tail if count == tail.shape[1] else tail[:, tail.shape[1] - count :]
        parts.insert(0, lax.ppermute(rows, "ctx", pairs))
    return jnp.concatenate(parts, axis=1) if len(parts) > 1 else parts[0]


def halo_parts(d_halo, tok_rows):
    cuts = halo_cuts(tok_rows, d_halo.shape[1])
    parts = []
    end = d_halo.shape[1]
    for step, count in enumerate(cuts, 1):
        rows = d_halo if len(cuts) == 1 else d_halo[:, end - count : end]
        parts.append((rows, [(target, at) for at, target in halo_pairs(step, tok_rows)]))
        end -= count
    return parts


def last_kernel(part_count, vis_ref, dkv_ref, down_ref, *refs):
    text_refs, refs = refs[:4], refs[4:]
    part_refs = refs[:part_count]
    *dq_refs, image_ref, kv_ref = refs[part_count:]
    here = lax.axis_index("ctx")
    tok_rows = down_ref.shape[1]
    at = 0
    for dq_ref in dq_refs:
        image_ref[0, at : at + dq_ref.shape[0], :Q_WIDTH] = dq_ref[...]
        at += dq_ref.shape[0]
    image_ref[0, :, Q_WIDTH : Q_WIDTH + KV_WIDTH] = dkv_ref[0]
    image_ref[0, :, Q_WIDTH + KV_WIDTH :] = dkv_ref[1]
    at = lax.broadcasted_iota(jnp.int32, (PROMPT, KV_WIDTH), 0)
    ahead = jnp.where(here == 0, 1, 0)
    behind = jnp.where(here == VIS // tok_rows, 1, 0)
    kept = jnp.where(at < vis_ref[0], ahead, behind) == 1
    for part in range(2):
        text = text_refs[part][...].astype(jnp.float32)
        text = text + text_refs[2 + part][...].astype(jnp.float32)
        text = jnp.where(kept, text, 0.0)
        sums = down_ref[part] + jnp.concatenate(
            [text, jnp.zeros((tok_rows - PROMPT, KV_WIDTH), jnp.float32)], axis=0
        )
        for part_ref in part_refs:
            back = part_ref[part].astype(jnp.float32)
            if back.shape[0] < tok_rows:
                missing = jnp.zeros((tok_rows - back.shape[0], KV_WIDTH), jnp.float32)
                back = jnp.concatenate([missing, back], axis=0)
            sums = sums + back
        kv_ref[0, part] = sums.astype(jnp.bfloat16)


def last_arrays(vis_start, image_dq, image_dkv, d_own_kv, texts, parts):
    rows = image_dkv.shape[1]
    smem = pl.BlockSpec(memory_space=pltpu.SMEM)
    vmem = pl.BlockSpec(memory_space=pltpu.VMEM)
    return pl.pallas_call(
        functools.partial(last_kernel, len(parts)),
        in_specs=[smem] + [vmem] * (6 + len(parts) + len(image_dq)),
        out_specs=[vmem, vmem],
        out_shape=[
            jax.ShapeDtypeStruct((1, rows, Q_WIDTH + 2 * KV_WIDTH), jnp.bfloat16),
            jax.ShapeDtypeStruct((1,) + d_own_kv.shape, jnp.bfloat16),
        ],
    )(vis_start, image_dkv, d_own_kv, *texts, *parts, *image_dq)


def gather_queries(image_q):
    every = lax.all_gather(image_q, "rollout", axis=0)
    missing = IMAGE_BLOCK - every.shape[1]
    return jnp.pad(every, ((0, 0), (0, missing), (0, 0))) if missing else every


def per_device(queries, keys_values, image_rows, cotangent, seq_image, vis_start, comp_lengths):
    tok_rows = queries.shape[1]
    image_count = image_rows.shape[1]
    ctx_size = lax.axis_size("ctx")
    seq_len = tok_rows * ctx_size
    late_shard = VIS // tok_rows
    longest = 4 * (seq_len - PREFIX) // (3 * NCOMP)
    halo = -(-(longest - 1) // 64) * 64
    q_own, d_own = queries[0], cotangent[0]

    number, image_kv, image_q, text, tail = first_arrays(
        seq_image, vis_start, image_rows, keys_values, halo
    )
    every_q = gather_queries(image_q)
    image_kv, swapped = route(image_kv, number, False, [(text, xor_pairs(late_shard))])
    image_kv, d_later = lax.optimization_barrier((image_kv, d_own))
    windows, rounds, (*masks, text) = second_arrays(
        vis_start, comp_lengths, d_later, image_kv, text, swapped, halo
    )
    blocks, texts = gather_prefix(image_kv, text, late_shard)
    windows = image_windows(windows, rounds)
    halo_kv = halo_rows(tail, halo, tok_rows)

    grad_q, *d_image_q, d_mine, d_pair, d_halo, d_own_kv = attend(
        number,
        masks,
        q_own,
        d_own,
        every_q,
        halo_kv,
        keys_values,
        blocks,
        [] if ctx_size == 8 else texts,
        windows,
    )

    d_image_q = [
        half[: image_count - at * IMAGE_HALF]
        for at, half in enumerate(d_image_q)
        if at * IMAGE_HALF < image_count
    ]
    image_dq, other, *halo_back = route(
        d_image_q[0], number, True, [(d_pair, xor_pairs(1))] + halo_parts(d_halo, tok_rows)
    )
    image_dq = [image_dq]
    steps = chip_steps(ctx_size)
    own, *sent, keys_text, values_text = on_device(
        functools.partial(split_sums, image_count, steps), d_mine, d_pair, other
    )
    beside = [(rows, xor_pairs(step)) for rows, step in zip(sent, steps)]
    if len(d_image_q) > 1:
        second, *moved = route(d_image_q[1], number, True, beside)
        image_dq.append(second)
    else:
        moved = [lax.ppermute(rows, "ctx", pairs) for rows, pairs in beside]
    sums, keys_text, values_text = on_device(
        functools.partial(add_sums, image_count), own, keys_text, values_text, *moved
    )
    if ctx_size != 8:
        keys_text = collect_text(keys_text, late_shard)
        values_text = collect_text(values_text, late_shard)
    keys_step = late_shard
    values_step = 4 if ctx_size == 8 else late_shard
    image_dkv, *other_texts = route(
        sums,
        number,
        True,
        [(keys_text, xor_pairs(keys_step)), (values_text, xor_pairs(values_step))],
    )
    grad_image, grad_kv = last_arrays(
        vis_start,
        image_dq,
        image_dkv,
        d_own_kv,
        [keys_text, values_text, *other_texts],
        halo_back,
    )
    return (grad_q[None], grad_kv, grad_image)


def solution(mesh):
    placed = (
        P("rollout", "ctx", None),
        P("rollout", None, "ctx", None),
        P("rollout", "ctx", None),
        P("rollout", "ctx", None),
        P(),
        P("rollout"),
        P("rollout", None),
    )
    return jax.shard_map(
        per_device,
        mesh=mesh,
        in_specs=placed,
        out_specs=(
            P("rollout", "ctx", None),
            P("rollout", None, "ctx", None),
            P("rollout", "ctx", None),
        ),
        check_vma=False,
    )
```

```python
import functools
import itertools
import math

import jax
import jax.numpy as jnp
from jax import lax
from jax.experimental import pallas as pl
from jax.experimental.pallas import tpu as pltpu
from jax.sharding import PartitionSpec as P

HEADS = 32
KV_HEADS = 8
HEAD_DIM = 128
VIS = 256
PROMPT = 64
NCOMP = 16

RATIO = HEADS // KV_HEADS
PREFIX = VIS + PROMPT
Q_WIDTH = HEADS * HEAD_DIM
KV_WIDTH = KV_HEADS * HEAD_DIM
GROUP_WIDTH = RATIO * HEAD_DIM
IMAGE_BLOCK = 32
IMAGE_HALF = IMAGE_BLOCK // 2
KEY_CHUNK = 128
HIDDEN = -1e30
SCORE_SCALE = 1.0 / math.sqrt(HEAD_DIM)


def dot_nt(left, right):
    return lax.dot_general(
        left, right, (((1,), (1,)), ((), ())), preferred_element_type=jnp.float32
    )


def dot_nn(left, right):
    return lax.dot_general(
        left, right, (((1,), (0,)), ((), ())), preferred_element_type=jnp.float32
    )


def dot_tn(left, right):
    return lax.dot_general(
        left, right, (((0,), (0,)), ((), ())), preferred_element_type=jnp.float32
    )


def first_kernel(halo, seq_ref, vis_ref, image_ref, kv_ref, number_ref, *out_refs):
    ikv_ref, iq_ref, text_ref, tail_ref = out_refs
    groups = seq_ref.shape[0]
    group = lax.axis_index("rollout")
    here = lax.axis_index("ctx")
    images = [seq_ref[at] for at in range(groups)]
    number = jnp.int32(0)
    if groups == 4:
        for at, weight in enumerate((6, 2, 1)):
            for later in range(at + 1, groups):
                number = number + jnp.where(images[later] < images[at], weight, 0)
    place = jnp.int32(0)
    user = jnp.int32(0)
    for at in range(groups):
        place = place + jnp.where(group == at, images[at], 0)
        user = user + jnp.where(images[at] == group, at, 0)
    number_ref[0] = number
    number_ref[1] = place
    number_ref[2] = user
    iq_ref[...] = image_ref[0, :, :Q_WIDTH]
    ikv_ref[0] = image_ref[0, :, Q_WIDTH : Q_WIDTH + KV_WIDTH]
    ikv_ref[1] = image_ref[0, :, Q_WIDTH + KV_WIDTH :]
    tok_rows = kv_ref.shape[2]
    late_shard = VIS // tok_rows
    at = lax.broadcasted_iota(jnp.int32, (PROMPT, KV_WIDTH), 0)
    ahead = jnp.where(here == 0, 1, 0)
    behind = jnp.where(here == late_shard, 1, 0)
    kept = jnp.where(at < vis_ref[0], ahead, behind) == 1
    for part in range(2):
        rows = kv_ref[0, part, :PROMPT].astype(jnp.float32)
        text_ref[part] = jnp.where(kept, rows, 0.0).astype(jnp.bfloat16)
        tail_ref[part] = kv_ref[0, part, tok_rows - halo :]


def first_arrays(seq_image, vis_start, image_rows, keys_values, halo):
    rows = image_rows.shape[1]
    smem = pl.BlockSpec(memory_space=pltpu.SMEM)
    vmem = pl.BlockSpec(memory_space=pltpu.VMEM)
    tail = min(halo, keys_values.shape[2])
    return pl.pallas_call(
        functools.partial(first_kernel, tail),
        in_specs=[smem, smem, vmem, vmem],
        out_specs=[smem, vmem, vmem, vmem, vmem],
        out_shape=[
            jax.ShapeDtypeStruct((3,), jnp.int32),
            jax.ShapeDtypeStruct((2, rows, KV_WIDTH), jnp.bfloat16),
            jax.ShapeDtypeStruct((rows, Q_WIDTH), jnp.bfloat16),
            jax.ShapeDtypeStruct((2, PROMPT, KV_WIDTH), jnp.bfloat16),
            jax.ShapeDtypeStruct((2, tail, KV_WIDTH), jnp.bfloat16),
        ],
    )(seq_image, vis_start, image_rows, keys_values)


def segments(positions, length_ref):
    end = jnp.int32(PREFIX)
    segment = jnp.where(positions < PREFIX, 0, 1)
    for at in range(NCOMP):
        end = end + length_ref[0, at]
        segment = segment + jnp.where(positions >= end, 1, 0)
    return segment


def hide(visible):
    return jnp.where(visible, 0.0, HIDDEN)


def second_kernel(
    rounds, tok_rows, image_rows, halo, vis_ref, length_ref, d_ref, kv_ref, t_ref, r_ref, *out_refs
):
    *window_refs, near_ref, whole_ref, image_ref, text_ref = out_refs
    here = lax.axis_index("ctx")
    ctx_size = lax.axis_size("ctx")
    row = lax.broadcasted_iota(jnp.int32, (IMAGE_BLOCK, tok_rows), 0)
    column = lax.broadcasted_iota(jnp.int32, (IMAGE_BLOCK, tok_rows), 1)
    place = jnp.where(row < image_rows, row, 1 << 20)
    picks = []
    for pairs in [[]] + rounds:
        target = here
        for source, other in pairs:
            target = jnp.where(here == source, other, target)
        begin = vis_ref[0] + image_rows * target - tok_rows * here
        picks.append(jnp.where(column == place + begin, 1.0, 0.0).astype(jnp.bfloat16))
    picked = dot_nn(jnp.concatenate(picks, axis=0), d_ref[...]).astype(jnp.bfloat16)
    for at, window_ref in enumerate(window_refs):
        window_ref[...] = picked[at * IMAGE_BLOCK : (at + 1) * IMAGE_BLOCK]

    @pl.when(pl.program_id(0) == 0)
    def _():
        vis = vis_ref[0]
        text = t_ref[...].astype(jnp.float32) + r_ref[...].astype(jnp.float32)
        if kv_ref.shape[1] == IMAGE_BLOCK:
            text_ref[:, :IMAGE_BLOCK] = kv_ref[...]
        text_ref[:, text_ref.shape[1] - PROMPT :] = text.astype(jnp.bfloat16)
        own_at = lax.broadcasted_iota(jnp.int32, (8, tok_rows), 1) + here * tok_rows
        own_segment = segments(own_at, length_ref)[:1]
        placeholder = (own_at >= vis) & (own_at < vis + VIS)
        own_row = jnp.where(placeholder, -1, own_at)
        whole_ref[...] = hide(own_row >= vis + VIS).astype(jnp.float32)
        own_row = own_row[:1]
        image_at = lax.broadcasted_iota(jnp.int32, (1, RATIO * IMAGE_BLOCK), 1) % IMAGE_BLOCK
        image_row = jnp.where(image_at < image_rows, vis + here * image_rows + image_at, -1)
        text_at = lax.broadcasted_iota(jnp.int32, (PROMPT, tok_rows), 0)
        text_at = text_at + jnp.where(text_at < vis, 0, VIS)
        near_ref[:PROMPT] = hide(text_at <= own_row)
        near_at = lax.broadcasted_iota(jnp.int32, (halo + tok_rows, tok_rows), 0)
        near_at = near_at + (here * tok_rows - halo)
        sees = (near_at <= own_row) & (near_at >= PREFIX)
        sees = sees & (segments(near_at, length_ref) == own_segment)
        near_ref[PROMPT:] = hide(sees)
        at = 0
        for core in range(2):
            for step in range(0, ctx_size, 2):
                begin = (here ^ (step + core)) * image_rows + vis
                shape = (image_rows, RATIO * IMAGE_BLOCK)
                block_at = lax.broadcasted_iota(jnp.int32, shape, 0) + begin
                image_ref[at : at + image_rows] = hide(block_at <= image_row)
                at += image_rows
        image_ref[VIS:] = hide(text_at <= image_row)


def second_arrays(vis_start, lengths, cotangent, image_kv, text, received, halo):
    tok_rows, width = cotangent.shape
    image_rows = image_kv.shape[1]
    text_rows = PROMPT + (image_rows if image_rows == IMAGE_BLOCK else 0)
    rounds = window_rounds(lax.axis_size("ctx"), tok_rows, image_rows)
    count = len(rounds) + 1
    block = 2048
    spec = pl.BlockSpec
    smem = spec(memory_space=pltpu.SMEM)
    lanes = RATIO * IMAGE_BLOCK
    near = PROMPT + halo + tok_rows
    whole = lambda *shape: spec(shape, lambda at: (0,) * len(shape))
    out = pl.pallas_call(
        functools.partial(second_kernel, rounds, tok_rows, image_rows, halo),
        grid=(width // block,),
        in_specs=[
            smem,
            smem,
            spec((tok_rows, block), lambda at: (0, at)),
            whole(2, image_rows, KV_WIDTH),
            whole(2, PROMPT, KV_WIDTH),
            whole(2, PROMPT, KV_WIDTH),
        ],
        out_specs=[spec((IMAGE_BLOCK, block), lambda at: (0, at)) for _ in range(count)]
        + [
            whole(near, tok_rows),
            whole(8, tok_rows),
            whole(PREFIX, lanes),
            whole(2, text_rows, KV_WIDTH),
        ],
        out_shape=[jax.ShapeDtypeStruct((IMAGE_BLOCK, width), jnp.bfloat16) for _ in range(count)]
        + [
            jax.ShapeDtypeStruct((near, tok_rows), jnp.float32),
            jax.ShapeDtypeStruct((8, tok_rows), jnp.float32),
            jax.ShapeDtypeStruct((PREFIX, lanes), jnp.float32),
            jax.ShapeDtypeStruct((2, text_rows, KV_WIDTH), jnp.bfloat16),
        ],
    )(vis_start, lengths, cotangent, image_kv, text, received)
    return out[:count], rounds, out[count:]


def first_products(parts, q_rows, d_rows):
    return [(dot_nt(keys, q_rows), dot_nt(values, d_rows)) for keys, values, _ in parts]


def chunks_of(rows):
    return [rows[at : at + KEY_CHUNK] for at in range(0, rows.shape[0], KEY_CHUNK)]


def fold_rows(rows, combine):
    folded = rows[:8]
    for at in range(8, rows.shape[0], 8):
        folded = combine(folded, rows[at : at + 8])
    return folded


def rows_backward(parts, products):
    scale = SCORE_SCALE * math.log2(math.e)
    scores, tops = [], []
    for (keys, values, bias), (raw, _) in zip(parts, products):
        one_row = bias.shape[0] == 1
        top = None
        for at, chunk in enumerate(chunks_of(raw)):
            chunk = chunk * scale
            if not one_row:
                chunk = chunk + bias[at * KEY_CHUNK : (at + 1) * KEY_CHUNK]
            scores.append((chunk, bias if one_row else None))
            folded = fold_rows(chunk, jnp.maximum)
            top = folded if top is None else jnp.maximum(top, folded)
        top = jnp.max(top, axis=0, keepdims=True)
        tops.append(top + bias if one_row else top)
    top = functools.reduce(jnp.maximum, tops)
    d_weights = [chunk for _, product in products for chunk in chunks_of(product)]
    total = mix = None
    kept = []
    for (chunk, bias), d_chunk in zip(scores, d_weights):
        terms = jnp.exp2(chunk + ((bias if bias is not None else 0.0) - top))
        folded = fold_rows(terms, jnp.add)
        total = folded if total is None else total + folded
        folded = fold_rows(terms * d_chunk, jnp.add)
        mix = folded if mix is None else mix + folded
        kept.append(terms)
    total = jnp.sum(total, axis=0, keepdims=True)
    mix = jnp.sum(mix, axis=0, keepdims=True)
    inverse = jnp.where(top > 0.5 * HIDDEN, 1.0 / total, 0.0)
    delta = mix * inverse
    weights, d_scores = [], []
    for terms, d_chunk in zip(kept, d_weights):
        chunk = terms * inverse
        weights.append(chunk.astype(jnp.bfloat16))
        d_scores.append((chunk * (d_chunk - delta)).astype(jnp.bfloat16))
    outcome = []
    for raw, _ in products:
        count = -(-raw.shape[0] // KEY_CHUNK)
        outcome.append(
            (jnp.concatenate(weights[:count], axis=0), jnp.concatenate(d_scores[:count], axis=0))
        )
        weights, d_scores = weights[count:], d_scores[count:]
    return outcome


def total_of(values):
    if len(values) == 1:
        return values[0]
    return sum(value.astype(jnp.float32) for value in values).astype(jnp.bfloat16)


def attend_kernel(
    block_rows,
    block_count,
    text_count,
    window_count,
    heads,
    halo,
    own,
    number_ref,
    near_ref,
    whole_ref,
    image_bias_ref,
    q_ref,
    d_ref,
    iq_ref,
    halo_ref,
    own_ref,
    *refs,
):
    block_refs, refs = refs[:block_count], refs[block_count:]
    text_refs, refs = refs[:text_count], refs[text_count:]
    window_refs, refs = refs[:window_count], refs[window_count:]
    dq_ref, *diq_refs, dmine_ref, dpair_ref, dhalo_ref, down_ref = refs
    text_refs = text_refs or [ref for ref in block_refs if ref.shape[1] > block_rows]
    near_bias = jnp.concatenate([near_ref[...]] * 2, axis=1)
    whole_bias = jnp.concatenate([whole_ref[:1]] * 2, axis=1)
    image_cotangent = total_of([ref[...] for ref in window_refs])
    image_queries = iq_ref[number_ref[1]]
    states = []
    units = []
    for head in range(heads):
        lanes = slice(head * HEAD_DIM, (head + 1) * HEAD_DIM)
        spans = [
            slice((head * RATIO + at) * HEAD_DIM, (head * RATIO + at + 1) * HEAD_DIM)
            for at in range(RATIO)
        ]
        visual, text, near = [], [], []
        for part in range(2):
            visual.append(
                jnp.concatenate([ref[part, :block_rows, lanes] for ref in block_refs], axis=0)
            )
            text.append(total_of([ref[part, -PROMPT:, lanes] for ref in text_refs]))
            near.append(
                jnp.concatenate(
                    [text[part], halo_ref[part, :, lanes], own_ref[0, part, :, lanes]], axis=0
                )
            )
        states.append((lanes, jnp.concatenate([visual[0], near[0]], axis=0).T, {}))
        own_parts = [(visual[0], visual[1], whole_bias), (near[0], near[1], near_bias)]
        for first in range(0, RATIO, 2):
            units.append((head, own_parts, q_ref, d_ref, spans[first : first + 2]))
        image_parts = [
            (visual[0], visual[1], image_bias_ref[:VIS]),
            (text[0], text[1], image_bias_ref[VIS:]),
        ]
        units.append((head, image_parts, image_queries, image_cotangent, spans))

    def begin(unit):
        _, parts, queries, cotangents, unit_spans = unit
        q_rows = jnp.concatenate([queries[:, span] for span in unit_spans], axis=0)
        d_rows = jnp.concatenate([cotangents[:, span] for span in unit_spans], axis=0)
        return q_rows, d_rows, first_products(parts, q_rows, d_rows)

    def finish(unit, begun):
        head, parts, _, _, unit_spans = unit
        lanes, keys_across, sums = states[head]
        q_rows, d_rows, products = begun
        outcome = rows_backward(parts, products)
        d_scores = jnp.concatenate([part[1] for part in outcome], axis=0)
        dq = dot_nn(keys_across[:, : d_scores.shape[0]], d_scores) * SCORE_SCALE
        dq = dq.astype(jnp.bfloat16).T
        rows = dq.shape[0] // len(unit_spans)
        for at, span in enumerate(unit_spans):
            if len(unit_spans) == 2:
                dq_ref[:, span] = dq[at * rows : (at + 1) * rows]
            else:
                for half, out_ref in enumerate(diq_refs):
                    place = at * rows + half * IMAGE_HALF
                    out_ref[:, span] = dq[place : place + IMAGE_HALF]
        for at, (weights, d_part) in enumerate(outcome):
            for kind, rows in ((0, dot_nn(d_part, q_rows)), (1, dot_nn(weights, d_rows))):
                count = rows.shape[0]
                earlier = sums.get((kind, at))
                if earlier is not None and count < earlier.shape[0]:
                    rows = jnp.concatenate([earlier[:count] + rows, earlier[count:]], axis=0)
                elif earlier is not None:
                    rows = earlier + rows
                sums[kind, at] = rows
        if len(unit_spans) == 2:
            return
        for part, scale in ((0, SCORE_SCALE), (1, 1.0)):
            of_visual = (sums[part, 0] * scale).astype(jnp.bfloat16)
            rest = sums[part, 1] * scale
            dmine_ref[part, :, lanes] = of_visual[: VIS // 2]
            dpair_ref[part, : VIS // 2, lanes] = of_visual[VIS // 2 :]
            dpair_ref[part, VIS // 2 :, lanes] = rest[:PROMPT].astype(jnp.bfloat16)
            dhalo_ref[part, :, lanes] = rest[PROMPT : PROMPT + halo].astype(jnp.bfloat16)
            down_ref[part, :, lanes] = rest[PROMPT + halo :]

    begun = begin(units[0])
    for at, unit in enumerate(units):
        later = begin(units[at + 1]) if at + 1 < len(units) else None
        finish(unit, begun)
        begun = later


def attend(
    number, masks, queries, cotangent, every_q, halo_kv, own_kv, blocks, texts, windows
):
    heads = 2
    near_bias, whole_bias, image_bias = masks
    own = queries.shape[0]
    halo = halo_kv.shape[1]
    groups = every_q.shape[0]
    columns = PREFIX + halo + own
    products = RATIO * (own * columns + IMAGE_BLOCK * PREFIX) * KV_HEADS
    spec = pl.BlockSpec
    kv_spec = lambda rows: spec((2, rows, heads * HEAD_DIM), lambda at: (0, 0, at))
    q_spec = lambda rows: spec((rows, heads * GROUP_WIDTH), lambda at: (0, at))
    whole = lambda rows: spec((rows, 128), lambda at: (0, 0))
    return pl.pallas_call(
        functools.partial(
            attend_kernel,
            VIS // len(blocks),
            len(blocks),
            len(texts),
            len(windows),
            heads,
            halo,
            own,
        ),
        grid=(KV_HEADS // heads,),
        in_specs=[
            spec(memory_space=pltpu.SMEM),
            whole(columns - VIS),
            whole(8),
            whole(PREFIX),
            q_spec(own),
            q_spec(own),
            spec((groups, IMAGE_BLOCK, heads * GROUP_WIDTH), lambda at: (0, 0, at)),
            kv_spec(halo),
            spec((1, 2, own, heads * HEAD_DIM), lambda at: (0, 0, 0, at)),
        ]
        + [kv_spec(block.shape[1]) for block in [*blocks, *texts]]
        + [q_spec(IMAGE_BLOCK) for _ in windows],
        out_specs=[
            q_spec(own),
            q_spec(IMAGE_HALF),
            q_spec(IMAGE_HALF),
            kv_spec(VIS // 2),
            kv_spec(VIS // 2 + PROMPT),
            kv_spec(halo),
            kv_spec(own),
        ],
        out_shape=[
            jax.ShapeDtypeStruct((own, Q_WIDTH), jnp.bfloat16),
            jax.ShapeDtypeStruct((IMAGE_HALF, Q_WIDTH), jnp.bfloat16),
            jax.ShapeDtypeStruct((IMAGE_HALF, Q_WIDTH), jnp.bfloat16),
            jax.ShapeDtypeStruct((2, VIS // 2, KV_WIDTH), jnp.bfloat16),
            jax.ShapeDtypeStruct((2, VIS // 2 + PROMPT, KV_WIDTH), jnp.bfloat16),
            jax.ShapeDtypeStruct((2, halo, KV_WIDTH), jnp.bfloat16),
            jax.ShapeDtypeStruct((2, own, KV_WIDTH), jnp.float32),
        ],
        cost_estimate=pl.CostEstimate(
            flops=10 * products * HEAD_DIM,
            bytes_accessed=12 * 1024 * 1024,
            transcendentals=products,
        ),
    )(
        number,
        near_bias,
        whole_bias,
        image_bias,
        queries,
        cotangent,
        every_q,
        halo_kv,
        own_kv,
        *blocks,
        *texts,
        *windows,
    )


def route(rows, number, back, beside=()):
    groups = lax.axis_size("rollout")
    arrays = [array for array, _ in beside]

    def move_beside(arrays):
        return [lax.ppermute(array, "ctx", pairs) for array, (_, pairs) in zip(arrays, beside)]

    if groups != 4:
        every = lax.all_gather(rows, "rollout", axis=0)
        picked = lax.dynamic_index_in_dim(every, number[2 if back else 1], 0, keepdims=False)
        return [picked] + move_beside(arrays)

    def branch(images):
        pairs = [(g, i) if back else (i, g) for g, i in enumerate(images)]
        if all(source == target for source, target in pairs):
            return lambda rows, arrays: [rows] + move_beside(arrays)
        return lambda rows, arrays: [lax.ppermute(rows, "rollout", pairs)] + move_beside(arrays)

    orders = itertools.permutations(range(groups))
    return lax.switch(number[0], [branch(images) for images in orders], rows, arrays)


def window_rounds(ctx_size, tok_rows, image_rows):
    rounds = []
    for target in range(ctx_size):
        lowest = (image_rows * target + 1) // tok_rows
        highest = (image_rows * target + image_rows - 1 + PROMPT - 1) // tok_rows
        for source in range(lowest, highest + 1):
            if source == target:
                continue
            for pairs in rounds:
                if all(s != source and t != target for s, t in pairs):
                    pairs.append((source, target))
                    break
            else:
                rounds.append([(source, target)])
    return rounds


def image_windows(windows, rounds):
    parts = [windows[0]] + [
        lax.ppermute(rows, "ctx", pairs) for rows, pairs in zip(windows[1:], rounds)
    ]
    if len(parts) > 8:
        parts = [sum(part.astype(jnp.float32) for part in parts).astype(jnp.bfloat16)]
    return parts


def xor_pairs(step):
    return [(at, at ^ step) for at in range(lax.axis_size("ctx"))]


def xor_permute(rows, step):
    return lax.ppermute(rows, "ctx", xor_pairs(step))


def on_device(function, *arrays):
    if lax.axis_size("ctx") != 8:
        return function(*arrays)
    shapes = jax.eval_shape(function, *arrays)

    def kernel(*refs):
        for out_ref, value in zip(
            refs[len(arrays) :], function(*[ref[...] for ref in refs[: len(arrays)]])
        ):
            out_ref[...] = value

    def spec(array):
        *rows, width = array.shape
        return pl.BlockSpec((*rows, width // 2), lambda at: (0,) * len(rows) + (at,))

    return pl.pallas_call(
        kernel,
        grid=(2,),
        in_specs=[spec(array) for array in arrays],
        out_specs=[spec(shape) for shape in shapes],
        out_shape=[jax.ShapeDtypeStruct(shape.shape, shape.dtype) for shape in shapes],
        cost_estimate=pl.CostEstimate(flops=1, bytes_accessed=1, transcendentals=0),
    )(*arrays)


def text_strides(ctx_size, late_shard):
    strides = [1 << at for at in range(1, ctx_size.bit_length() - 1)]
    return [stride for stride in reversed(strides) if stride != late_shard]


def chip_steps(ctx_size):
    return list(range(2, ctx_size, 2))


def gather_prefix(image_kv, text, late_shard):
    ctx_size = lax.axis_size("ctx")
    steps = chip_steps(ctx_size)
    if ctx_size == 8:
        mine = [text, xor_permute(image_kv, 2), xor_permute(text, 4), xor_permute(image_kv, 6)]
        blocks = mine + [xor_permute(block, 1) for block in mine]
        return blocks, [blocks[at] for at in (0, 2, 4, 6)]
    mine = jnp.concatenate(
        [image_kv] + [xor_permute(image_kv, step) for step in steps], axis=1
    )
    return [mine, xor_permute(mine, 1)], list(spread_text(text, late_shard))


def split_sums(image_rows, steps, d_mine, d_pair, other):
    half = VIS // 2
    add = lambda one, two: one.astype(jnp.float32) + two.astype(jnp.float32)
    text = add(d_pair[:, half:], other[:, half:])
    out = []
    for at in range(len(steps) + 1):
        rows = slice(at * image_rows, (at + 1) * image_rows)
        sums = add(d_mine[:, rows], other[:, rows])
        if len(steps) == 3 and at in (1, 2):
            halves = text[2 - at]
            halves = jnp.stack([halves[: PROMPT // 2], halves[PROMPT // 2 :]])
            sums = jnp.concatenate([sums, halves], axis=1)
        out.append(sums.astype(jnp.bfloat16) if at else sums)
    return out + [text[0], text[1]]


def add_sums(image_rows, own, keys_text, values_text, *parts):
    texts = [values_text, keys_text]
    for at, part in enumerate(parts):
        own = own + part[:, :image_rows].astype(jnp.float32)
        if part.shape[1] > image_rows:
            rows = part[:, image_rows:].astype(jnp.float32)
            texts[at] = texts[at] + jnp.concatenate([rows[0], rows[1]], axis=0)
    return [part.astype(jnp.bfloat16) for part in (own, texts[1], texts[0])]


def spread_text(text, late_shard):
    for stride in text_strides(lax.axis_size("ctx"), late_shard):
        text = text + xor_permute(text, stride)
    return text, xor_permute(text, 1)


def collect_text(text, late_shard):
    for stride in reversed(text_strides(lax.axis_size("ctx"), late_shard)):
        moved = xor_permute(text.astype(jnp.bfloat16), stride)
        text = text.astype(jnp.float32) + moved.astype(jnp.float32)
    return text.astype(jnp.bfloat16)


def halo_cuts(tok_rows, halo):
    cuts = []
    left = halo
    while left > 0:
        cuts.append(min(left, tok_rows))
        left -= cuts[-1]
    return cuts


def halo_pairs(step, tok_rows):
    first = PREFIX // tok_rows
    return [(at, at + step) for at in range(first, lax.axis_size("ctx") - step)]


def halo_rows(tail, halo, tok_rows):
    parts = []
    for step, count in enumerate(halo_cuts(tok_rows, halo), 1):
        pairs = halo_pairs(step, tok_rows)
        rows = tail if count == tail.shape[1] else tail[:, tail.shape[1] - count :]
        parts.insert(0, lax.ppermute(rows, "ctx", pairs))
    return jnp.concatenate(parts, axis=1) if len(parts) > 1 else parts[0]


def halo_parts(d_halo, tok_rows):
    cuts = halo_cuts(tok_rows, d_halo.shape[1])
    parts = []
    end = d_halo.shape[1]
    for step, count in enumerate(cuts, 1):
        rows = d_halo if len(cuts) == 1 else d_halo[:, end - count : end]
        parts.append((rows, [(target, at) for at, target in halo_pairs(step, tok_rows)]))
        end -= count
    return parts


def last_kernel(part_count, vis_ref, dkv_ref, down_ref, *refs):
    text_refs, refs = refs[:4], refs[4:]
    part_refs = refs[:part_count]
    *dq_refs, image_ref, kv_ref = refs[part_count:]
    here = lax.axis_index("ctx")
    tok_rows = down_ref.shape[1]
    at = 0
    for dq_ref in dq_refs:
        image_ref[0, at : at + dq_ref.shape[0], :Q_WIDTH] = dq_ref[...]
        at += dq_ref.shape[0]
    image_ref[0, :, Q_WIDTH : Q_WIDTH + KV_WIDTH] = dkv_ref[0]
    image_ref[0, :, Q_WIDTH + KV_WIDTH :] = dkv_ref[1]
    at = lax.broadcasted_iota(jnp.int32, (PROMPT, KV_WIDTH), 0)
    ahead = jnp.where(here == 0, 1, 0)
    behind = jnp.where(here == VIS // tok_rows, 1, 0)
    kept = jnp.where(at < vis_ref[0], ahead, behind) == 1
    for part in range(2):
        text = text_refs[part][...].astype(jnp.float32)
        text = text + text_refs[2 + part][...].astype(jnp.float32)
        text = jnp.where(kept, text, 0.0)
        sums = down_ref[part] + jnp.concatenate(
            [text, jnp.zeros((tok_rows - PROMPT, KV_WIDTH), jnp.float32)], axis=0
        )
        for part_ref in part_refs:
            back = part_ref[part].astype(jnp.float32)
            if back.shape[0] < tok_rows:
                missing = jnp.zeros((tok_rows - back.shape[0], KV_WIDTH), jnp.float32)
                back = jnp.concatenate([missing, back], axis=0)
            sums = sums + back
        kv_ref[0, part] = sums.astype(jnp.bfloat16)


def last_arrays(vis_start, image_dq, image_dkv, d_own_kv, texts, parts):
    rows = image_dkv.shape[1]
    smem = pl.BlockSpec(memory_space=pltpu.SMEM)
    vmem = pl.BlockSpec(memory_space=pltpu.VMEM)
    return pl.pallas_call(
        functools.partial(last_kernel, len(parts)),
        in_specs=[smem] + [vmem] * (6 + len(parts) + len(image_dq)),
        out_specs=[vmem, vmem],
        out_shape=[
            jax.ShapeDtypeStruct((1, rows, Q_WIDTH + 2 * KV_WIDTH), jnp.bfloat16),
            jax.ShapeDtypeStruct((1,) + d_own_kv.shape, jnp.bfloat16),
        ],
    )(vis_start, image_dkv, d_own_kv, *texts, *parts, *image_dq)


def gather_queries(image_q):
    every = lax.all_gather(image_q, "rollout", axis=0)
    missing = IMAGE_BLOCK - every.shape[1]
    return jnp.pad(every, ((0, 0), (0, missing), (0, 0))) if missing else every


def per_device(queries, keys_values, image_rows, cotangent, seq_image, vis_start, comp_lengths):
    tok_rows = queries.shape[1]
    image_count = image_rows.shape[1]
    ctx_size = lax.axis_size("ctx")
    seq_len = tok_rows * ctx_size
    late_shard = VIS // tok_rows
    longest = 4 * (seq_len - PREFIX) // (3 * NCOMP)
    halo = -(-(longest - 1) // 64) * 64
    q_own, d_own = queries[0], cotangent[0]

    number, image_kv, image_q, text, tail = first_arrays(
        seq_image, vis_start, image_rows, keys_values, halo
    )
    every_q = gather_queries(image_q)
    image_kv, swapped = route(image_kv, number, False, [(text, xor_pairs(late_shard))])
    image_kv, d_later = lax.optimization_barrier((image_kv, d_own))
    windows, rounds, (*masks, text) = second_arrays(
        vis_start, comp_lengths, d_later, image_kv, text, swapped, halo
    )
    blocks, texts = gather_prefix(image_kv, text, late_shard)
    windows = image_windows(windows, rounds)
    halo_kv = halo_rows(tail, halo, tok_rows)

    grad_q, *d_image_q, d_mine, d_pair, d_halo, d_own_kv = attend(
        number,
        masks,
        q_own,
        d_own,
        every_q,
        halo_kv,
        keys_values,
        blocks,
        [] if ctx_size == 8 else texts,
        windows,
    )

    d_image_q = [
        half[: image_count - at * IMAGE_HALF]
        for at, half in enumerate(d_image_q)
        if at * IMAGE_HALF < image_count
    ]
    image_dq, other, *halo_back = route(
        d_image_q[0], number, True, [(d_pair, xor_pairs(1))] + halo_parts(d_halo, tok_rows)
    )
    image_dq = [image_dq]
    steps = chip_steps(ctx_size)
    own, *sent, keys_text, values_text = on_device(
        functools.partial(split_sums, image_count, steps), d_mine, d_pair, other
    )
    beside = [(rows, xor_pairs(step)) for rows, step in zip(sent, steps)]
    if len(d_image_q) > 1:
        second, *moved = route(d_image_q[1], number, True, beside)
        image_dq.append(second)
    else:
        moved = [lax.ppermute(rows, "ctx", pairs) for rows, pairs in beside]
    sums, keys_text, values_text = on_device(
        functools.partial(add_sums, image_count), own, keys_text, values_text, *moved
    )
    if ctx_size != 8:
        keys_text = collect_text(keys_text, late_shard)
        values_text = collect_text(values_text, late_shard)
    keys_step = late_shard
    values_step = 4 if ctx_size == 8 else late_shard
    image_dkv, *other_texts = route(
        sums,
        number,
        True,
        [(keys_text, xor_pairs(keys_step)), (values_text, xor_pairs(values_step))],
    )
    grad_image, grad_kv = last_arrays(
        vis_start,
        image_dq,
        image_dkv,
        d_own_kv,
        [keys_text, values_text, *other_texts],
        halo_back,
    )
    return (grad_q[None], grad_kv, grad_image)


def solution(mesh):
    placed = (
        P("rollout", "ctx", None),
        P("rollout", None, "ctx", None),
        P("rollout", "ctx", None),
        P("rollout", "ctx", None),
        P(),
        P("rollout"),
        P("rollout", None),
    )
    return jax.shard_map(
        per_device,
        mesh=mesh,
        in_specs=placed,
        out_specs=(
            P("rollout", "ctx", None),
            P("rollout", None, "ctx", None),
            P("rollout", "ctx", None),
        ),
        check_vma=False,
    )
```

```python
import functools
import itertools
import math

import jax
import jax.numpy as jnp
from jax import lax
from jax.experimental import pallas as pl
from jax.experimental.pallas import tpu as pltpu
from jax.sharding import PartitionSpec as P

HEADS = 32
KV_HEADS = 8
HEAD_DIM = 128
VIS = 256
PROMPT = 64
NCOMP = 16

RATIO = HEADS // KV_HEADS
PREFIX = VIS + PROMPT
Q_WIDTH = HEADS * HEAD_DIM
KV_WIDTH = KV_HEADS * HEAD_DIM
GROUP_WIDTH = RATIO * HEAD_DIM
IMAGE_BLOCK = 32
IMAGE_HALF = IMAGE_BLOCK // 2
KEY_CHUNK = 64
HIDDEN = -1e30
SCORE_SCALE = 1.0 / math.sqrt(HEAD_DIM)


def dot_nt(left, right):
    return lax.dot_general(
        left, right, (((1,), (1,)), ((), ())), preferred_element_type=jnp.float32
    )


def dot_nn(left, right):
    return lax.dot_general(
        left, right, (((1,), (0,)), ((), ())), preferred_element_type=jnp.float32
    )


def dot_tn(left, right):
    return lax.dot_general(
        left, right, (((0,), (0,)), ((), ())), preferred_element_type=jnp.float32
    )


def first_kernel(halo, seq_ref, vis_ref, image_ref, kv_ref, number_ref, *out_refs):
    ikv_ref, iq_ref, text_ref, tail_ref = out_refs
    groups = seq_ref.shape[0]
    group = lax.axis_index("rollout")
    here = lax.axis_index("ctx")
    images = [seq_ref[at] for at in range(groups)]
    number = jnp.int32(0)
    if groups == 4:
        for at, weight in enumerate((6, 2, 1)):
            for later in range(at + 1, groups):
                number = number + jnp.where(images[later] < images[at], weight, 0)
    place = jnp.int32(0)
    user = jnp.int32(0)
    for at in range(groups):
        place = place + jnp.where(group == at, images[at], 0)
        user = user + jnp.where(images[at] == group, at, 0)
    number_ref[0] = number
    number_ref[1] = place
    number_ref[2] = user
    iq_ref[...] = image_ref[0, :, :Q_WIDTH]
    ikv_ref[0] = image_ref[0, :, Q_WIDTH : Q_WIDTH + KV_WIDTH]
    ikv_ref[1] = image_ref[0, :, Q_WIDTH + KV_WIDTH :]
    tok_rows = kv_ref.shape[2]
    late_shard = VIS // tok_rows
    at = lax.broadcasted_iota(jnp.int32, (PROMPT, KV_WIDTH), 0)
    ahead = jnp.where(here == 0, 1, 0)
    behind = jnp.where(here == late_shard, 1, 0)
    kept = jnp.where(at < vis_ref[0], ahead, behind) == 1
    for part in range(2):
        rows = kv_ref[0, part, :PROMPT].astype(jnp.float32)
        text_ref[part] = jnp.where(kept, rows, 0.0).astype(jnp.bfloat16)
        tail_ref[part] = kv_ref[0, part, tok_rows - halo :]


def first_arrays(seq_image, vis_start, image_rows, keys_values, halo):
    rows = image_rows.shape[1]
    smem = pl.BlockSpec(memory_space=pltpu.SMEM)
    vmem = pl.BlockSpec(memory_space=pltpu.VMEM)
    tail = min(halo, keys_values.shape[2])
    return pl.pallas_call(
        functools.partial(first_kernel, tail),
        in_specs=[smem, smem, vmem, vmem],
        out_specs=[smem, vmem, vmem, vmem, vmem],
        out_shape=[
            jax.ShapeDtypeStruct((3,), jnp.int32),
            jax.ShapeDtypeStruct((2, rows, KV_WIDTH), jnp.bfloat16),
            jax.ShapeDtypeStruct((rows, Q_WIDTH), jnp.bfloat16),
            jax.ShapeDtypeStruct((2, PROMPT, KV_WIDTH), jnp.bfloat16),
            jax.ShapeDtypeStruct((2, tail, KV_WIDTH), jnp.bfloat16),
        ],
    )(seq_image, vis_start, image_rows, keys_values)


def segments(positions, length_ref):
    end = jnp.int32(PREFIX)
    segment = jnp.where(positions < PREFIX, 0, 1)
    for at in range(NCOMP):
        end = end + length_ref[0, at]
        segment = segment + jnp.where(positions >= end, 1, 0)
    return segment


def hide(visible):
    return jnp.where(visible, 0.0, HIDDEN)


def second_kernel(
    rounds, tok_rows, image_rows, halo, vis_ref, length_ref, d_ref, kv_ref, t_ref, r_ref, *out_refs
):
    *window_refs, near_ref, whole_ref, image_ref, text_ref = out_refs
    here = lax.axis_index("ctx")
    ctx_size = lax.axis_size("ctx")
    row = lax.broadcasted_iota(jnp.int32, (IMAGE_BLOCK, tok_rows), 0)
    column = lax.broadcasted_iota(jnp.int32, (IMAGE_BLOCK, tok_rows), 1)
    place = jnp.where(row < image_rows, row, 1 << 20)
    picks = []
    for pairs in [[]] + rounds:
        target = here
        for source, other in pairs:
            target = jnp.where(here == source, other, target)
        begin = vis_ref[0] + image_rows * target - tok_rows * here
        picks.append(jnp.where(column == place + begin, 1.0, 0.0).astype(jnp.bfloat16))
    picked = dot_nn(jnp.concatenate(picks, axis=0), d_ref[...]).astype(jnp.bfloat16)
    for at, window_ref in enumerate(window_refs):
        window_ref[...] = picked[at * IMAGE_BLOCK : (at + 1) * IMAGE_BLOCK]

    @pl.when(pl.program_id(0) == 0)
    def _():
        vis = vis_ref[0]
        text = t_ref[...].astype(jnp.float32) + r_ref[...].astype(jnp.float32)
        if kv_ref.shape[1] == IMAGE_BLOCK:
            text_ref[:, :IMAGE_BLOCK] = kv_ref[...]
        text_ref[:, text_ref.shape[1] - PROMPT :] = text.astype(jnp.bfloat16)
        own_at = lax.broadcasted_iota(jnp.int32, (8, tok_rows), 1) + here * tok_rows
        own_segment = segments(own_at, length_ref)[:1]
        placeholder = (own_at >= vis) & (own_at < vis + VIS)
        own_row = jnp.where(placeholder, -1, own_at)
        whole_ref[...] = hide(own_row >= vis + VIS).astype(jnp.float32)
        own_row = own_row[:1]
        image_at = lax.broadcasted_iota(jnp.int32, (1, RATIO * IMAGE_BLOCK), 1) % IMAGE_BLOCK
        image_row = jnp.where(image_at < image_rows, vis + here * image_rows + image_at, -1)
        text_at = lax.broadcasted_iota(jnp.int32, (PROMPT, tok_rows), 0)
        text_at = text_at + jnp.where(text_at < vis, 0, VIS)
        near_ref[:PROMPT] = hide(text_at <= own_row)
        near_at = lax.broadcasted_iota(jnp.int32, (halo + tok_rows, tok_rows), 0)
        near_at = near_at + (here * tok_rows - halo)
        sees = (near_at <= own_row) & (near_at >= PREFIX)
        sees = sees & (segments(near_at, length_ref) == own_segment)
        near_ref[PROMPT:] = hide(sees)
        at = 0
        for core in range(2):
            for step in range(0, ctx_size, 2):
                begin = (here ^ (step + core)) * image_rows + vis
                shape = (image_rows, RATIO * IMAGE_BLOCK)
                block_at = lax.broadcasted_iota(jnp.int32, shape, 0) + begin
                image_ref[at : at + image_rows] = hide(block_at <= image_row)
                at += image_rows
        image_ref[VIS:] = hide(text_at <= image_row)


def second_arrays(vis_start, lengths, cotangent, image_kv, text, received, halo):
    tok_rows, width = cotangent.shape
    image_rows = image_kv.shape[1]
    text_rows = PROMPT + (image_rows if image_rows == IMAGE_BLOCK else 0)
    rounds = window_rounds(lax.axis_size("ctx"), tok_rows, image_rows)
    count = len(rounds) + 1
    block = 2048
    spec = pl.BlockSpec
    smem = spec(memory_space=pltpu.SMEM)
    lanes = RATIO * IMAGE_BLOCK
    near = PROMPT + halo + tok_rows
    whole = lambda *shape: spec(shape, lambda at: (0,) * len(shape))
    out = pl.pallas_call(
        functools.partial(second_kernel, rounds, tok_rows, image_rows, halo),
        grid=(width // block,),
        in_specs=[
            smem,
            smem,
            spec((tok_rows, block), lambda at: (0, at)),
            whole(2, image_rows, KV_WIDTH),
            whole(2, PROMPT, KV_WIDTH),
            whole(2, PROMPT, KV_WIDTH),
        ],
        out_specs=[spec((IMAGE_BLOCK, block), lambda at: (0, at)) for _ in range(count)]
        + [
            whole(near, tok_rows),
            whole(8, tok_rows),
            whole(PREFIX, lanes),
            whole(2, text_rows, KV_WIDTH),
        ],
        out_shape=[jax.ShapeDtypeStruct((IMAGE_BLOCK, width), jnp.bfloat16) for _ in range(count)]
        + [
            jax.ShapeDtypeStruct((near, tok_rows), jnp.float32),
            jax.ShapeDtypeStruct((8, tok_rows), jnp.float32),
            jax.ShapeDtypeStruct((PREFIX, lanes), jnp.float32),
            jax.ShapeDtypeStruct((2, text_rows, KV_WIDTH), jnp.bfloat16),
        ],
    )(vis_start, lengths, cotangent, image_kv, text, received)
    return out[:count], rounds, out[count:]


def first_products(parts, q_rows, d_rows):
    return [(dot_nt(keys, q_rows), dot_nt(values, d_rows)) for keys, values, _ in parts]


def chunks_of(rows):
    return [rows[at : at + KEY_CHUNK] for at in range(0, rows.shape[0], KEY_CHUNK)]


def fold_rows(rows, combine):
    folded = rows[:8]
    for at in range(8, rows.shape[0], 8):
        folded = combine(folded, rows[at : at + 8])
    return folded


def rows_backward(parts, products):
    scale = SCORE_SCALE * math.log2(math.e)
    scores, tops = [], []
    for (keys, values, bias), (raw, _) in zip(parts, products):
        one_row = bias.shape[0] == 1
        top = None
        for at, chunk in enumerate(chunks_of(raw)):
            chunk = chunk * scale
            if not one_row:
                chunk = chunk + bias[at * KEY_CHUNK : (at + 1) * KEY_CHUNK]
            scores.append((chunk, bias if one_row else None))
            folded = fold_rows(chunk, jnp.maximum)
            top = folded if top is None else jnp.maximum(top, folded)
        top = jnp.max(top, axis=0, keepdims=True)
        tops.append(top + bias if one_row else top)
    top = functools.reduce(jnp.maximum, tops)
    d_weights = [chunk for _, product in products for chunk in chunks_of(product)]
    total = mix = None
    kept = []
    for (chunk, bias), d_chunk in zip(scores, d_weights):
        terms = jnp.exp2(chunk + ((bias if bias is not None else 0.0) - top))
        folded = fold_rows(terms, jnp.add)
        total = folded if total is None else total + folded
        folded = fold_rows(terms * d_chunk, jnp.add)
        mix = folded if mix is None else mix + folded
        kept.append(terms)
    total = jnp.sum(total, axis=0, keepdims=True)
    mix = jnp.sum(mix, axis=0, keepdims=True)
    inverse = jnp.where(top > 0.5 * HIDDEN, 1.0 / total, 0.0)
    delta = mix * inverse
    weights, d_scores = [], []
    for terms, d_chunk in zip(kept, d_weights):
        chunk = terms * inverse
        weights.append(chunk.astype(jnp.bfloat16))
        d_scores.append((chunk * (d_chunk - delta)).astype(jnp.bfloat16))
    outcome = []
    for raw, _ in products:
        count = raw.shape[0] // KEY_CHUNK
        outcome.append(
            (jnp.concatenate(weights[:count], axis=0), jnp.concatenate(d_scores[:count], axis=0))
        )
        weights, d_scores = weights[count:], d_scores[count:]
    return outcome


def total_of(values):
    if len(values) == 1:
        return values[0]
    return sum(value.astype(jnp.float32) for value in values).astype(jnp.bfloat16)


def attend_kernel(
    block_rows,
    block_count,
    text_count,
    window_count,
    heads,
    halo,
    own,
    number_ref,
    near_ref,
    whole_ref,
    image_bias_ref,
    q_ref,
    d_ref,
    iq_ref,
    halo_ref,
    own_ref,
    *refs,
):
    block_refs, refs = refs[:block_count], refs[block_count:]
    text_refs, refs = refs[:text_count], refs[text_count:]
    window_refs, refs = refs[:window_count], refs[window_count:]
    dq_ref, *diq_refs, dmine_ref, dpair_ref, dhalo_ref, down_ref = refs
    text_refs = text_refs or [ref for ref in block_refs if ref.shape[1] > block_rows]
    near_bias = jnp.concatenate([near_ref[...]] * 2, axis=1)
    whole_bias = jnp.concatenate([whole_ref[:1]] * 2, axis=1)
    image_cotangent = total_of([ref[...] for ref in window_refs])
    image_queries = iq_ref[number_ref[1]]
    states = []
    units = []
    for head in range(heads):
        lanes = slice(head * HEAD_DIM, (head + 1) * HEAD_DIM)
        spans = [
            slice((head * RATIO + at) * HEAD_DIM, (head * RATIO + at + 1) * HEAD_DIM)
            for at in range(RATIO)
        ]
        visual, text, near = [], [], []
        for part in range(2):
            visual.append(
                jnp.concatenate([ref[part, :block_rows, lanes] for ref in block_refs], axis=0)
            )
            text.append(total_of([ref[part, -PROMPT:, lanes] for ref in text_refs]))
            near.append(
                jnp.concatenate(
                    [text[part], halo_ref[part, :, lanes], own_ref[0, part, :, lanes]], axis=0
                )
            )
        states.append((lanes, jnp.concatenate([visual[0], near[0]], axis=0).T, {}))
        own_parts = [(visual[0], visual[1], whole_bias), (near[0], near[1], near_bias)]
        for first in range(0, RATIO, 2):
            units.append((head, own_parts, q_ref, d_ref, spans[first : first + 2]))
        image_parts = [
            (visual[0], visual[1], image_bias_ref[:VIS]),
            (text[0], text[1], image_bias_ref[VIS:]),
        ]
        units.append((head, image_parts, image_queries, image_cotangent, spans))

    def begin(unit):
        _, parts, queries, cotangents, unit_spans = unit
        q_rows = jnp.concatenate([queries[:, span] for span in unit_spans], axis=0)
        d_rows = jnp.concatenate([cotangents[:, span] for span in unit_spans], axis=0)
        return q_rows, d_rows, first_products(parts, q_rows, d_rows)

    def finish(unit, begun):
        head, parts, _, _, unit_spans = unit
        lanes, keys_across, sums = states[head]
        q_rows, d_rows, products = begun
        outcome = rows_backward(parts, products)
        d_scores = jnp.concatenate([part[1] for part in outcome], axis=0)
        dq = dot_nn(keys_across[:, : d_scores.shape[0]], d_scores) * SCORE_SCALE
        dq = dq.astype(jnp.bfloat16).T
        rows = dq.shape[0] // len(unit_spans)
        for at, span in enumerate(unit_spans):
            if len(unit_spans) == 2:
                dq_ref[:, span] = dq[at * rows : (at + 1) * rows]
            else:
                for half, out_ref in enumerate(diq_refs):
                    place = at * rows + half * IMAGE_HALF
                    out_ref[:, span] = dq[place : place + IMAGE_HALF]
        for at, (weights, d_part) in enumerate(outcome):
            for kind, rows in ((0, dot_nn(d_part, q_rows)), (1, dot_nn(weights, d_rows))):
                count = rows.shape[0]
                earlier = sums.get((kind, at))
                if earlier is not None and count < earlier.shape[0]:
                    rows = jnp.concatenate([earlier[:count] + rows, earlier[count:]], axis=0)
                elif earlier is not None:
                    rows = earlier + rows
                sums[kind, at] = rows
        if len(unit_spans) == 2:
            return
        for part, scale in ((0, SCORE_SCALE), (1, 1.0)):
            of_visual = (sums[part, 0] * scale).astype(jnp.bfloat16)
            rest = sums[part, 1] * scale
            dmine_ref[part, :, lanes] = of_visual[: VIS // 2]
            dpair_ref[part, : VIS // 2, lanes] = of_visual[VIS // 2 :]
            dpair_ref[part, VIS // 2 :, lanes] = rest[:PROMPT].astype(jnp.bfloat16)
            dhalo_ref[part, :, lanes] = rest[PROMPT : PROMPT + halo].astype(jnp.bfloat16)
            down_ref[part, :, lanes] = rest[PROMPT + halo :]

    begun = begin(units[0])
    for at, unit in enumerate(units):
        later = begin(units[at + 1]) if at + 1 < len(units) else None
        finish(unit, begun)
        begun = later


def attend(
    number, masks, queries, cotangent, every_q, halo_kv, own_kv, blocks, texts, windows
):
    heads = 2
    near_bias, whole_bias, image_bias = masks
    own = queries.shape[0]
    halo = halo_kv.shape[1]
    groups = every_q.shape[0]
    columns = PREFIX + halo + own
    products = RATIO * (own * columns + IMAGE_BLOCK * PREFIX) * KV_HEADS
    spec = pl.BlockSpec
    kv_spec = lambda rows: spec((2, rows, heads * HEAD_DIM), lambda at: (0, 0, at))
    q_spec = lambda rows: spec((rows, heads * GROUP_WIDTH), lambda at: (0, at))
    whole = lambda rows: spec((rows, 128), lambda at: (0, 0))
    return pl.pallas_call(
        functools.partial(
            attend_kernel,
            VIS // len(blocks),
            len(blocks),
            len(texts),
            len(windows),
            heads,
            halo,
            own,
        ),
        grid=(KV_HEADS // heads,),
        in_specs=[
            spec(memory_space=pltpu.SMEM),
            whole(columns - VIS),
            whole(8),
            whole(PREFIX),
            q_spec(own),
            q_spec(own),
            spec((groups, IMAGE_BLOCK, heads * GROUP_WIDTH), lambda at: (0, 0, at)),
            kv_spec(halo),
            spec((1, 2, own, heads * HEAD_DIM), lambda at: (0, 0, 0, at)),
        ]
        + [kv_spec(block.shape[1]) for block in [*blocks, *texts]]
        + [q_spec(IMAGE_BLOCK) for _ in windows],
        out_specs=[
            q_spec(own),
            q_spec(IMAGE_HALF),
            q_spec(IMAGE_HALF),
            kv_spec(VIS // 2),
            kv_spec(VIS // 2 + PROMPT),
            kv_spec(halo),
            kv_spec(own),
        ],
        out_shape=[
            jax.ShapeDtypeStruct((own, Q_WIDTH), jnp.bfloat16),
            jax.ShapeDtypeStruct((IMAGE_HALF, Q_WIDTH), jnp.bfloat16),
            jax.ShapeDtypeStruct((IMAGE_HALF, Q_WIDTH), jnp.bfloat16),
            jax.ShapeDtypeStruct((2, VIS // 2, KV_WIDTH), jnp.bfloat16),
            jax.ShapeDtypeStruct((2, VIS // 2 + PROMPT, KV_WIDTH), jnp.bfloat16),
            jax.ShapeDtypeStruct((2, halo, KV_WIDTH), jnp.bfloat16),
            jax.ShapeDtypeStruct((2, own, KV_WIDTH), jnp.float32),
        ],
        cost_estimate=pl.CostEstimate(
            flops=10 * products * HEAD_DIM,
            bytes_accessed=12 * 1024 * 1024,
            transcendentals=products,
        ),
    )(
        number,
        near_bias,
        whole_bias,
        image_bias,
        queries,
        cotangent,
        every_q,
        halo_kv,
        own_kv,
        *blocks,
        *texts,
        *windows,
    )


def route(rows, number, back, beside=()):
    groups = lax.axis_size("rollout")
    arrays = [array for array, _ in beside]

    def move_beside(arrays):
        return [lax.ppermute(array, "ctx", pairs) for array, (_, pairs) in zip(arrays, beside)]

    if groups != 4:
        every = lax.all_gather(rows, "rollout", axis=0)
        picked = lax.dynamic_index_in_dim(every, number[2 if back else 1], 0, keepdims=False)
        return [picked] + move_beside(arrays)

    def branch(images):
        pairs = [(g, i) if back else (i, g) for g, i in enumerate(images)]
        if all(source == target for source, target in pairs):
            return lambda rows, arrays: [rows] + move_beside(arrays)
        return lambda rows, arrays: [lax.ppermute(rows, "rollout", pairs)] + move_beside(arrays)

    orders = itertools.permutations(range(groups))
    return lax.switch(number[0], [branch(images) for images in orders], rows, arrays)


def window_rounds(ctx_size, tok_rows, image_rows):
    rounds = []
    for target in range(ctx_size):
        lowest = (image_rows * target + 1) // tok_rows
        highest = (image_rows * target + image_rows - 1 + PROMPT - 1) // tok_rows
        for source in range(lowest, highest + 1):
            if source == target:
                continue
            for pairs in rounds:
                if all(s != source and t != target for s, t in pairs):
                    pairs.append((source, target))
                    break
            else:
                rounds.append([(source, target)])
    return rounds


def image_windows(windows, rounds):
    parts = [windows[0]] + [
        lax.ppermute(rows, "ctx", pairs) for rows, pairs in zip(windows[1:], rounds)
    ]
    if len(parts) > 8:
        parts = [sum(part.astype(jnp.float32) for part in parts).astype(jnp.bfloat16)]
    return parts


def xor_pairs(step):
    return [(at, at ^ step) for at in range(lax.axis_size("ctx"))]


def xor_permute(rows, step):
    return lax.ppermute(rows, "ctx", xor_pairs(step))


def on_device(function, *arrays):
    if lax.axis_size("ctx") != 8:
        return function(*arrays)
    shapes = jax.eval_shape(function, *arrays)

    def kernel(*refs):
        for out_ref, value in zip(
            refs[len(arrays) :], function(*[ref[...] for ref in refs[: len(arrays)]])
        ):
            out_ref[...] = value

    def spec(array):
        *rows, width = array.shape
        return pl.BlockSpec((*rows, width // 4), lambda at: (0,) * len(rows) + (at,))

    return pl.pallas_call(
        kernel,
        grid=(4,),
        in_specs=[spec(array) for array in arrays],
        out_specs=[spec(shape) for shape in shapes],
        out_shape=[jax.ShapeDtypeStruct(shape.shape, shape.dtype) for shape in shapes],
        cost_estimate=pl.CostEstimate(flops=1, bytes_accessed=1, transcendentals=0),
    )(*arrays)


def text_strides(ctx_size, late_shard):
    strides = [1 << at for at in range(1, ctx_size.bit_length() - 1)]
    return [stride for stride in reversed(strides) if stride != late_shard]


def chip_steps(ctx_size):
    return list(range(2, ctx_size, 2))


def gather_prefix(image_kv, text, late_shard):
    ctx_size = lax.axis_size("ctx")
    steps = chip_steps(ctx_size)
    if ctx_size == 8:
        mine = [text, xor_permute(image_kv, 2), xor_permute(text, 4), xor_permute(image_kv, 6)]
        blocks = mine + [xor_permute(block, 1) for block in mine]
        return blocks, [blocks[at] for at in (0, 2, 4, 6)]
    mine = jnp.concatenate(
        [image_kv] + [xor_permute(image_kv, step) for step in steps], axis=1
    )
    return [mine, xor_permute(mine, 1)], list(spread_text(text, late_shard))


def split_sums(image_rows, steps, d_mine, d_pair, other):
    half = VIS // 2
    add = lambda one, two: one.astype(jnp.float32) + two.astype(jnp.float32)
    text = add(d_pair[:, half:], other[:, half:])
    out = []
    for at in range(len(steps) + 1):
        rows = slice(at * image_rows, (at + 1) * image_rows)
        sums = add(d_mine[:, rows], other[:, rows])
        if len(steps) == 3 and at in (1, 2):
            halves = text[2 - at]
            halves = jnp.stack([halves[: PROMPT // 2], halves[PROMPT // 2 :]])
            sums = jnp.concatenate([sums, halves], axis=1)
        out.append(sums.astype(jnp.bfloat16) if at else sums)
    return out + [text[0], text[1]]


def add_sums(image_rows, own, keys_text, values_text, *parts):
    texts = [values_text, keys_text]
    for at, part in enumerate(parts):
        own = own + part[:, :image_rows].astype(jnp.float32)
        if part.shape[1] > image_rows:
            rows = part[:, image_rows:].astype(jnp.float32)
            texts[at] = texts[at] + jnp.concatenate([rows[0], rows[1]], axis=0)
    return [part.astype(jnp.bfloat16) for part in (own, texts[1], texts[0])]


def spread_text(text, late_shard):
    for stride in text_strides(lax.axis_size("ctx"), late_shard):
        text = text + xor_permute(text, stride)
    return text, xor_permute(text, 1)


def collect_text(text, late_shard):
    for stride in reversed(text_strides(lax.axis_size("ctx"), late_shard)):
        moved = xor_permute(text.astype(jnp.bfloat16), stride)
        text = text.astype(jnp.float32) + moved.astype(jnp.float32)
    return text.astype(jnp.bfloat16)


def halo_cuts(tok_rows, halo):
    cuts = []
    left = halo
    while left > 0:
        cuts.append(min(left, tok_rows))
        left -= cuts[-1]
    return cuts


def halo_pairs(step, tok_rows):
    first = PREFIX // tok_rows
    return [(at, at + step) for at in range(first, lax.axis_size("ctx") - step)]


def halo_rows(tail, halo, tok_rows):
    parts = []
    for step, count in enumerate(halo_cuts(tok_rows, halo), 1):
        pairs = halo_pairs(step, tok_rows)
        rows = tail if count == tail.shape[1] else tail[:, tail.shape[1] - count :]
        parts.insert(0, lax.ppermute(rows, "ctx", pairs))
    return jnp.concatenate(parts, axis=1) if len(parts) > 1 else parts[0]


def halo_parts(d_halo, tok_rows):
    cuts = halo_cuts(tok_rows, d_halo.shape[1])
    parts = []
    end = d_halo.shape[1]
    for step, count in enumerate(cuts, 1):
        rows = d_halo if len(cuts) == 1 else d_halo[:, end - count : end]
        parts.append((rows, [(target, at) for at, target in halo_pairs(step, tok_rows)]))
        end -= count
    return parts


def last_kernel(part_count, vis_ref, dkv_ref, down_ref, *refs):
    text_refs, refs = refs[:4], refs[4:]
    part_refs = refs[:part_count]
    *dq_refs, image_ref, kv_ref = refs[part_count:]
    here = lax.axis_index("ctx")
    tok_rows = down_ref.shape[1]
    at = 0
    for dq_ref in dq_refs:
        image_ref[0, at : at + dq_ref.shape[0], :Q_WIDTH] = dq_ref[...]
        at += dq_ref.shape[0]
    image_ref[0, :, Q_WIDTH : Q_WIDTH + KV_WIDTH] = dkv_ref[0]
    image_ref[0, :, Q_WIDTH + KV_WIDTH :] = dkv_ref[1]
    at = lax.broadcasted_iota(jnp.int32, (PROMPT, KV_WIDTH), 0)
    ahead = jnp.where(here == 0, 1, 0)
    behind = jnp.where(here == VIS // tok_rows, 1, 0)
    kept = jnp.where(at < vis_ref[0], ahead, behind) == 1
    for part in range(2):
        text = text_refs[part][...].astype(jnp.float32)
        text = text + text_refs[2 + part][...].astype(jnp.float32)
        text = jnp.where(kept, text, 0.0)
        sums = down_ref[part] + jnp.concatenate(
            [text, jnp.zeros((tok_rows - PROMPT, KV_WIDTH), jnp.float32)], axis=0
        )
        for part_ref in part_refs:
            back = part_ref[part].astype(jnp.float32)
            if back.shape[0] < tok_rows:
                missing = jnp.zeros((tok_rows - back.shape[0], KV_WIDTH), jnp.float32)
                back = jnp.concatenate([missing, back], axis=0)
            sums = sums + back
        kv_ref[0, part] = sums.astype(jnp.bfloat16)


def last_arrays(vis_start, image_dq, image_dkv, d_own_kv, texts, parts):
    rows = image_dkv.shape[1]
    smem = pl.BlockSpec(memory_space=pltpu.SMEM)
    vmem = pl.BlockSpec(memory_space=pltpu.VMEM)
    return pl.pallas_call(
        functools.partial(last_kernel, len(parts)),
        in_specs=[smem] + [vmem] * (6 + len(parts) + len(image_dq)),
        out_specs=[vmem, vmem],
        out_shape=[
            jax.ShapeDtypeStruct((1, rows, Q_WIDTH + 2 * KV_WIDTH), jnp.bfloat16),
            jax.ShapeDtypeStruct((1,) + d_own_kv.shape, jnp.bfloat16),
        ],
    )(vis_start, image_dkv, d_own_kv, *texts, *parts, *image_dq)


def gather_queries(image_q):
    every = lax.all_gather(image_q, "rollout", axis=0)
    missing = IMAGE_BLOCK - every.shape[1]
    return jnp.pad(every, ((0, 0), (0, missing), (0, 0))) if missing else every


def per_device(queries, keys_values, image_rows, cotangent, seq_image, vis_start, comp_lengths):
    tok_rows = queries.shape[1]
    image_count = image_rows.shape[1]
    ctx_size = lax.axis_size("ctx")
    seq_len = tok_rows * ctx_size
    late_shard = VIS // tok_rows
    longest = 4 * (seq_len - PREFIX) // (3 * NCOMP)
    halo = -(-(longest - 1) // 64) * 64
    q_own, d_own = queries[0], cotangent[0]

    number, image_kv, image_q, text, tail = first_arrays(
        seq_image, vis_start, image_rows, keys_values, halo
    )
    every_q = gather_queries(image_q)
    image_kv, swapped = route(image_kv, number, False, [(text, xor_pairs(late_shard))])
    image_kv, d_later = lax.optimization_barrier((image_kv, d_own))
    windows, rounds, (*masks, text) = second_arrays(
        vis_start, comp_lengths, d_later, image_kv, text, swapped, halo
    )
    blocks, texts = gather_prefix(image_kv, text, late_shard)
    windows = image_windows(windows, rounds)
    halo_kv = halo_rows(tail, halo, tok_rows)

    grad_q, *d_image_q, d_mine, d_pair, d_halo, d_own_kv = attend(
        number,
        masks,
        q_own,
        d_own,
        every_q,
        halo_kv,
        keys_values,
        blocks,
        [] if ctx_size == 8 else texts,
        windows,
    )

    d_image_q = [
        half[: image_count - at * IMAGE_HALF]
        for at, half in enumerate(d_image_q)
        if at * IMAGE_HALF < image_count
    ]
    image_dq, other, *halo_back = route(
        d_image_q[0], number, True, [(d_pair, xor_pairs(1))] + halo_parts(d_halo, tok_rows)
    )
    image_dq = [image_dq]
    steps = chip_steps(ctx_size)
    own, *sent, keys_text, values_text = on_device(
        functools.partial(split_sums, image_count, steps), d_mine, d_pair, other
    )
    beside = [(rows, xor_pairs(step)) for rows, step in zip(sent, steps)]
    if len(d_image_q) > 1:
        second, *moved = route(d_image_q[1], number, True, beside)
        image_dq.append(second)
    else:
        moved = [lax.ppermute(rows, "ctx", pairs) for rows, pairs in beside]
    sums, keys_text, values_text = on_device(
        functools.partial(add_sums, image_count), own, keys_text, values_text, *moved
    )
    if ctx_size != 8:
        keys_text = collect_text(keys_text, late_shard)
        values_text = collect_text(values_text, late_shard)
    keys_step = late_shard
    values_step = 4 if ctx_size == 8 else late_shard
    image_dkv, *other_texts = route(
        sums,
        number,
        True,
        [(keys_text, xor_pairs(keys_step)), (values_text, xor_pairs(values_step))],
    )
    grad_image, grad_kv = last_arrays(
        vis_start,
        image_dq,
        image_dkv,
        d_own_kv,
        [keys_text, values_text, *other_texts],
        halo_back,
    )
    return (grad_q[None], grad_kv, grad_image)


def solution(mesh):
    placed = (
        P("rollout", "ctx", None),
        P("rollout", None, "ctx", None),
        P("rollout", "ctx", None),
        P("rollout", "ctx", None),
        P(),
        P("rollout"),
        P("rollout", None),
    )
    return jax.shard_map(
        per_device,
        mesh=mesh,
        in_specs=placed,
        out_specs=(
            P("rollout", "ctx", None),
            P("rollout", None, "ctx", None),
            P("rollout", "ctx", None),
        ),
        check_vma=False,
    )
```
